512 devices in a mesh: row: 32 (over x_hi, z), col: 16 (over y, x_lo, core).
Axes of the slice: x: 4 (x_hi: 2, x_lo: 2; x = x_hi * 2 + x_lo), y: 4, z: 16, core: 2. Of those that a mesh axis runs over, the one named last changes fastest.
Arguments:
- pair_elements: bfloat16 [1024, 61440], P(('row', 'col')), may hold values from -6 to 6
- energy_gaps: float32 [1024], replicated, may hold values from 0.5 to 3
- frequencies: float32 [3], replicated, may hold values from 0.3 to 3
Outputs:
- polarizability: bfloat16 [3, 4096, 61440], P(None, 'row', 'col')
The draws below stay inside these ranges and needn't reach their ends.
All inputs are finite; a program needn't handle non-finite values.
Results may differ from the reference program's by a relative error of at most 0.0048.
Values may be sent and summed in bfloat16 or wider, within the bound.
A program may use at most 64 MiB of HBM per device.

```python
import math
import jax
import jax.numpy as jnp
from jax import lax

NG = 61440
NW = 3
PAIRS = 1024
GS = 4096
SLC = 256
N_COL = 16


def block_levels(key, extent, cuts, smallest, largest):
    def one(dim, blocks):
        steps = jax.random.uniform(jax.random.fold_in(jax.random.fold_in(key, 6), dim), (blocks,), jnp.float32, smallest / len(cuts), largest / len(cuts))
        return jnp.repeat(jnp.exp(steps), extent[dim] // blocks).reshape((-1,) + (1,) * (len(extent) - dim - 1))

    loudness = one(*cuts[0])
    for cut in cuts[1:]:
        loudness = loudness * one(*cut)
    return loudness


def bell_draw(stream_key, shape, spread, reach, cuts=(), kind=jnp.bfloat16):
    level = block_levels(stream_key, shape, cuts, -0.22, 0.18) if cuts else 1.0
    array = jax.random.normal(stream_key, shape, jnp.float32) * spread * level
    return jnp.minimum(jnp.maximum(array, -reach), reach).astype(kind)


def setup_inputs(seed: int = 0) -> dict:
    splits = jax.random.split(jax.random.key(seed), 4)
    pair_elements = bell_draw(splits[0], (PAIRS, NG), 1.0, 6.0, ((0, 512),))
    energy_gaps = jnp.clip(jnp.exp(jax.random.uniform(splits[1], (PAIRS,), jnp.float32, math.log(0.5), math.log(3.0))), 0.5, 3.0)
    frequencies = jnp.clip(jnp.exp(jax.random.uniform(splits[2], (NW,), jnp.float32, math.log(0.3), math.log(3.0))), 0.3, 3.0)
    return {"pair_elements": pair_elements, "energy_gaps": energy_gaps, "frequencies": frequencies}


def reference(pair_elements, energy_gaps, frequencies):
    pair_count = pair_elements.shape[0]
    window = pair_elements.reshape(pair_count, N_COL, NG // N_COL)[:, :, :SLC].reshape(pair_count, GS)
    gaps = energy_gaps[:, None]
    weights = -4.0 * gaps / ((gaps * gaps + frequencies[None, :] * frequencies[None, :]) * math.sqrt(pair_count))
    scaled = (window.astype(jnp.float32)[:, None, :] * weights[:, :, None]).astype(jnp.bfloat16)

    def per_freq(index):
        chosen = lax.dynamic_index_in_dim(scaled, index, 1, keepdims=False)
        return jnp.dot(chosen.T, pair_elements, preferred_element_type=jnp.float32).astype(jnp.bfloat16)
    return lax.map(per_freq, jnp.arange(NW, dtype=jnp.int32))
```

```python
import functools
import math

import jax
import jax.numpy as jnp
from jax import lax
from jax.experimental import pallas as pl
from jax.experimental.pallas import tpu as pltpu
from jax.sharding import PartitionSpec as P

NW = 3
GSR = 128
WIDTH = 384
KEPT = 4
LENT = 3
MESH = pl.DeviceIdType.MESH


def kernel(nz, ny, pairs, arrived, gaps, freqs, out, buf, stage, wbuf, lhs, obuf,
           zrecv, zsend, xrecv, xsend, first_recv, first_send, wrecv, wsend, osem):
    row, col = lax.axis_index("row"), lax.axis_index("col")
    hi, z = row // nz, lax.rem(row, nz)
    y = col // 4
    in_y = lax.rem(col, 4)
    lo, core = in_y // 2, lax.rem(in_y, 2)
    up = (hi * nz + lax.rem(z + 1, nz), col)
    down = (hi * nz + lax.rem(z + nz - 1, nz), col)
    other_lo = y * 4 + (1 - lo) * 2 + core
    side = [(z, other_lo), (nz + z, other_lo)]
    across = ((1 - hi) * nz + z, col)
    in_column = [(row, lax.rem(y + k, ny) * 4 + in_y) for k in range(1, ny)]
    twin_lo = (row, other_lo)
    twin_core = (row, y * 4 + lo * 2 + (1 - core))
    half = nz // 2

    barrier = pltpu.get_barrier_semaphore()
    partners = [up, down, side[0], side[1], across, twin_core] + in_column
    for partner in partners:
        pl.semaphore_signal(barrier, inc=1, device_id=partner, device_id_type=MESH)

    for j in range(KEPT):
        buf[j, hi, z] = arrived[:, j * WIDTH:(j + 1) * WIDTH]
    for h in range(2):
        for j in range(LENT):
            at = (KEPT + h * LENT + j) * WIDTH
            stage[h, j] = arrived[:, at:at + WIDTH]
    pl.semaphore_wait(barrier, len(partners))

    def remote(src, dst, send, recv, device):
        return pltpu.make_async_remote_copy(
            src_ref=src, dst_ref=dst, send_sem=send, recv_sem=recv, device_id=device, device_id_type=MESH
        )

    def wait(ref, sem):
        pltpu.make_async_copy(ref, ref, sem).wait()

    own = buf.at[pl.ds(0, KEPT), hi, z]
    lent = buf.at[pl.ds(KEPT, LENT), hi, z]
    for h in range(2):
        remote(stage.at[h], lent, first_send.at[h], first_recv.at[hi], side[h]).start()
    remote(own, own, first_send.at[2], first_recv.at[2], across).start()

    def slab(chunk, k):
        return buf.at[chunk, :, lax.rem(z + k + nz, nz)]

    def push(chunk, k):
        j = chunk - KEPT
        for h in range(2):
            part = lax.rem(z + k + nz, nz)
            remote(
                buf.at[chunk, :, part],
                buf.at[KEPT + LENT + hi * LENT + j, :, part],
                xsend.at[h, j], xrecv.at[hi, j], side[h],
            ).start()

    def tick(chunk, s):
        for way, device, sign in ((0, up, -1), (1, down, 1)):
            if s > 0:
                wait(slab(chunk, sign * s), zrecv.at[way, chunk, s - 1])
            part = slab(chunk, sign * s)
            if s == half - 1:
                part = part.at[way]
            remote(part, part, zsend.at[way, chunk], zrecv.at[way, chunk, s], device).start()
        if chunk >= KEPT:
            push(chunk, -s)
            if s > 0:
                push(chunk, s)

    def last(chunk):
        for way in range(2):
            wait(slab(chunk, half).at[way], zrecv.at[way, chunk, half - 1])
        if chunk >= KEPT:
            push(chunk, half)

    window_col = row // 2
    in_w = lax.rem(window_col, 4)
    same_core = core == lax.rem(in_w, 2)
    same_line = jnp.logical_and(same_core, lo == in_w // 2)
    is_source = jnp.logical_and(same_line, y == window_col // 4)

    def window_y():
        @pl.when(is_source)
        def _():
            for b in range(2):
                @pl.when(lax.rem(row, 2) == b)
                def _():
                    wbuf[...] = buf[0, :, :, :, b * GSR:(b + 1) * GSR]
            for k, device in enumerate(in_column):
                remote(wbuf, wbuf, wsend.at[k], wrecv.at[0], device).start()

    def window_x():
        @pl.when(same_line)
        def _():
            @pl.when(jnp.logical_not(is_source))
            def _():
                wait(wbuf, wrecv.at[0])
            remote(wbuf, wbuf, wsend.at[ny - 1], wrecv.at[1], twin_lo).start()

    def window_core():
        @pl.when(same_core)
        def _():
            @pl.when(jnp.logical_not(same_line))
            def _():
                wait(wbuf, wrecv.at[1])
            remote(wbuf, wbuf, wsend.at[ny], wrecv.at[2], twin_core).start()

    def window_done():
        @pl.when(jnp.logical_not(same_core))
        def _():
            wait(wbuf, wrecv.at[2])
        gap_row = gaps[...]
        w_all = [
            -4.0 * gap_row / ((gap_row * gap_row + freqs[w] * freqs[w]) * math.sqrt(pairs))
            for w in range(NW)
        ]
        flat = wbuf[...].reshape(pairs, GSR)
        for at in range(0, pairs, GSR):
            turned = flat[at:at + GSR].astype(jnp.float32).T
            for w in range(NW):
                lhs[w * GSR:(w + 1) * GSR, at:at + GSR] = (turned * w_all[w][:, at:at + GSR]).astype(jnp.bfloat16)

    def multiply(chunk):
        place = chunk if chunk < KEPT else chunk - LENT
        panel = buf[chunk].reshape(pairs, WIDTH)
        chi = jnp.dot(lhs[...], panel, preferred_element_type=jnp.float32)
        obuf[place] = chi.astype(jnp.bfloat16).reshape(NW, GSR, WIDTH)
        write(place).start()

    def write(place):
        return pltpu.make_async_copy(
            obuf.at[place], out.at[:, :, pl.ds(place * WIDTH, WIDTH)], osem.at[place]
        )

    def received(h, j):
        chunk = KEPT + LENT + h * LENT + j
        wait(buf.at[chunk], xrecv.at[h, j])
        multiply(chunk)

    for h in range(2):
        wait(buf.at[pl.ds(KEPT, LENT), h, z], first_recv.at[h])
    wait(buf.at[pl.ds(0, KEPT), 1 - hi, z], first_recv.at[2])

    f0, f1, f2 = range(KEPT, KEPT + LENT)
    rounds = [(0, f0), (1, f1), (2, f2, 3)]
    todo = {
        (1, 0): [window_y], (1, 3): [window_x], (1, 5): [window_core],
        (2, 0): [window_done],
        (2, 1): [lambda: multiply(0)], (2, 2): [lambda: multiply(1)],
        (2, 3): [lambda: received(0, 0)], (2, 4): [lambda: received(1, 0)],
        (2, 6): [lambda: received(0, 1)], (2, 7): [lambda: received(1, 1)],
    }
    before = ()
    for n, chunks in enumerate(rounds):
        for s in range(half):
            for chunk in chunks:
                tick(chunk, s)
            if s == 0:
                for chunk in before:
                    last(chunk)
            for work in todo.get((n, s), ()):
                work()
        before = chunks
    for chunk in (f2, 2, 3):
        last(chunk)
    multiply(2)
    multiply(3)
    received(0, 2)
    received(1, 2)

    for chunk in range(KEPT + LENT):
        for way in range(2):
            wait(buf.at[chunk, 0, pl.ds(0, nz - 1)], zsend.at[way, chunk])
    for j in range(LENT):
        for h in range(2):
            wait(buf.at[KEPT + j], xsend.at[h, j])
    for h in range(2):
        wait(stage.at[h], first_send.at[h])
    wait(own, first_send.at[2])

    @pl.when(is_source)
    def _():
        for k in range(ny - 1):
            wait(wbuf, wsend.at[k])

    @pl.when(same_line)
    def _():
        wait(wbuf, wsend.at[ny - 1])

    @pl.when(same_core)
    def _():
        wait(wbuf, wsend.at[ny])

    for place in range(KEPT + 2 * LENT):
        write(place).wait()


def on_device(pair_elements, energy_gaps, frequencies):
    rows, cols = lax.axis_size("row"), lax.axis_size("col")
    local, full = pair_elements.shape
    pairs = local * rows * cols
    block = full // cols
    nz, ny = rows // 2, cols // 4
    arrived = lax.all_to_all(pair_elements, "col", split_axis=1, concat_axis=0, tiled=True)
    depth = arrived.shape[0]
    dma = pltpu.SemaphoreType.DMA
    n_out = KEPT + 2 * LENT
    return pl.pallas_call(
        functools.partial(kernel, nz, ny, pairs),
        out_shape=jax.ShapeDtypeStruct((NW, GSR, block), jnp.bfloat16),
        in_specs=[
            pl.BlockSpec(memory_space=pltpu.VMEM),
            pl.BlockSpec(memory_space=pltpu.VMEM),
            pl.BlockSpec(memory_space=pltpu.SMEM),
        ],
        out_specs=pl.BlockSpec(memory_space=pl.ANY),
        scratch_shapes=[
            pltpu.VMEM((KEPT + 3 * LENT, 2, nz, depth, WIDTH), jnp.bfloat16),
            pltpu.VMEM((2, LENT, depth, WIDTH), jnp.bfloat16),
            pltpu.VMEM((2, nz, depth, GSR), jnp.bfloat16),
            pltpu.VMEM((NW * GSR, pairs), jnp.bfloat16),
            pltpu.VMEM((n_out, NW, GSR, WIDTH), jnp.bfloat16),
            dma((2, KEPT + LENT, nz // 2)),
            dma((2, KEPT + LENT)),
            dma((2, LENT)),
            dma((2, LENT)),
            dma((3,)),
            dma((3,)),
            dma((3,)),
            dma((ny + 1,)),
            dma((n_out,)),
        ],
        compiler_params=pltpu.CompilerParams(
            collective_id=0, has_side_effects=True, vmem_limit_bytes=40 * 1024 * 1024
        ),
        cost_estimate=pl.CostEstimate(
            flops=2 * NW * GSR * pairs * block, bytes_accessed=2 * NW * GSR * block, transcendentals=0
        ),
    )(arrived, energy_gaps.reshape(1, pairs), frequencies)


def solution(mesh):
    in_specs = (P(("row", "col"), None), P(), P())
    out_specs = P(None, "row", "col")
    return jax.shard_map(
        on_device, mesh=mesh, in_specs=in_specs, out_specs=out_specs, check_vma=False
    )
```

```python
import functools
import math

import jax
import jax.numpy as jnp
from jax import lax
from jax.experimental import pallas as pl
from jax.experimental.pallas import tpu as pltpu
from jax.sharding import PartitionSpec as P

NW = 3
GSR = 128
WIDTH = 384
KEPT = 4
LENT = 3
MESH = pl.DeviceIdType.MESH


def kernel(nz, ny, pairs, arrived, gaps, freqs, out, buf, stage, wbuf, lhs, obuf,
           zrecv, zsend, xrecv, xsend, first_recv, first_send, wrecv, wsend, osem):
    row, col = lax.axis_index("row"), lax.axis_index("col")
    hi, z = row // nz, lax.rem(row, nz)
    y = col // 4
    in_y = lax.rem(col, 4)
    lo, core = in_y // 2, lax.rem(in_y, 2)
    up = (hi * nz + lax.rem(z + 1, nz), col)
    down = (hi * nz + lax.rem(z + nz - 1, nz), col)
    other_lo = y * 4 + (1 - lo) * 2 + core
    side = [(z, other_lo), (nz + z, other_lo)]
    across = ((1 - hi) * nz + z, col)
    in_column = [(row, lax.rem(y + k, ny) * 4 + in_y) for k in range(1, ny)]
    twin_lo = (row, other_lo)
    twin_core = (row, y * 4 + lo * 2 + (1 - core))
    half = nz // 2

    barrier = pltpu.get_barrier_semaphore()
    partners = [up, down, side[0], side[1], across, twin_core] + in_column
    for partner in partners:
        pl.semaphore_signal(barrier, inc=1, device_id=partner, device_id_type=MESH)

    for j in range(KEPT):
        buf[j, hi, z] = arrived[:, j * WIDTH:(j + 1) * WIDTH]
    for h in range(2):
        for j in range(LENT):
            at = (KEPT + h * LENT + j) * WIDTH
            stage[h, j] = arrived[:, at:at + WIDTH]
    pl.semaphore_wait(barrier, len(partners))

    def remote(src, dst, send, recv, device):
        return pltpu.make_async_remote_copy(
            src_ref=src, dst_ref=dst, send_sem=send, recv_sem=recv, device_id=device, device_id_type=MESH
        )

    def wait(ref, sem):
        pltpu.make_async_copy(ref, ref, sem).wait()

    own = buf.at[pl.ds(0, KEPT), hi, z]
    lent = buf.at[pl.ds(KEPT, LENT), hi, z]
    for h in range(2):
        remote(stage.at[h], lent, first_send.at[h], first_recv.at[hi], side[h]).start()
    remote(own, own, first_send.at[2], first_recv.at[2], across).start()

    def slab(chunk, k):
        return buf.at[chunk, :, lax.rem(z + k + nz, nz)]

    def push(chunk, k):
        j = chunk - KEPT
        for h in range(2):
            part = lax.rem(z + k + nz, nz)
            remote(
                buf.at[chunk, :, part],
                buf.at[KEPT + LENT + hi * LENT + j, :, part],
                xsend.at[h, j], xrecv.at[hi, j], side[h],
            ).start()

    def tick(chunk, s):
        for way, device, sign in ((0, up, -1), (1, down, 1)):
            if s > 0:
                wait(slab(chunk, sign * s), zrecv.at[way, chunk, s - 1])
            part = slab(chunk, sign * s)
            if s == half - 1:
                part = part.at[way]
            remote(part, part, zsend.at[way, chunk], zrecv.at[way, chunk, s], device).start()
        if chunk >= KEPT:
            push(chunk, -s)
            if s > 0:
                push(chunk, s)

    def last(chunk):
        for way in range(2):
            wait(slab(chunk, half).at[way], zrecv.at[way, chunk, half - 1])
        if chunk >= KEPT:
            push(chunk, half)

    window_col = row // 2
    in_w = lax.rem(window_col, 4)
    same_core = core == lax.rem(in_w, 2)
    same_line = jnp.logical_and(same_core, lo == in_w // 2)
    is_source = jnp.logical_and(same_line, y == window_col // 4)

    def window_y():
        @pl.when(is_source)
        def _():
            for b in range(2):
                @pl.when(lax.rem(row, 2) == b)
                def _():
                    wbuf[...] = buf[0, :, :, :, b * GSR:(b + 1) * GSR]
            for k, device in enumerate(in_column):
                remote(wbuf, wbuf, wsend.at[k], wrecv.at[0], device).start()

    def window_x():
        @pl.when(same_line)
        def _():
            @pl.when(jnp.logical_not(is_source))
            def _():
                wait(wbuf, wrecv.at[0])
            remote(wbuf, wbuf, wsend.at[ny - 1], wrecv.at[1], twin_lo).start()

    def window_core():
        @pl.when(same_core)
        def _():
            @pl.when(jnp.logical_not(same_line))
            def _():
                wait(wbuf, wrecv.at[1])
            remote(wbuf, wbuf, wsend.at[ny], wrecv.at[2], twin_core).start()

    def window_done():
        @pl.when(jnp.logical_not(same_core))
        def _():
            wait(wbuf, wrecv.at[2])
        gap_row = gaps[...]
        w_all = [
            -4.0 * gap_row / ((gap_row * gap_row + freqs[w] * freqs[w]) * math.sqrt(pairs))
            for w in range(NW)
        ]
        flat = wbuf[...].reshape(pairs, GSR)
        for at in range(0, pairs, GSR):
            turned = flat[at:at + GSR].astype(jnp.float32).T
            for w in range(NW):
                lhs[w * GSR:(w + 1) * GSR, at:at + GSR] = (turned * w_all[w][:, at:at + GSR]).astype(jnp.bfloat16)

    def multiply(chunk):
        place = chunk if chunk < KEPT else chunk - LENT
        panel = buf[chunk].reshape(pairs, WIDTH)
        chi = jnp.dot(lhs[...], panel, preferred_element_type=jnp.float32)
        obuf[place] = chi.astype(jnp.bfloat16).reshape(NW, GSR, WIDTH)
        write(place).start()

    def write(place):
        return pltpu.make_async_copy(
            obuf.at[place], out.at[:, :, pl.ds(place * WIDTH, WIDTH)], osem.at[place]
        )

    def received(h, j):
        chunk = KEPT + LENT + h * LENT + j
        wait(buf.at[chunk], xrecv.at[h, j])
        multiply(chunk)

    for h in range(2):
        wait(buf.at[pl.ds(KEPT, LENT), h, z], first_recv.at[h])
    wait(buf.at[pl.ds(0, KEPT), 1 - hi, z], first_recv.at[2])

    f0, f1, f2 = range(KEPT, KEPT + LENT)
    rounds = [(0, f0, f1, 1), (f2, 2, 3)]
    todo = {
        (1, 0): [window_y], (1, 2): [window_x], (1, 4): [window_core],
        (1, 5): [window_done, lambda: multiply(0)],
        (1, 6): [lambda: multiply(1), lambda: received(0, 0), lambda: received(1, 0)],
        (1, 7): [lambda: received(0, 1), lambda: received(1, 1)],
    }
    before = ()
    for n, chunks in enumerate(rounds):
        for s in range(half):
            for chunk in chunks:
                tick(chunk, s)
            if s == 0:
                for chunk in before:
                    last(chunk)
            for work in todo.get((n, s), ()):
                work()
        before = chunks
    for chunk in (f2, 2, 3):
        last(chunk)
    multiply(2)
    multiply(3)
    received(0, 2)
    received(1, 2)

    for chunk in range(KEPT + LENT):
        for way in range(2):
            wait(buf.at[chunk, 0, pl.ds(0, nz - 1)], zsend.at[way, chunk])
    for j in range(LENT):
        for h in range(2):
            wait(buf.at[KEPT + j], xsend.at[h, j])
    for h in range(2):
        wait(stage.at[h], first_send.at[h])
    wait(own, first_send.at[2])

    @pl.when(is_source)
    def _():
        for k in range(ny - 1):
            wait(wbuf, wsend.at[k])

    @pl.when(same_line)
    def _():
        wait(wbuf, wsend.at[ny - 1])

    @pl.when(same_core)
    def _():
        wait(wbuf, wsend.at[ny])

    for place in range(KEPT + 2 * LENT):
        write(place).wait()


def on_device(pair_elements, energy_gaps, frequencies):
    rows, cols = lax.axis_size("row"), lax.axis_size("col")
    local, full = pair_elements.shape
    pairs = local * rows * cols
    block = full // cols
    nz, ny = rows // 2, cols // 4
    arrived = lax.all_to_all(pair_elements, "col", split_axis=1, concat_axis=0, tiled=True)
    depth = arrived.shape[0]
    dma = pltpu.SemaphoreType.DMA
    n_out = KEPT + 2 * LENT
    return pl.pallas_call(
        functools.partial(kernel, nz, ny, pairs),
        out_shape=jax.ShapeDtypeStruct((NW, GSR, block), jnp.bfloat16),
        in_specs=[
            pl.BlockSpec(memory_space=pltpu.VMEM),
            pl.BlockSpec(memory_space=pltpu.VMEM),
            pl.BlockSpec(memory_space=pltpu.SMEM),
        ],
        out_specs=pl.BlockSpec(memory_space=pl.ANY),
        scratch_shapes=[
            pltpu.VMEM((KEPT + 3 * LENT, 2, nz, depth, WIDTH), jnp.bfloat16),
            pltpu.VMEM((2, LENT, depth, WIDTH), jnp.bfloat16),
            pltpu.VMEM((2, nz, depth, GSR), jnp.bfloat16),
            pltpu.VMEM((NW * GSR, pairs), jnp.bfloat16),
            pltpu.VMEM((n_out, NW, GSR, WIDTH), jnp.bfloat16),
            dma((2, KEPT + LENT, nz // 2)),
            dma((2, KEPT + LENT)),
            dma((2, LENT)),
            dma((2, LENT)),
            dma((3,)),
            dma((3,)),
            dma((3,)),
            dma((ny + 1,)),
            dma((n_out,)),
        ],
        compiler_params=pltpu.CompilerParams(
            collective_id=0, has_side_effects=True, vmem_limit_bytes=40 * 1024 * 1024
        ),
        cost_estimate=pl.CostEstimate(
            flops=2 * NW * GSR * pairs * block, bytes_accessed=2 * NW * GSR * block, transcendentals=0
        ),
    )(arrived, energy_gaps.reshape(1, pairs), frequencies)


def solution(mesh):
    in_specs = (P(("row", "col"), None), P(), P())
    out_specs = P(None, "row", "col")
    return jax.shard_map(
        on_device, mesh=mesh, in_specs=in_specs, out_specs=out_specs, check_vma=False
    )
```

```python
import functools
import math

import jax
import jax.numpy as jnp
from jax import lax
from jax.experimental import pallas as pl
from jax.experimental.pallas import tpu as pltpu
from jax.sharding import PartitionSpec as P

NW = 3
GSR = 128
WIDTH = 384
KEPT = 4
LENT = 3
ROUNDS = ((0, 4, 5, 1), (6, 2, 3))
MESH = pl.DeviceIdType.MESH


def kernel(nz, ny, pairs, elements, gaps_in, freqs_in, out, raw, gaps, freqs, packed_a, packed_b, parts_a, parts_b,
           buf, wbuf, lhs, obuf, in_sem, part_recv, part_send,
           zrecv, zsend, xrecv, xsend, wrecv, wsend, osem):
    row, col = lax.axis_index("row"), lax.axis_index("col")
    hi, z = row // nz, lax.rem(row, nz)
    ncol = ny * 4
    plane = 2 * ncol
    seat = hi * ncol + col
    y = col // 4
    in_y = lax.rem(col, 4)
    lo, core = in_y // 2, lax.rem(in_y, 2)
    up = (hi * nz + lax.rem(z + 1, nz), col)
    down = (hi * nz + lax.rem(z + nz - 1, nz), col)
    other_lo = y * 4 + (1 - lo) * 2 + core
    side = [(z, other_lo), (nz + z, other_lo)]
    in_column = [(row, lax.rem(y + k, ny) * 4 + in_y) for k in range(1, ny)]
    twin_lo = (row, other_lo)
    twin_core = (row, y * 4 + lo * 2 + (1 - core))
    half = nz // 2

    barrier = pltpu.get_barrier_semaphore()

    def seated(k):
        to = lax.rem(seat + k, plane)
        return to, (to // ncol * nz + z, lax.rem(to, ncol))

    for partner in (up, down):
        pl.semaphore_signal(barrier, inc=1, device_id=partner, device_id_type=MESH)

    @pl.loop(1, plane)
    def _(k):
        pl.semaphore_signal(barrier, inc=1, device_id=seated(k)[1], device_id_type=MESH)

    loads = [
        pltpu.make_async_copy(elements, raw, in_sem.at[0]),
        pltpu.make_async_copy(gaps_in, gaps, in_sem.at[1]),
        pltpu.make_async_copy(freqs_in, freqs, in_sem.at[2]),
    ]
    for load in loads:
        load.start()
    loads[0].wait()

    def start_column(chunk, h, c):
        block = (KEPT + 2 * LENT) * WIDTH
        if chunk < KEPT:
            return c * block + chunk * WIDTH
        return (c ^ 2) * block + (chunk + h * LENT) * WIDTH

    for packed, chunks in ((packed_a, ROUNDS[0]), (packed_b, ROUNDS[1])):
        for to in range(plane):
            for n, chunk in enumerate(chunks):
                at = start_column(chunk, to // ncol, to % ncol)
                packed[to, :, n * WIDTH:(n + 1) * WIDTH] = raw[:, at:at + WIDTH]
    pl.semaphore_wait(barrier, plane + 1)

    def remote(src, dst, send, recv, device):
        return pltpu.make_async_remote_copy(
            src_ref=src, dst_ref=dst, send_sem=send, recv_sem=recv, device_id=device, device_id_type=MESH
        )

    def wait(ref, sem):
        pltpu.make_async_copy(ref, ref, sem).wait()

    for n, (packed, parts) in enumerate(((packed_a, parts_a), (packed_b, parts_b))):
        @pl.loop(1, plane)
        def _(k):
            to, device = seated(k)
            remote(packed.at[to], parts.at[seat], part_send.at[n], part_recv.at[n], device).start()

        parts[seat] = packed[seat]

    def begin(n):
        parts = (parts_a, parts_b)[n]
        wait(parts.at[pl.ds(0, plane - 1)], part_recv.at[n])
        for h in range(2):
            for m, chunk in enumerate(ROUNDS[n]):
                part = parts[h * ncol:(h + 1) * ncol, :, m * WIDTH:(m + 1) * WIDTH]
                buf[chunk, h, z] = part.reshape(2 * ncol, WIDTH)

    def slab(chunk, k):
        return buf.at[chunk, :, lax.rem(z + k + nz, nz)]

    def push(chunk, k):
        j = chunk - KEPT
        for h in range(2):
            part = lax.rem(z + k + nz, nz)
            remote(
                buf.at[chunk, :, part],
                buf.at[KEPT + LENT + hi * LENT + j, :, part],
                xsend.at[h, j], xrecv.at[hi, j], side[h],
            ).start()

    def tick(chunk, s):
        for way, device, sign in ((0, up, -1), (1, down, 1)):
            if s > 0:
                wait(slab(chunk, sign * s), zrecv.at[way, chunk, s - 1])
            part = slab(chunk, sign * s)
            if s == half - 1:
                part = part.at[way]
            remote(part, part, zsend.at[way, chunk], zrecv.at[way, chunk, s], device).start()
        if chunk >= KEPT:
            push(chunk, -s)
            if s > 0:
                push(chunk, s)

    def last(chunk):
        for way in range(2):
            wait(slab(chunk, half).at[way], zrecv.at[way, chunk, half - 1])
        if chunk >= KEPT:
            push(chunk, half)

    window_col = row // 2
    in_w = lax.rem(window_col, 4)
    same_core = core == lax.rem(in_w, 2)
    same_line = jnp.logical_and(same_core, lo == in_w // 2)
    is_source = jnp.logical_and(same_line, y == window_col // 4)

    def window_y():
        @pl.when(is_source)
        def _():
            for b in range(2):
                @pl.when(lax.rem(row, 2) == b)
                def _():
                    wbuf[...] = buf[0, :, :, :, b * GSR:(b + 1) * GSR]
            for k, device in enumerate(in_column):
                remote(wbuf, wbuf, wsend.at[k], wrecv.at[0], device).start()

    def window_x():
        @pl.when(same_line)
        def _():
            @pl.when(jnp.logical_not(is_source))
            def _():
                wait(wbuf, wrecv.at[0])
            remote(wbuf, wbuf, wsend.at[ny - 1], wrecv.at[1], twin_lo).start()

    def window_core():
        @pl.when(same_core)
        def _():
            @pl.when(jnp.logical_not(same_line))
            def _():
                wait(wbuf, wrecv.at[1])
            remote(wbuf, wbuf, wsend.at[ny], wrecv.at[2], twin_core).start()

    def window_done():
        @pl.when(jnp.logical_not(same_core))
        def _():
            wait(wbuf, wrecv.at[2])
        loads[1].wait()
        loads[2].wait()
        gap_row = gaps[...]
        w_all = [
            -4.0 * gap_row / ((gap_row * gap_row + freqs[w] * freqs[w]) * math.sqrt(pairs))
            for w in range(NW)
        ]
        flat = wbuf[...].reshape(pairs, GSR)
        for at in range(0, pairs, GSR):
            turned = flat[at:at + GSR].astype(jnp.float32).T
            for w in range(NW):
                lhs[w * GSR:(w + 1) * GSR, at:at + GSR] = (turned * w_all[w][:, at:at + GSR]).astype(jnp.bfloat16)

    def multiply(chunk):
        place = chunk if chunk < KEPT else chunk - LENT
        panel = buf[chunk].reshape(pairs, WIDTH)
        chi = jnp.dot(lhs[...], panel, preferred_element_type=jnp.float32)
        obuf[place] = chi.astype(jnp.bfloat16).reshape(NW, GSR, WIDTH)
        write(place).start()

    def write(place):
        return pltpu.make_async_copy(
            obuf.at[place], out.at[:, :, pl.ds(place * WIDTH, WIDTH)], osem.at[place]
        )

    def received(h, j):
        chunk = KEPT + LENT + h * LENT + j
        wait(buf.at[chunk], xrecv.at[h, j])
        multiply(chunk)

    f2 = ROUNDS[1][0]
    todo = {
        (1, 0): [window_y], (1, 2): [window_x], (1, 4): [window_core],
        (1, 5): [window_done, lambda: multiply(0)],
        (1, 6): [lambda: multiply(1), lambda: received(0, 0), lambda: received(1, 0)],
        (1, 7): [lambda: received(0, 1), lambda: received(1, 1)],
    }
    before = ()
    for n, chunks in enumerate(ROUNDS):
        begin(n)
        for s in range(half):
            for chunk in chunks:
                tick(chunk, s)
            if s == 0:
                for chunk in before:
                    last(chunk)
            for work in todo.get((n, s), ()):
                work()
        before = chunks
    for chunk in (f2, 2, 3):
        last(chunk)
    multiply(2)
    multiply(3)
    received(0, 2)
    received(1, 2)

    for chunk in range(KEPT + LENT):
        for way in range(2):
            wait(buf.at[chunk, 0, pl.ds(0, nz - 1)], zsend.at[way, chunk])
    for j in range(LENT):
        for h in range(2):
            wait(buf.at[KEPT + j], xsend.at[h, j])
    for n, packed in enumerate((packed_a, packed_b)):
        wait(packed.at[pl.ds(0, plane - 1)], part_send.at[n])

    @pl.when(is_source)
    def _():
        for k in range(ny - 1):
            wait(wbuf, wsend.at[k])

    @pl.when(same_line)
    def _():
        wait(wbuf, wsend.at[ny - 1])

    @pl.when(same_core)
    def _():
        wait(wbuf, wsend.at[ny])

    for place in range(KEPT + 2 * LENT):
        write(place).wait()


def on_device(pair_elements, energy_gaps, frequencies):
    rows, cols = lax.axis_size("row"), lax.axis_size("col")
    local, full = pair_elements.shape
    pairs = local * rows * cols
    block = full // cols
    nz, ny = rows // 2, cols // 4
    depth = local * cols
    plane = 2 * cols
    dma = pltpu.SemaphoreType.DMA
    n_out = KEPT + 2 * LENT
    return pl.pallas_call(
        functools.partial(kernel, nz, ny, pairs),
        out_shape=jax.ShapeDtypeStruct((NW, GSR, block), jnp.bfloat16),
        in_specs=[pl.BlockSpec(memory_space=pl.ANY)] * 3,
        out_specs=pl.BlockSpec(memory_space=pl.ANY),
        scratch_shapes=[
            pltpu.VMEM((local, full), jnp.bfloat16),
            pltpu.VMEM((1, pairs), jnp.float32),
            pltpu.SMEM((NW,), jnp.float32),
            pltpu.VMEM((plane, local, len(ROUNDS[0]) * WIDTH), jnp.bfloat16),
            pltpu.VMEM((plane, local, len(ROUNDS[1]) * WIDTH), jnp.bfloat16),
            pltpu.VMEM((plane, local, len(ROUNDS[0]) * WIDTH), jnp.bfloat16),
            pltpu.VMEM((plane, local, len(ROUNDS[1]) * WIDTH), jnp.bfloat16),
            pltpu.VMEM((KEPT + 3 * LENT, 2, nz, depth, WIDTH), jnp.bfloat16),
            pltpu.VMEM((2, nz, depth, GSR), jnp.bfloat16),
            pltpu.VMEM((NW * GSR, pairs), jnp.bfloat16),
            pltpu.VMEM((n_out, NW, GSR, WIDTH), jnp.bfloat16),
            dma((3,)),
            dma((2,)),
            dma((2,)),
            dma((2, KEPT + LENT, nz // 2)),
            dma((2, KEPT + LENT)),
            dma((2, LENT)),
            dma((2, LENT)),
            dma((3,)),
            dma((ny + 1,)),
            dma((n_out,)),
        ],
        compiler_params=pltpu.CompilerParams(
            collective_id=0, has_side_effects=True, vmem_limit_bytes=60 * 1024 * 1024
        ),
        cost_estimate=pl.CostEstimate(
            flops=2 * NW * GSR * pairs * block, bytes_accessed=2 * NW * GSR * block, transcendentals=0
        ),
    )(pair_elements, energy_gaps.reshape(1, pairs), frequencies)


def solution(mesh):
    in_specs = (P(("row", "col"), None), P(), P())
    out_specs = P(None, "row", "col")
    return jax.shard_map(
        on_device, mesh=mesh, in_specs=in_specs, out_specs=out_specs, check_vma=False
    )
```

```python
import functools
import math

import jax
import jax.numpy as jnp
from jax import lax
from jax.experimental import pallas as pl
from jax.experimental.pallas import tpu as pltpu
from jax.sharding import PartitionSpec as P

NW = 3
GSR = 128
WIDTH = 384
KEPT = 4
LENT = 3
FIRST, SECOND = (0, 4, 5), (6, 1, 2, 3)
MESH = pl.DeviceIdType.MESH


def ring_order(steps):
    spacing = {0: 4, 4: 5, 5: 5, 6: 4, 1: 4, 2: 4, 3: 4}
    rank = FIRST + SECOND
    done = {chunk: 0 for chunk in rank}
    seen = {chunk: -100 for chunk in rank}
    order = []
    while any(n < steps for n in done.values()):
        at = len(order)
        ready = [c for c in rank if done[c] < steps and at - seen[c] >= spacing[c]]
        if not ready:
            ready = [min((c for c in rank if done[c] < steps), key=lambda c: seen[c])]
        leaders = [c for c in ready if c in FIRST]
        pick = leaders[0] if leaders else min(ready, key=lambda c: (done[c], rank.index(c)))
        order.append((pick, done[pick]))
        done[pick] += 1
        seen[pick] = at
    return order


def kernel(nz, ny, pairs, elements, gaps_in, freqs_in, out, raw, gaps, turned_gaps, ordered_gaps, freqs, packed_a, packed_b, parts_a, parts_b,
           buf, wbuf, lhs, obuf, in_sem, part_recv, part_send,
           zrecv, zsend, xrecv, xsend, wrecv, wsend, osem):
    row, col = lax.axis_index("row"), lax.axis_index("col")
    hi, z = row // nz, lax.rem(row, nz)
    ncol = ny * 4
    plane = 2 * ncol
    seat = hi * ncol + col
    y = col // 4
    in_y = lax.rem(col, 4)
    lo, core = in_y // 2, lax.rem(in_y, 2)
    up = (hi * nz + lax.rem(z + 1, nz), col)
    down = (hi * nz + lax.rem(z + nz - 1, nz), col)
    other_lo = y * 4 + (1 - lo) * 2 + core
    side = [(z, other_lo), (nz + z, other_lo)]
    in_column = [(row, lax.rem(y + k, ny) * 4 + in_y) for k in (1, 3, 2)]
    twin_lo = (row, other_lo)
    twin_core = (row, y * 4 + lo * 2 + (1 - core))
    half = nz // 2

    barrier = pltpu.get_barrier_semaphore()

    def seated(k):
        to = lax.rem(seat + k, plane)
        return to, (to // ncol * nz + z, lax.rem(to, ncol))

    for partner in (up, down):
        pl.semaphore_signal(barrier, inc=1, device_id=partner, device_id_type=MESH)

    @pl.loop(1, plane)
    def _(k):
        pl.semaphore_signal(barrier, inc=1, device_id=seated(k)[1], device_id_type=MESH)

    loads = [
        pltpu.make_async_copy(elements, raw, in_sem.at[0]),
        pltpu.make_async_copy(gaps_in, gaps, in_sem.at[1]),
        pltpu.make_async_copy(freqs_in, freqs, in_sem.at[2]),
    ]
    for load in loads:
        load.start()
    loads[0].wait()

    def start_column(chunk, h, c):
        block = (KEPT + 2 * LENT) * WIDTH
        if chunk < KEPT:
            return c * block + chunk * WIDTH
        return (c ^ 2) * block + (chunk + h * LENT) * WIDTH

    for packed, chunks in ((packed_a, FIRST), (packed_b, SECOND)):
        for to in range(plane):
            for n, chunk in enumerate(chunks):
                at = start_column(chunk, to // ncol, to % ncol)
                packed[to, :, n * WIDTH:(n + 1) * WIDTH] = raw[:, at:at + WIDTH]
    pl.semaphore_wait(barrier, plane + 1)

    def remote(src, dst, send, recv, device):
        return pltpu.make_async_remote_copy(
            src_ref=src, dst_ref=dst, send_sem=send, recv_sem=recv, device_id=device, device_id_type=MESH
        )

    def wait(ref, sem):
        pltpu.make_async_copy(ref, ref, sem).wait()

    for n, (packed, parts) in enumerate(((packed_a, parts_a), (packed_b, parts_b))):
        @pl.loop(1, plane)
        def _(k):
            to, device = seated(k)
            remote(packed.at[to], parts.at[seat], part_send.at[n], part_recv.at[n], device).start()

        parts[seat] = packed[seat]

    def begin(n):
        parts = (parts_a, parts_b)[n]
        wait(parts.at[pl.ds(0, plane - 1)], part_recv.at[n])
        for h in range(2):
            for m, chunk in enumerate((FIRST, SECOND)[n]):
                part = parts[h * ncol:(h + 1) * ncol, :, m * WIDTH:(m + 1) * WIDTH]
                buf[chunk, 0, h] = part.reshape(2 * ncol, WIDTH)

    def place(way, s):
        return 0 if s == 0 else 2 * s - 1 + way

    def push(chunk, first, count):
        j = chunk - KEPT
        for h in range(2):
            remote(
                buf.at[chunk, pl.ds(first, count)],
                buf.at[KEPT + LENT + hi * LENT + j, pl.ds(first, count)],
                xsend.at[h, j], xrecv.at[hi, j], side[h],
            ).start()

    def arrived(chunk, way, s):
        slab = buf.at[chunk, place(way, s)] if s < half else buf.at[chunk, nz - 1, way]
        wait(slab, zrecv.at[way, chunk, s - 1])

    def tick(chunk, s):
        for way, device in ((0, up), (1, down)):
            if s > 0:
                arrived(chunk, way, s)
            src = buf.at[chunk, place(way, s)]
            dst = buf.at[chunk, place(way, s + 1)]
            if s == half - 1:
                src, dst = src.at[way], buf.at[chunk, nz - 1, way]
            remote(src, dst, zsend.at[way, chunk], zrecv.at[way, chunk, s], device).start()
        if chunk >= KEPT:
            push(chunk, place(0, s), 1 if s == 0 else 2)

    def last(chunk):
        for way in range(2):
            arrived(chunk, way, half)
        if chunk >= KEPT:
            push(chunk, nz - 1, 1)

    window_col = row // 2
    in_w = lax.rem(window_col, 4)
    same_core = core == lax.rem(in_w, 2)
    same_line = jnp.logical_and(same_core, lo == in_w // 2)
    is_source = jnp.logical_and(same_line, y == window_col // 4)

    def window_y():
        @pl.when(is_source)
        def _():
            for b in range(2):
                @pl.when(lax.rem(row, 2) == b)
                def _():
                    wbuf[...] = buf[0, :, :, :, b * GSR:(b + 1) * GSR]
            for k, device in enumerate(in_column):
                remote(wbuf, wbuf, wsend.at[k], wrecv.at[0], device).start()

    def window_x():
        @pl.when(same_line)
        def _():
            @pl.when(jnp.logical_not(is_source))
            def _():
                wait(wbuf, wrecv.at[0])
            remote(wbuf, wbuf, wsend.at[ny - 1], wrecv.at[1], twin_lo).start()

    def window_core():
        @pl.when(same_core)
        def _():
            @pl.when(jnp.logical_not(same_line))
            def _():
                wait(wbuf, wrecv.at[1])
            remote(wbuf, wbuf, wsend.at[ny], wrecv.at[2], twin_core).start()

    def window_done():
        @pl.when(jnp.logical_not(same_core))
        def _():
            wait(wbuf, wrecv.at[2])
        loads[1].wait()
        loads[2].wait()
        for k in range(4):
            turned_gaps[k] = pltpu.roll(gaps[...], k * 32, 1)
        quarter = lax.broadcasted_iota(jnp.int32, (1, GSR), 1) // 32
        for b in range(pairs // GSR):
            line = jnp.zeros((1, GSR), jnp.float32)
            for q in range(4):
                at = 2 * b + q // 2
                away = half if at == nz - 1 else (at // 2 if at % 2 == 0 else -((at + 1) // 2))
                plane_at = lax.rem(z + away + nz, nz)
                shift = lax.rem(q + 4 - lax.rem(plane_at, 4), 4)
                piece = turned_gaps[shift, pl.ds(q % 2 * 4 + plane_at // 4, 1), :]
                line = jnp.where(quarter == q, piece, line)
            ordered_gaps[b:b + 1, :] = line
        gap = ordered_gaps[...]
        w_all = [
            -4.0 * gap / ((gap * gap + freqs[w] * freqs[w]) * math.sqrt(pairs)) for w in range(NW)
        ]
        flat = wbuf[...].reshape(pairs, GSR)
        for b in range(pairs // GSR):
            at = b * GSR
            turned = flat[at:at + GSR].astype(jnp.float32).T
            for w in range(NW):
                lhs[w * GSR:(w + 1) * GSR, at:at + GSR] = (turned * w_all[w][b:b + 1]).astype(jnp.bfloat16)

    def multiply(chunk):
        block = chunk if chunk < KEPT else chunk - LENT
        panel = buf[chunk].reshape(pairs, WIDTH)
        chi = jnp.dot(lhs[...], panel, preferred_element_type=jnp.float32)
        obuf[block] = chi.astype(jnp.bfloat16).reshape(NW, GSR, WIDTH)
        write(block).start()

    def write(block):
        return pltpu.make_async_copy(
            obuf.at[block], out.at[:, :, pl.ds(block * WIDTH, WIDTH)], osem.at[block]
        )

    def received(h, j):
        chunk = KEPT + LENT + h * LENT + j
        wait(buf.at[chunk], xrecv.at[h, j])
        multiply(chunk)

    order = ring_order(half)
    todo = {
        32: [lambda: last(0), window_y], 40: [window_x], 45: [window_core], 48: [window_done],
        42: [lambda: last(4)], 44: [lambda: last(5)],
        49: [lambda: multiply(0)], 51: [lambda: received(0, 0)], 52: [lambda: received(1, 0)],
        54: [lambda: received(0, 1)], 55: [lambda: received(1, 1)],
    }
    begin(0)
    for n, (chunk, s) in enumerate(order):
        if n == len(FIRST):
            begin(1)
        tick(chunk, s)
        for work in todo.get(n, ()):
            work()
    last(6)
    for chunk in (1, 2, 3):
        last(chunk)
        multiply(chunk)
    received(0, 2)
    received(1, 2)

    for chunk in range(KEPT + LENT):
        for way in range(2):
            wait(buf.at[chunk, pl.ds(0, nz - 1), 0], zsend.at[way, chunk])
    for j in range(LENT):
        for h in range(2):
            wait(buf.at[KEPT + j], xsend.at[h, j])
    for n, packed in enumerate((packed_a, packed_b)):
        wait(packed.at[pl.ds(0, plane - 1)], part_send.at[n])

    @pl.when(is_source)
    def _():
        for k in range(ny - 1):
            wait(wbuf, wsend.at[k])

    @pl.when(same_line)
    def _():
        wait(wbuf, wsend.at[ny - 1])

    @pl.when(same_core)
    def _():
        wait(wbuf, wsend.at[ny])

    for block in range(KEPT + 2 * LENT):
        write(block).wait()


def on_device(pair_elements, energy_gaps, frequencies):
    rows, cols = lax.axis_size("row"), lax.axis_size("col")
    local, full = pair_elements.shape
    pairs = local * rows * cols
    block = full // cols
    nz, ny = rows // 2, cols // 4
    depth = local * cols
    plane = 2 * cols
    dma = pltpu.SemaphoreType.DMA
    n_out = KEPT + 2 * LENT
    return pl.pallas_call(
        functools.partial(kernel, nz, ny, pairs),
        out_shape=jax.ShapeDtypeStruct((NW, GSR, block), jnp.bfloat16),
        in_specs=[pl.BlockSpec(memory_space=pl.ANY)] * 3,
        out_specs=pl.BlockSpec(memory_space=pl.ANY),
        scratch_shapes=[
            pltpu.VMEM((local, full), jnp.bfloat16),
            pltpu.VMEM((pairs // GSR, GSR), jnp.float32),
            pltpu.VMEM((4, pairs // GSR, GSR), jnp.float32),
            pltpu.VMEM((pairs // GSR, GSR), jnp.float32),
            pltpu.SMEM((NW,), jnp.float32),
            pltpu.VMEM((plane, local, len(FIRST) * WIDTH), jnp.bfloat16),
            pltpu.VMEM((plane, local, len(SECOND) * WIDTH), jnp.bfloat16),
            pltpu.VMEM((plane, local, len(FIRST) * WIDTH), jnp.bfloat16),
            pltpu.VMEM((plane, local, len(SECOND) * WIDTH), jnp.bfloat16),
            pltpu.VMEM((KEPT + 3 * LENT, nz, 2, depth, WIDTH), jnp.bfloat16),
            pltpu.VMEM((nz, 2, depth, GSR), jnp.bfloat16),
            pltpu.VMEM((NW * GSR, pairs), jnp.bfloat16),
            pltpu.VMEM((n_out, NW, GSR, WIDTH), jnp.bfloat16),
            dma((3,)),
            dma((2,)),
            dma((2,)),
            dma((2, KEPT + LENT, nz // 2)),
            dma((2, KEPT + LENT)),
            dma((2, LENT)),
            dma((2, LENT)),
            dma((3,)),
            dma((ny + 1,)),
            dma((n_out,)),
        ],
        compiler_params=pltpu.CompilerParams(
            collective_id=0, has_side_effects=True, vmem_limit_bytes=60 * 1024 * 1024
        ),
        cost_estimate=pl.CostEstimate(
            flops=2 * NW * GSR * pairs * block, bytes_accessed=2 * NW * GSR * block, transcendentals=0
        ),
    )(pair_elements, energy_gaps.reshape(pairs // GSR, GSR), frequencies)


def solution(mesh):
    in_specs = (P(("row", "col"), None), P(), P())
    out_specs = P(None, "row", "col")
    return jax.shard_map(
        on_device, mesh=mesh, in_specs=in_specs, out_specs=out_specs, check_vma=False
    )
```

```python
import functools
import math

import jax
import jax.numpy as jnp
from jax import lax
from jax.experimental import pallas as pl
from jax.experimental.pallas import tpu as pltpu
from jax.sharding import PartitionSpec as P

NW = 3
GSR = 128
WIDTH = 384
KEPT = 4
LENT = 3
OWN, LENDING = (0, 1, 2, 3), (4, 5, 6)
MESH = pl.DeviceIdType.MESH


def ring_order(steps):
    head, leaders = (0, 1, 2, 3, 4, 5), (0, 4, 5, 6)
    chunks = OWN + LENDING
    done = {chunk: 0 for chunk in chunks}
    seen = {chunk: -steps * len(chunks) for chunk in chunks}
    order = []
    while len(order) < steps * len(chunks):
        at = len(order)
        if at < len(head):
            pick = head[at]
        else:
            live = [c for c in chunks if done[c] < steps and (c != 6 or done[0] == steps)]
            ready = [c for c in live if at - seen[c] >= (3 if c == 6 else 4)] or [min(live, key=seen.get)]
            first = [c for c in leaders if c in ready]
            pick = first[0] if first else min(ready, key=done.get)
        order.append((pick, done[pick]))
        done[pick] += 1
        seen[pick] = at
    return order


def kernel(nz, ny, pairs, elements, gaps_in, freqs_in, out, gaps, turned_gaps, ordered_gaps, freqs, parts_own, parts_lent,
           buf, wbuf, lhs, obuf, in_sem, part_sem, part_recv, part_send,
           zrecv, zsend, xrecv, xsend, wrecv, wsend, osem):
    row, col = lax.axis_index("row"), lax.axis_index("col")
    hi, z = row // nz, lax.rem(row, nz)
    ncol = ny * 4
    plane = 2 * ncol
    seat = hi * ncol + col
    y = col // 4
    in_y = lax.rem(col, 4)
    lo, core = in_y // 2, lax.rem(in_y, 2)
    up = (hi * nz + lax.rem(z + 1, nz), col)
    down = (hi * nz + lax.rem(z + nz - 1, nz), col)
    other_lo = y * 4 + (1 - lo) * 2 + core
    side = [(z, other_lo), (nz + z, other_lo)]
    in_column = [(row, lax.rem(y + k, ny) * 4 + in_y) for k in (1, 3, 2)]
    twin_lo = (row, other_lo)
    twin_core = (row, y * 4 + lo * 2 + (1 - core))
    half = nz // 2

    barrier = pltpu.get_barrier_semaphore()

    bits = [core, lo, lax.rem(y, 2), y // 2, hi]

    def seated(mask):
        flip = [1 - bit if mask >> k & 1 else bit for k, bit in enumerate(bits)]
        return flip[4], flip[3] * 8 + flip[2] * 4 + flip[1] * 2 + flip[0]

    def hops(mask):
        return (0, 1, 2, 1)[mask >> 2 & 3] + (0, 1, 2, 1)[(mask >> 4 & 1) * 2 + (mask >> 1 & 1)]

    masks = sorted(range(1, plane), key=hops, reverse=True)
    others = {mask: seated(mask) for mask in masks}
    for device in [up, down] + [(h * nz + z, c) for h, c in others.values()]:
        pl.semaphore_signal(barrier, inc=1, device_id=device, device_id_type=MESH)

    loads = [
        pltpu.make_async_copy(gaps_in, gaps, in_sem.at[0]),
        pltpu.make_async_copy(freqs_in, freqs, in_sem.at[1]),
    ]
    for load in loads:
        load.start()

    def own_range(h, c):
        return elements.at[c, :, pl.ds(0, KEPT * WIDTH)]

    def lent_range(h, c):
        at = pl.multiple_of((KEPT + h * LENT) * WIDTH, 128)
        return elements.at[c + 2 - 4 * lax.rem(c // 2, 2), :, pl.ds(at, LENT * WIDTH)]

    ranges = ((own_range, parts_own), (lent_range, parts_lent))
    mine = [
        pltpu.make_async_copy(source(hi, col), parts.at[seat], part_sem.at[n])
        for n, (source, parts) in enumerate(ranges)
    ]
    for copy in mine:
        copy.start()
    pl.semaphore_wait(barrier, plane + 1)

    def remote(src, dst, send, recv, device):
        return pltpu.make_async_remote_copy(
            src_ref=src, dst_ref=dst, send_sem=send, recv_sem=recv, device_id=device, device_id_type=MESH
        )

    def wait(ref, sem):
        pltpu.make_async_copy(ref, ref, sem).wait()

    for n, (source, parts) in enumerate(ranges):
        for mask in masks:
            h, c = others[mask]
            remote(source(h, c), parts.at[seat], part_send.at[n], part_recv.at[n], (h * nz + z, c)).start()

    def begin(n, chunks):
        parts = ranges[n][1]
        mine[n].wait()
        wait(parts.at[pl.ds(0, plane - 1)], part_recv.at[n])
        for m, chunk in enumerate(chunks):
            for h in range(2):
                part = parts[h * ncol:(h + 1) * ncol, :, m * WIDTH:(m + 1) * WIDTH]
                buf[chunk, 0, h] = part.reshape(2 * ncol, WIDTH)

    def place(way, s):
        return 0 if s == 0 else 2 * s - 1 + way

    def push(chunk, first, count):
        j = chunk - KEPT
        for h in range(2):
            remote(
                buf.at[chunk, pl.ds(first, count)],
                buf.at[KEPT + LENT + hi * LENT + j, pl.ds(first, count)],
                xsend.at[h, j], xrecv.at[hi, j], side[h],
            ).start()

    def arrived(chunk, way, s):
        slab = buf.at[chunk, place(way, s)] if s < half else buf.at[chunk, nz - 1, way]
        wait(slab, zrecv.at[way, chunk, s - 1])

    def tick(chunk, s):
        for way, device in ((0, up), (1, down)):
            if s > 0:
                arrived(chunk, way, s)
            src = buf.at[chunk, place(way, s)]
            dst = buf.at[chunk, place(way, s + 1)]
            if s == half - 1:
                src, dst = src.at[way], buf.at[chunk, nz - 1, way]
            remote(src, dst, zsend.at[way, chunk], zrecv.at[way, chunk, s], device).start()
        if chunk >= KEPT:
            push(chunk, place(0, s), 1 if s == 0 else 2)

    def last(chunk):
        for way in range(2):
            arrived(chunk, way, half)
        if chunk >= KEPT:
            push(chunk, nz - 1, 1)

    window_col = row // 2
    in_w = lax.rem(window_col, 4)
    same_core = core == lax.rem(in_w, 2)
    same_line = jnp.logical_and(same_core, lo == in_w // 2)
    is_source = jnp.logical_and(same_line, y == window_col // 4)

    def window_y():
        @pl.when(is_source)
        def _():
            for b in range(2):
                @pl.when(lax.rem(row, 2) == b)
                def _():
                    wbuf[...] = buf[0, :, :, :, b * GSR:(b + 1) * GSR]
            for k, device in enumerate(in_column):
                remote(wbuf, wbuf, wsend.at[k], wrecv.at[0], device).start()

    def window_x():
        @pl.when(same_line)
        def _():
            @pl.when(jnp.logical_not(is_source))
            def _():
                wait(wbuf, wrecv.at[0])
            remote(wbuf, wbuf, wsend.at[ny - 1], wrecv.at[1], twin_lo).start()

    def window_core():
        @pl.when(same_core)
        def _():
            @pl.when(jnp.logical_not(same_line))
            def _():
                wait(wbuf, wrecv.at[1])
            remote(wbuf, wbuf, wsend.at[ny], wrecv.at[2], twin_core).start()

    def window_done():
        @pl.when(jnp.logical_not(same_core))
        def _():
            wait(wbuf, wrecv.at[2])
        for load in loads:
            load.wait()
        for k in range(4):
            turned_gaps[k] = pltpu.roll(gaps[...], k * 32, 1)
        quarter = lax.broadcasted_iota(jnp.int32, (1, GSR), 1) // 32
        for b in range(pairs // GSR):
            line = jnp.zeros((1, GSR), jnp.float32)
            for q in range(4):
                at = 2 * b + q // 2
                away = half if at == nz - 1 else (at // 2 if at % 2 == 0 else -((at + 1) // 2))
                plane_at = lax.rem(z + away + nz, nz)
                shift = lax.rem(q + 4 - lax.rem(plane_at, 4), 4)
                piece = turned_gaps[shift, pl.ds(q % 2 * 4 + plane_at // 4, 1), :]
                line = jnp.where(quarter == q, piece, line)
            ordered_gaps[b:b + 1, :] = line
        gap = ordered_gaps[...]
        w_all = [
            -4.0 * gap / ((gap * gap + freqs[w] * freqs[w]) * math.sqrt(pairs)) for w in range(NW)
        ]
        flat = wbuf[...].reshape(pairs, GSR)
        for b in range(pairs // GSR):
            at = b * GSR
            turned = flat[at:at + GSR].astype(jnp.float32).T
            for w in range(NW):
                lhs[w * GSR:(w + 1) * GSR, at:at + GSR] = (turned * w_all[w][b:b + 1]).astype(jnp.bfloat16)

    def multiply(chunk):
        block = chunk if chunk < KEPT else chunk - LENT
        panel = buf[chunk].reshape(pairs, WIDTH)
        chi = jnp.dot(lhs[...], panel, preferred_element_type=jnp.float32)
        obuf[block] = chi.astype(jnp.bfloat16).reshape(NW, GSR, WIDTH)
        write(block).start()

    def write(block):
        return pltpu.make_async_copy(
            obuf.at[block], out.at[:, :, pl.ds(block * WIDTH, WIDTH)], osem.at[block]
        )

    def received(h, j):
        chunk = KEPT + LENT + h * LENT + j
        wait(buf.at[chunk], xrecv.at[h, j])
        multiply(chunk)

    order = ring_order(half)
    end = {chunk: order.index((chunk, half - 1)) + 4 for chunk in range(KEPT + LENT)}
    todo = {
        end[0]: [lambda: last(0), window_y], end[4]: [lambda: last(4)], end[5]: [lambda: last(5)],
        41: [window_x], 45: [window_core], 48: [window_done],
        49: [lambda: multiply(0)], 51: [lambda: received(0, 0)], 53: [lambda: received(1, 0)],
        55: [lambda: last(6)],
    }
    begin(0, OWN)
    for n, (chunk, s) in enumerate(order):
        if n == len(OWN):
            begin(1, LENDING)
        tick(chunk, s)
        for work in todo.get(n, ()):
            work()
    received(0, 1)
    received(1, 1)
    for chunk in (1, 2, 3):
        last(chunk)
        multiply(chunk)
    received(0, 2)
    received(1, 2)

    for chunk in range(KEPT + LENT):
        for way in range(2):
            wait(buf.at[chunk, pl.ds(0, nz - 1), 0], zsend.at[way, chunk])
    for j in range(LENT):
        for h in range(2):
            wait(buf.at[KEPT + j], xsend.at[h, j])
    for n, (_, parts) in enumerate(ranges):
        wait(parts.at[pl.ds(0, plane - 1)], part_send.at[n])

    @pl.when(is_source)
    def _():
        for k in range(ny - 1):
            wait(wbuf, wsend.at[k])

    @pl.when(same_line)
    def _():
        wait(wbuf, wsend.at[ny - 1])

    @pl.when(same_core)
    def _():
        wait(wbuf, wsend.at[ny])

    for block in range(KEPT + 2 * LENT):
        write(block).wait()


def on_device(pair_elements, energy_gaps, frequencies):
    rows, cols = lax.axis_size("row"), lax.axis_size("col")
    local, full = pair_elements.shape
    pairs = local * rows * cols
    block = full // cols
    nz, ny = rows // 2, cols // 4
    depth = local * cols
    plane = 2 * cols
    dma = pltpu.SemaphoreType.DMA
    n_out = KEPT + 2 * LENT
    return pl.pallas_call(
        functools.partial(kernel, nz, ny, pairs),
        out_shape=jax.ShapeDtypeStruct((NW, GSR, block), jnp.bfloat16),
        in_specs=[pl.BlockSpec(memory_space=pl.ANY)] * 3,
        out_specs=pl.BlockSpec(memory_space=pl.ANY),
        scratch_shapes=[
            pltpu.VMEM((pairs // GSR, GSR), jnp.float32),
            pltpu.VMEM((4, pairs // GSR, GSR), jnp.float32),
            pltpu.VMEM((pairs // GSR, GSR), jnp.float32),
            pltpu.SMEM((NW,), jnp.float32),
            pltpu.VMEM((plane, local, KEPT * WIDTH), jnp.bfloat16),
            pltpu.VMEM((plane, local, LENT * WIDTH), jnp.bfloat16),
            pltpu.VMEM((KEPT + 3 * LENT, nz, 2, depth, WIDTH), jnp.bfloat16),
            pltpu.VMEM((nz, 2, depth, GSR), jnp.bfloat16),
            pltpu.VMEM((NW * GSR, pairs), jnp.bfloat16),
            pltpu.VMEM((n_out, NW, GSR, WIDTH), jnp.bfloat16),
            dma((2,)),
            dma((2,)),
            dma((2,)),
            dma((2,)),
            dma((2, KEPT + LENT, nz // 2)),
            dma((2, KEPT + LENT)),
            dma((2, LENT)),
            dma((2, LENT)),
            dma((3,)),
            dma((ny + 1,)),
            dma((n_out,)),
        ],
        compiler_params=pltpu.CompilerParams(
            collective_id=0, has_side_effects=True, vmem_limit_bytes=60 * 1024 * 1024
        ),
        cost_estimate=pl.CostEstimate(
            flops=2 * NW * GSR * pairs * block, bytes_accessed=2 * NW * GSR * block, transcendentals=0
        ),
    )(pair_elements.reshape(local, cols, block).transpose(1, 0, 2), energy_gaps.reshape(pairs // GSR, GSR), frequencies)


def solution(mesh):
    in_specs = (P(("row", "col"), None), P(), P())
    out_specs = P(None, "row", "col")
    return jax.shard_map(
        on_device, mesh=mesh, in_specs=in_specs, out_specs=out_specs, check_vma=False
    )
```

```python
import functools
import math

import jax
import jax.numpy as jnp
from jax import lax
from jax.experimental import pallas as pl
from jax.experimental.pallas import tpu as pltpu
from jax.sharding import PartitionSpec as P

NW = 3
GSR = 128
WIDTH = 384
KEPT = 6
LENT = 2
OWN = tuple(range(KEPT))
LENDING = tuple(range(KEPT, KEPT + LENT))
GAP = 4
MESH = pl.DeviceIdType.MESH


def ring_order(steps):
    total = steps * (KEPT + LENT)
    lent = []
    for first in range(0, LENT, 2):
        lent += [c for _ in range(steps) for c in LENDING[first:first + 2]]
    lent_at = [3 + round(i * 0.92 * total / len(lent)) for i in range(len(lent))]
    done = dict.fromkeys(OWN + LENDING, 0)
    seen = dict.fromkeys(OWN, -total)
    order = []
    for at in range(total):
        live = [c for c in OWN if done[c] < steps]
        if lent and (not live or lent_at[0] <= at):
            pick = lent.pop(0)
            lent_at.pop(0)
        else:
            ready = [c for c in live if at - seen[c] >= GAP] or [min(live, key=seen.get)]
            urgent = [c for c in ready if (steps - done[c]) * GAP >= total - at]
            if urgent and 0 not in ready:
                pick = min(urgent, key=done.get)
            else:
                pick = min(ready)
            seen[pick] = at
        order.append((pick, done[pick]))
        done[pick] += 1
    return order


def kernel(nz, ny, pairs, elements, gaps_in, freqs_in, out, gaps, turned_gaps, ordered_gaps, freqs, parts_own, parts_lent,
           buf, wbuf, lhs, obuf, in_sem, part_sem, part_recv, part_send,
           zrecv, zsend, xrecv, xsend, wrecv, wsend, osem):
    row, col = lax.axis_index("row"), lax.axis_index("col")
    hi, z = row // nz, lax.rem(row, nz)
    ncol = ny * 4
    plane = 2 * ncol
    seat = hi * ncol + col
    y = col // 4
    in_y = lax.rem(col, 4)
    lo, core = in_y // 2, lax.rem(in_y, 2)
    up = (hi * nz + lax.rem(z + 1, nz), col)
    down = (hi * nz + lax.rem(z + nz - 1, nz), col)
    other_lo = y * 4 + (1 - lo) * 2 + core
    side = [(z, other_lo), (nz + z, other_lo)]
    in_column = [(row, lax.rem(y + k, ny) * 4 + in_y) for k in (1, 3, 2)]
    twin_lo = (row, other_lo)
    twin_core = (row, y * 4 + lo * 2 + (1 - core))
    half = nz // 2

    barrier = pltpu.get_barrier_semaphore()

    bits = [core, lo, lax.rem(y, 2), y // 2, hi]

    def seated(mask):
        flip = [1 - bit if mask >> k & 1 else bit for k, bit in enumerate(bits)]
        return flip[4], flip[3] * 8 + flip[2] * 4 + flip[1] * 2 + flip[0]

    def hops(mask):
        return (0, 1, 2, 1)[mask >> 2 & 3] + (0, 1, 2, 1)[(mask >> 4 & 1) * 2 + (mask >> 1 & 1)]

    masks = sorted(range(1, plane), key=hops, reverse=True)
    others = {mask: seated(mask) for mask in masks}
    for device in [up, down] + [(h * nz + z, c) for h, c in others.values()]:
        pl.semaphore_signal(barrier, inc=1, device_id=device, device_id_type=MESH)

    loads = [
        pltpu.make_async_copy(gaps_in, gaps, in_sem.at[0]),
        pltpu.make_async_copy(freqs_in, freqs, in_sem.at[1]),
    ]
    for load in loads:
        load.start()

    def own_range(h, c):
        return elements.at[c, :, pl.ds(0, KEPT * WIDTH)]

    def lent_range(h, c):
        at = pl.multiple_of((KEPT + h * LENT) * WIDTH, 128)
        return elements.at[c + 2 - 4 * lax.rem(c // 2, 2), :, pl.ds(at, LENT * WIDTH)]

    ranges = ((own_range, parts_own), (lent_range, parts_lent))
    mine = [
        pltpu.make_async_copy(source(hi, col), parts.at[seat], part_sem.at[n])
        for n, (source, parts) in enumerate(ranges)
    ]
    for copy in mine:
        copy.start()
    pl.semaphore_wait(barrier, plane + 1)

    def remote(src, dst, send, recv, device):
        return pltpu.make_async_remote_copy(
            src_ref=src, dst_ref=dst, send_sem=send, recv_sem=recv, device_id=device, device_id_type=MESH
        )

    def wait(ref, sem):
        pltpu.make_async_copy(ref, ref, sem).wait()

    for n, (source, parts) in enumerate(ranges):
        for mask in masks:
            h, c = others[mask]
            remote(source(h, c), parts.at[seat], part_send.at[n], part_recv.at[n], (h * nz + z, c)).start()

    def begin(n, chunks):
        parts = ranges[n][1]
        mine[n].wait()
        wait(parts.at[pl.ds(0, plane - 1)], part_recv.at[n])
        for m, chunk in enumerate(chunks):
            for h in range(2):
                part = parts[h * ncol:(h + 1) * ncol, :, m * WIDTH:(m + 1) * WIDTH]
                buf[chunk, 0, h] = part.reshape(2 * ncol, WIDTH)

    def place(way, s):
        return 0 if s == 0 else 2 * s - 1 + way

    def push(chunk, first, count):
        j = chunk - KEPT
        for h in range(2):
            remote(
                buf.at[chunk, pl.ds(first, count)],
                buf.at[KEPT + LENT + hi * LENT + j, pl.ds(first, count)],
                xsend.at[h, j], xrecv.at[hi, j], side[h],
            ).start()

    def arrived(chunk, way, s):
        slab = buf.at[chunk, place(way, s)] if s < half else buf.at[chunk, nz - 1, way]
        wait(slab, zrecv.at[way, chunk, s - 1])

    def tick(chunk, s):
        for way, device in ((0, up), (1, down)):
            if s > 0:
                arrived(chunk, way, s)
            src = buf.at[chunk, place(way, s)]
            dst = buf.at[chunk, place(way, s + 1)]
            if s == half - 1:
                src, dst = src.at[way], buf.at[chunk, nz - 1, way]
            remote(src, dst, zsend.at[way, chunk], zrecv.at[way, chunk, s], device).start()
        if chunk >= KEPT:
            push(chunk, place(0, s), 1 if s == 0 else 2)

    def last(chunk):
        for way in range(2):
            arrived(chunk, way, half)
        if chunk >= KEPT:
            push(chunk, nz - 1, 1)

    window_col = row // 2
    in_w = lax.rem(window_col, 4)
    same_core = core == lax.rem(in_w, 2)
    same_line = jnp.logical_and(same_core, lo == in_w // 2)
    is_source = jnp.logical_and(same_line, y == window_col // 4)

    def window_y():
        @pl.when(is_source)
        def _():
            for b in range(2):
                @pl.when(lax.rem(row, 2) == b)
                def _():
                    wbuf[...] = buf[0, :, :, :, b * GSR:(b + 1) * GSR]
            for k, device in enumerate(in_column):
                remote(wbuf, wbuf, wsend.at[k], wrecv.at[0], device).start()

    def window_x():
        @pl.when(same_line)
        def _():
            @pl.when(jnp.logical_not(is_source))
            def _():
                wait(wbuf, wrecv.at[0])
            remote(wbuf, wbuf, wsend.at[ny - 1], wrecv.at[1], twin_lo).start()

    def window_core():
        @pl.when(same_core)
        def _():
            @pl.when(jnp.logical_not(same_line))
            def _():
                wait(wbuf, wrecv.at[1])
            remote(wbuf, wbuf, wsend.at[ny], wrecv.at[2], twin_core).start()

    def window_done():
        @pl.when(jnp.logical_not(same_core))
        def _():
            wait(wbuf, wrecv.at[2])
        for load in loads:
            load.wait()
        for k in range(4):
            turned_gaps[k] = pltpu.roll(gaps[...], k * 32, 1)
        quarter = lax.broadcasted_iota(jnp.int32, (1, GSR), 1) // 32
        for b in range(pairs // GSR):
            line = jnp.zeros((1, GSR), jnp.float32)
            for q in range(4):
                at = 2 * b + q // 2
                away = half if at == nz - 1 else (at // 2 if at % 2 == 0 else -((at + 1) // 2))
                plane_at = lax.rem(z + away + nz, nz)
                shift = lax.rem(q + 4 - lax.rem(plane_at, 4), 4)
                piece = turned_gaps[shift, pl.ds(q % 2 * 4 + plane_at // 4, 1), :]
                line = jnp.where(quarter == q, piece, line)
            ordered_gaps[b:b + 1, :] = line
        gap = ordered_gaps[...]
        w_all = [
            -4.0 * gap / ((gap * gap + freqs[w] * freqs[w]) * math.sqrt(pairs)) for w in range(NW)
        ]
        flat = wbuf[...].reshape(pairs, GSR)
        for b in range(pairs // GSR):
            at = b * GSR
            turned = flat[at:at + GSR].astype(jnp.float32).T
            for w in range(NW):
                lhs[w * GSR:(w + 1) * GSR, at:at + GSR] = (turned * w_all[w][b:b + 1]).astype(jnp.bfloat16)

    def multiply(chunk):
        block = chunk if chunk < KEPT else chunk - LENT
        panel = buf[chunk].reshape(pairs, WIDTH)
        chi = jnp.dot(lhs[...], panel, preferred_element_type=jnp.float32)
        obuf[block] = chi.astype(jnp.bfloat16).reshape(NW, GSR, WIDTH)
        write(block).start()

    def write(block):
        return pltpu.make_async_copy(
            obuf.at[block], out.at[:, :, pl.ds(block * WIDTH, WIDTH)], osem.at[block]
        )

    def received(h, j):
        chunk = KEPT + LENT + h * LENT + j
        wait(buf.at[chunk], xrecv.at[h, j])
        multiply(chunk)

    order = ring_order(half)
    final = len(order) - 1
    end = {chunk: order.index((chunk, half - 1)) + GAP for chunk in OWN + LENDING}
    window = end[0]
    todo = {}

    def plan(at, *work):
        todo.setdefault(min(at, final), []).extend(work)

    for chunk, at in end.items():
        plan(at, functools.partial(last, chunk))
    plan(window, window_y)
    plan(window + 8, window_x)
    plan(window + 12, window_core)
    plan(window + 15, window_done)
    at = window + 16
    for chunk in sorted(OWN, key=end.get):
        at = max(at, end[chunk])
        plan(at, functools.partial(multiply, chunk))
        at += 2
    begin(0, OWN)
    for n, (chunk, s) in enumerate(order):
        if n == 3:
            begin(1, LENDING)
        tick(chunk, s)
        for work in todo.get(n, ()):
            work()
    for j in range(LENT):
        for h in range(2):
            received(h, j)

    for chunk in range(KEPT + LENT):
        for way in range(2):
            wait(buf.at[chunk, pl.ds(0, nz - 1), 0], zsend.at[way, chunk])
    for j in range(LENT):
        for h in range(2):
            wait(buf.at[KEPT + j], xsend.at[h, j])
    for n, (_, parts) in enumerate(ranges):
        wait(parts.at[pl.ds(0, plane - 1)], part_send.at[n])

    @pl.when(is_source)
    def _():
        for k in range(ny - 1):
            wait(wbuf, wsend.at[k])

    @pl.when(same_line)
    def _():
        wait(wbuf, wsend.at[ny - 1])

    @pl.when(same_core)
    def _():
        wait(wbuf, wsend.at[ny])

    for block in range(KEPT + 2 * LENT):
        write(block).wait()


def on_device(pair_elements, energy_gaps, frequencies):
    rows, cols = lax.axis_size("row"), lax.axis_size("col")
    local, full = pair_elements.shape
    pairs = local * rows * cols
    block = full // cols
    nz, ny = rows // 2, cols // 4
    depth = local * cols
    plane = 2 * cols
    dma = pltpu.SemaphoreType.DMA
    n_out = KEPT + 2 * LENT
    return pl.pallas_call(
        functools.partial(kernel, nz, ny, pairs),
        out_shape=jax.ShapeDtypeStruct((NW, GSR, block), jnp.bfloat16),
        in_specs=[pl.BlockSpec(memory_space=pl.ANY)] * 3,
        out_specs=pl.BlockSpec(memory_space=pl.ANY),
        scratch_shapes=[
            pltpu.VMEM((pairs // GSR, GSR), jnp.float32),
            pltpu.VMEM((4, pairs // GSR, GSR), jnp.float32),
            pltpu.VMEM((pairs // GSR, GSR), jnp.float32),
            pltpu.SMEM((NW,), jnp.float32),
            pltpu.VMEM((plane, local, KEPT * WIDTH), jnp.bfloat16),
            pltpu.VMEM((plane, local, LENT * WIDTH), jnp.bfloat16),
            pltpu.VMEM((KEPT + 3 * LENT, nz, 2, depth, WIDTH), jnp.bfloat16),
            pltpu.VMEM((nz, 2, depth, GSR), jnp.bfloat16),
            pltpu.VMEM((NW * GSR, pairs), jnp.bfloat16),
            pltpu.VMEM((n_out, NW, GSR, WIDTH), jnp.bfloat16),
            dma((2,)),
            dma((2,)),
            dma((2,)),
            dma((2,)),
            dma((2, KEPT + LENT, nz // 2)),
            dma((2, KEPT + LENT)),
            dma((2, LENT)),
            dma((2, LENT)),
            dma((3,)),
            dma((ny + 1,)),
            dma((n_out,)),
        ],
        compiler_params=pltpu.CompilerParams(
            collective_id=0, has_side_effects=True, vmem_limit_bytes=60 * 1024 * 1024
        ),
        cost_estimate=pl.CostEstimate(
            flops=2 * NW * GSR * pairs * block, bytes_accessed=2 * NW * GSR * block, transcendentals=0
        ),
    )(pair_elements.reshape(local, cols, block).transpose(1, 0, 2), energy_gaps.reshape(pairs // GSR, GSR), frequencies)


def solution(mesh):
    in_specs = (P(("row", "col"), None), P(), P())
    out_specs = P(None, "row", "col")
    return jax.shard_map(
        on_device, mesh=mesh, in_specs=in_specs, out_specs=out_specs, check_vma=False
    )
```

```python
import functools
import math

import jax
import jax.numpy as jnp
from jax import lax
from jax.experimental import pallas as pl
from jax.experimental.pallas import tpu as pltpu
from jax.sharding import PartitionSpec as P

NW = 3
GSR = 128
WIDTH = 640
KEPT = 2
LENT = 2
ROUNDS = ((2, 0), (3, 1))
MESH = pl.DeviceIdType.MESH


def kernel(nz, ny, pairs, elements, gaps_in, freqs_in, out, gaps, turned_gaps, weights, freqs,
           parts_own, parts_lent, buf, wbuf, lhs, obuf, in_sem, part_sem, part_recv, part_send,
           zrecv, zsend, xrecv, xsend, wrecv, wsend, osem):
    row, col = lax.axis_index("row"), lax.axis_index("col")
    hi, z = row // nz, lax.rem(row, nz)
    ncol = ny * 4
    plane = 2 * ncol
    seat = hi * ncol + col
    y = col // 4
    in_y = lax.rem(col, 4)
    lo, core = in_y // 2, lax.rem(in_y, 2)
    up = (hi * nz + lax.rem(z + 1, nz), col)
    down = (hi * nz + lax.rem(z + nz - 1, nz), col)
    other_lo = y * 4 + (1 - lo) * 2 + core
    side = [(z, other_lo), (nz + z, other_lo)]
    in_column = [(row, lax.rem(y + k, ny) * 4 + in_y) for k in (1, 3, 2)]
    twin_lo = (row, other_lo)
    twin_core = (row, y * 4 + lo * 2 + (1 - core))
    half = nz // 2

    def seated(k):
        to = lax.rem(seat + k, plane)
        return to // ncol, lax.rem(to, ncol)

    barrier = pltpu.get_barrier_semaphore()
    for device in (up, down):
        pl.semaphore_signal(barrier, inc=1, device_id=device, device_id_type=MESH)

    @pl.loop(1, plane)
    def _(k):
        h, c = seated(k)
        pl.semaphore_signal(barrier, inc=1, device_id=(h * nz + z, c), device_id_type=MESH)

    loads = [
        pltpu.make_async_copy(gaps_in, gaps, in_sem.at[0]),
        pltpu.make_async_copy(freqs_in, freqs, in_sem.at[1]),
    ]
    for load in loads:
        load.start()

    def own_range(h, c):
        return elements.at[c, :, pl.ds(0, KEPT * WIDTH)]

    def lent_range(h, c):
        at = pl.multiple_of((KEPT + h * LENT) * WIDTH, 128)
        return elements.at[c + 2 - 4 * lax.rem(c // 2, 2), :, pl.ds(at, LENT * WIDTH)]

    ranges = ((lent_range, parts_lent), (own_range, parts_own))
    mine = [
        pltpu.make_async_copy(source(hi, col), parts.at[seat], part_sem.at[n])
        for n, (source, parts) in enumerate(ranges)
    ]
    for copy in mine:
        copy.start()
    pl.semaphore_wait(barrier, plane + 1)

    def remote(src, dst, send, recv, device):
        return pltpu.make_async_remote_copy(
            src_ref=src, dst_ref=dst, send_sem=send, recv_sem=recv, device_id=device, device_id_type=MESH
        )

    def wait(ref, sem):
        pltpu.make_async_copy(ref, ref, sem).wait()

    for n, (source, parts) in enumerate(ranges):
        @pl.loop(1, plane)
        def _(k):
            h, c = seated(k)
            remote(source(h, c), parts.at[seat], part_send.at[n], part_recv.at[n], (h * nz + z, c)).start()

    for load in loads:
        load.wait()
    for k in range(4):
        turned_gaps[k] = pltpu.roll(gaps[...], k * 32, 1)
    quarter = lax.broadcasted_iota(jnp.int32, (1, GSR), 1) // 32

    @pl.loop(0, pairs // GSR)
    def _(b):
        line = jnp.zeros((1, GSR), jnp.float32)
        for q in range(4):
            at = lax.rem(b, 4) * 4 + q
            away = (at + 1) // 2 if q % 2 == 0 else nz - (at + 1) // 2
            if q % 2 == 1:
                away = lax.rem(away, nz)
            plane_at = lax.rem(z + away, nz)
            shift = lax.rem(q + 4 - lax.rem(plane_at, 4), 4)
            piece = turned_gaps[shift, pl.ds(b // 4 * 4 + plane_at // 4, 1), :]
            line = jnp.where(quarter == q, piece, line)
        for w in range(NW):
            weights[w, pl.ds(b, 1), :] = (
                -4.0 * line / ((line * line + freqs[w] * freqs[w]) * math.sqrt(pairs))
            )

    def begin(n, chunk, m):
        parts = ranges[n][1]
        for h in range(2):
            part = parts[h * ncol:(h + 1) * ncol, :, m * WIDTH:(m + 1) * WIDTH]
            buf[chunk, h, 0] = part.reshape(2 * ncol, WIDTH)

    def place(way, s):
        return 2 * s - 1 + way

    def push(chunk, h, first, count):
        j = chunk - KEPT
        for n in range(2):
            remote(
                buf.at[chunk, h, pl.ds(first, count)],
                buf.at[KEPT + LENT + hi * LENT + j, h, pl.ds(first, count)],
                xsend.at[n, j], xrecv.at[hi, j], side[n],
            ).start()

    def arrived(chunk, h, way, s):
        at = place(way, s) if not isinstance(s, int) or s < half else nz - 1
        wait(buf.at[chunk, h, at], zrecv.at[way, chunk, h, s - 1])

    def tick(chunk, h, s):
        first, final = isinstance(s, int) and s == 0, isinstance(s, int) and s == half - 1
        for way, device in ((0, up), (1, down)):
            if not first:
                arrived(chunk, h, way, s)
            if final and way != h:
                continue
            src = 0 if first else place(way, s)
            dst = nz - 1 if final else place(way, s + 1)
            remote(
                buf.at[chunk, h, src], buf.at[chunk, h, dst],
                zsend.at[way, chunk, h], zrecv.at[way, chunk, h, s], device,
            ).start()
        if chunk >= KEPT:
            if first:
                push(chunk, h, 0, 1)
            else:
                push(chunk, h, place(0, s), 2)

    def last(chunk):
        for h in range(2):
            arrived(chunk, h, h, half)
            if chunk >= KEPT:
                push(chunk, h, nz - 1, 1)

    def ticks(n, low, high):
        if high - low == 1:
            for chunk in ROUNDS[n]:
                for h in range(2):
                    tick(chunk, h, low)
        else:
            @pl.loop(low, high)
            def _(s):
                for chunk in ROUNDS[n]:
                    for h in range(2):
                        tick(chunk, h, s)

    window_col = row // 2
    in_w = lax.rem(window_col, 4)
    same_core = core == lax.rem(in_w, 2)
    same_line = jnp.logical_and(same_core, lo == in_w // 2)
    is_source = jnp.logical_and(same_line, y == window_col // 4)

    def window_y():
        @pl.when(is_source)
        def _():
            for b in range(2):
                @pl.when(lax.rem(row, 2) == b)
                def _():
                    wbuf[...] = buf[0, :, :, :, b * GSR:(b + 1) * GSR]
            for k, device in enumerate(in_column):
                remote(wbuf, wbuf, wsend.at[k], wrecv.at[0], device).start()

    def window_x():
        @pl.when(same_line)
        def _():
            @pl.when(jnp.logical_not(is_source))
            def _():
                wait(wbuf, wrecv.at[0])
            remote(wbuf, wbuf, wsend.at[ny - 1], wrecv.at[1], twin_lo).start()

    def window_core():
        @pl.when(same_core)
        def _():
            @pl.when(jnp.logical_not(same_line))
            def _():
                wait(wbuf, wrecv.at[1])
            remote(wbuf, wbuf, wsend.at[ny], wrecv.at[2], twin_core).start()

    def window_done():
        @pl.when(jnp.logical_not(same_core))
        def _():
            wait(wbuf, wrecv.at[2])

        @pl.loop(0, pairs // GSR)
        def _(b):
            at = pl.multiple_of(b * GSR, GSR)
            block = wbuf[b // 4, pl.ds(lax.rem(b, 4) * 4, 4)].reshape(GSR, GSR)
            turned = block.astype(jnp.float32).T
            for w in range(NW):
                lhs[w * GSR:(w + 1) * GSR, pl.ds(at, GSR)] = (
                    turned * weights[w, pl.ds(b, 1), :]
                ).astype(jnp.bfloat16)

    def write(block, chunk):
        at = pl.multiple_of(block * WIDTH, 128)
        return pltpu.make_async_copy(obuf.at[block], out.at[:, :, pl.ds(at, WIDTH)], osem.at[block])

    def received(n, j):
        wait(buf.at[KEPT + LENT + n * LENT + j], xrecv.at[n, j])

    for n, (lent, own) in enumerate(ROUNDS):
        if n == 0:
            mine[0].wait()
            wait(parts_lent.at[pl.ds(0, plane - 1)], part_recv.at[0])
        begin(0, lent, n)
        for h in range(2):
            tick(lent, h, 0)
        if n == 0:
            mine[1].wait()
            wait(parts_own.at[pl.ds(0, plane - 1)], part_recv.at[1])
        begin(1, own, n)
        for h in range(2):
            tick(own, h, 0)
        if n == 0:
            ticks(0, 1, half - 1)
        else:
            for chunk in ROUNDS[0]:
                last(chunk)
            window_y()
            ticks(1, 1, 3)
            window_x()
            ticks(1, 3, 5)
            window_core()
            ticks(1, 5, half - 1)
        ticks(n, half - 1, half)
    window_done()

    @pl.loop(0, KEPT + 2 * LENT)
    def _(i):
        for n in range(2):
            @pl.when(i == 1 + n)
            def _():
                received(n, 0)

            @pl.when(i == 4 + n)
            def _():
                received(n, 1)

        @pl.when(i == 1)
        def _():
            last(3)

        @pl.when(i == 3)
        def _():
            last(1)

        second, place_in = i // 3, lax.rem(i, 3)
        other = (place_in + 1) // 2
        block = second + other * (KEPT + (place_in - 1) * LENT)
        chunk = block + other * LENT
        panel = buf[chunk].reshape(pairs, WIDTH)
        chi = jnp.dot(lhs[...], panel, preferred_element_type=jnp.float32)
        obuf[block] = chi.astype(jnp.bfloat16).reshape(NW, GSR, WIDTH)
        write(block, chunk).start()

    for chunk in range(KEPT + LENT):
        for way in range(2):
            for h in range(2):
                wait(buf.at[chunk, h, pl.ds(0, half if way == h else half - 1)], zsend.at[way, chunk, h])
    for j in range(LENT):
        for n in range(2):
            wait(buf.at[KEPT + j], xsend.at[n, j])
    for n, (_, parts) in enumerate(ranges):
        wait(parts.at[pl.ds(0, plane - 1)], part_send.at[n])

    @pl.when(is_source)
    def _():
        for k in range(ny - 1):
            wait(wbuf, wsend.at[k])

    @pl.when(same_line)
    def _():
        wait(wbuf, wsend.at[ny - 1])

    @pl.when(same_core)
    def _():
        wait(wbuf, wsend.at[ny])

    for block in range(KEPT + 2 * LENT):
        write(block, block).wait()


def on_device(pair_elements, energy_gaps, frequencies):
    rows, cols = lax.axis_size("row"), lax.axis_size("col")
    local, full = pair_elements.shape
    pairs = local * rows * cols
    block = full // cols
    nz, ny = rows // 2, cols // 4
    depth = local * cols
    plane = 2 * cols
    dma = pltpu.SemaphoreType.DMA
    n_out = KEPT + 2 * LENT
    return pl.pallas_call(
        functools.partial(kernel, nz, ny, pairs),
        out_shape=jax.ShapeDtypeStruct((NW, GSR, block), jnp.bfloat16),
        in_specs=[pl.BlockSpec(memory_space=pl.ANY)] * 3,
        out_specs=pl.BlockSpec(memory_space=pl.ANY),
        scratch_shapes=[
            pltpu.VMEM((pairs // GSR, GSR), jnp.float32),
            pltpu.VMEM((4, pairs // GSR, GSR), jnp.float32),
            pltpu.VMEM((NW, pairs // GSR, GSR), jnp.float32),
            pltpu.SMEM((NW,), jnp.float32),
            pltpu.VMEM((plane, local, KEPT * WIDTH), jnp.bfloat16),
            pltpu.VMEM((plane, local, LENT * WIDTH), jnp.bfloat16),
            pltpu.VMEM((KEPT + 3 * LENT, 2, nz, depth, WIDTH), jnp.bfloat16),
            pltpu.VMEM((2, nz, depth, GSR), jnp.bfloat16),
            pltpu.VMEM((NW * GSR, pairs), jnp.bfloat16),
            pltpu.VMEM((n_out, NW, GSR, WIDTH), jnp.bfloat16),
            dma((2,)),
            dma((2,)),
            dma((2,)),
            dma((2,)),
            dma((2, KEPT + LENT, 2, nz // 2)),
            dma((2, KEPT + LENT, 2)),
            dma((2, LENT)),
            dma((2, LENT)),
            dma((3,)),
            dma((ny + 1,)),
            dma((n_out,)),
        ],
        compiler_params=pltpu.CompilerParams(
            collective_id=0, has_side_effects=True, vmem_limit_bytes=60 * 1024 * 1024
        ),
        cost_estimate=pl.CostEstimate(
            flops=2 * NW * GSR * pairs * block, bytes_accessed=2 * NW * GSR * block, transcendentals=0
        ),
    )(
        pair_elements.reshape(local, cols, block).transpose(1, 0, 2),
        energy_gaps.reshape(pairs // GSR, GSR),
        frequencies,
    )


def solution(mesh):
    in_specs = (P(("row", "col"), None), P(), P())
    out_specs = P(None, "row", "col")
    return jax.shard_map(
        on_device, mesh=mesh, in_specs=in_specs, out_specs=out_specs, check_vma=False
    )
```

```python
import functools
import math

import jax
import jax.numpy as jnp
from jax import lax
from jax.experimental import pallas as pl
from jax.experimental.pallas import tpu as pltpu
from jax.sharding import PartitionSpec as P

NW = 3
GSR = 128
OWN = (512, 1024)
LENT = (512, 640)
MESH = pl.DeviceIdType.MESH


def kernel(nz, ny, pairs, elements, gaps_in, freqs_in, out, gaps, turned_gaps, weights, freqs,
           parts_own, parts_lent, own_a, own_b, lent_a, lent_b, got_a, got_b, wbuf, lhs,
           out_own_a, out_own_b, out_a, out_b, in_sem, part_sem, part_recv, part_send,
           zrecv, zsend, xrecv, xsend, wrecv, wsend, osem):
    row, col = lax.axis_index("row"), lax.axis_index("col")
    hi, z = row // nz, lax.rem(row, nz)
    ncol = ny * 4
    plane = 2 * ncol
    seat = hi * ncol + col
    y = col // 4
    in_y = lax.rem(col, 4)
    lo, core = in_y // 2, lax.rem(in_y, 2)
    up = (hi * nz + lax.rem(z + 1, nz), col)
    down = (hi * nz + lax.rem(z + nz - 1, nz), col)
    other_lo = y * 4 + (1 - lo) * 2 + core
    side = [(z, other_lo), (nz + z, other_lo)]
    in_column = [(row, lax.rem(y + k, ny) * 4 + in_y) for k in (1, 3, 2)]
    twin_lo = (row, other_lo)
    twin_core = (row, y * 4 + lo * 2 + (1 - core))
    half = nz // 2

    def seated(k):
        to = lax.rem(seat + k, plane)
        return to // ncol, lax.rem(to, ncol)

    barrier = pltpu.get_barrier_semaphore()
    for device in (up, down):
        pl.semaphore_signal(barrier, inc=1, device_id=device, device_id_type=MESH)

    @pl.loop(1, plane)
    def _(k):
        h, c = seated(k)
        pl.semaphore_signal(barrier, inc=1, device_id=(h * nz + z, c), device_id_type=MESH)

    loads = [
        pltpu.make_async_copy(gaps_in, gaps, in_sem.at[0]),
        pltpu.make_async_copy(freqs_in, freqs, in_sem.at[1]),
    ]
    for load in loads:
        load.start()

    def own_range(h, c):
        return elements.at[c, :, pl.ds(0, sum(OWN))]

    def lent_range(h, c):
        at = pl.multiple_of(sum(OWN) + h * sum(LENT), 128)
        return elements.at[c + 2 - 4 * lax.rem(c // 2, 2), :, pl.ds(at, sum(LENT))]

    ranges = ((lent_range, parts_lent), (own_range, parts_own))
    mine = [
        pltpu.make_async_copy(source(hi, col), parts.at[seat], part_sem.at[n])
        for n, (source, parts) in enumerate(ranges)
    ]
    for copy in mine:
        copy.start()
    pl.semaphore_wait(barrier, plane + 1)

    def remote(src, dst, send, recv, device):
        return pltpu.make_async_remote_copy(
            src_ref=src, dst_ref=dst, send_sem=send, recv_sem=recv, device_id=device, device_id_type=MESH
        )

    def wait(ref, sem):
        pltpu.make_async_copy(ref, ref, sem).wait()

    for n, (source, parts) in enumerate(ranges):
        @pl.loop(1, plane)
        def _(k):
            h, c = seated(k)
            remote(source(h, c), parts.at[seat], part_send.at[n], part_recv.at[n], (h * nz + z, c)).start()

    for load in loads:
        load.wait()
    for k in range(4):
        turned_gaps[k] = pltpu.roll(gaps[...], k * 32, 1)
    quarter = lax.broadcasted_iota(jnp.int32, (1, GSR), 1) // 32

    @pl.loop(0, pairs // GSR)
    def _(b):
        line = jnp.zeros((1, GSR), jnp.float32)
        for q in range(4):
            at = lax.rem(b, 4) * 4 + q
            away = (at + 1) // 2 if q % 2 == 0 else nz - (at + 1) // 2
            if q % 2 == 1:
                away = lax.rem(away, nz)
            plane_at = lax.rem(z + away, nz)
            shift = lax.rem(q + 4 - lax.rem(plane_at, 4), 4)
            piece = turned_gaps[shift, pl.ds(b // 4 * 4 + plane_at // 4, 1), :]
            line = jnp.where(quarter == q, piece, line)
        for w in range(NW):
            weights[w, pl.ds(b, 1), :] = (
                -4.0 * line / ((line * line + freqs[w] * freqs[w]) * math.sqrt(pairs))
            )

    bufs = (own_a, own_b, lent_a, lent_b)
    got = (got_a, got_b)
    rounds = ((2, 0), (3, 1))

    def begin(chunk):
        parts = (parts_own, parts_lent)[chunk // 2]
        start, width = ((0, OWN[0]), (OWN[0], OWN[1]), (0, LENT[0]), (LENT[0], LENT[1]))[chunk]
        for h in range(2):
            part = parts[h * ncol:(h + 1) * ncol, :, start:start + width]
            bufs[chunk][h, 0] = part.reshape(2 * ncol, width)

    def place(way, s):
        return 2 * s - 1 + way

    def push(chunk, h, first, count):
        j = chunk - 2
        for n in range(2):
            remote(
                bufs[chunk].at[h, pl.ds(first, count)], got[j].at[hi, h, pl.ds(first, count)],
                xsend.at[n, j], xrecv.at[hi, j], side[n],
            ).start()

    def arrived(chunk, h, way, s):
        at = place(way, s) if not isinstance(s, int) or s < half else nz - 1
        wait(bufs[chunk].at[h, at], zrecv.at[way, chunk, h, s - 1])

    def tick(chunk, h, s):
        first, final = isinstance(s, int) and s == 0, isinstance(s, int) and s == half - 1
        buf = bufs[chunk]
        for way, device in ((0, up), (1, down)):
            if not first:
                arrived(chunk, h, way, s)
            if final and way != h:
                continue
            src = 0 if first else place(way, s)
            dst = nz - 1 if final else place(way, s + 1)
            remote(
                buf.at[h, src], buf.at[h, dst],
                zsend.at[way, chunk, h], zrecv.at[way, chunk, h, s], device,
            ).start()
        if chunk >= 2:
            if first:
                push(chunk, h, 0, 1)
            else:
                push(chunk, h, place(0, s), 2)

    def last(chunk):
        for h in range(2):
            arrived(chunk, h, h, half)
            if chunk >= 2:
                push(chunk, h, nz - 1, 1)

    def ticks(n, low, high):
        if high - low == 1:
            for chunk in rounds[n]:
                for h in range(2):
                    tick(chunk, h, low)
        else:
            @pl.loop(low, high)
            def _(s):
                for chunk in rounds[n]:
                    for h in range(2):
                        tick(chunk, h, s)

    window_col = row // 2
    in_w = lax.rem(window_col, 4)
    same_core = core == lax.rem(in_w, 2)
    same_line = jnp.logical_and(same_core, lo == in_w // 2)
    is_source = jnp.logical_and(same_line, y == window_col // 4)

    def window_y():
        @pl.when(is_source)
        def _():
            for b in range(2):
                @pl.when(lax.rem(row, 2) == b)
                def _():
                    wbuf[...] = own_a[:, :, :, b * GSR:(b + 1) * GSR]
            for k, device in enumerate(in_column):
                remote(wbuf, wbuf, wsend.at[k], wrecv.at[0], device).start()

    def window_x():
        @pl.when(same_line)
        def _():
            @pl.when(jnp.logical_not(is_source))
            def _():
                wait(wbuf, wrecv.at[0])
            remote(wbuf, wbuf, wsend.at[ny - 1], wrecv.at[1], twin_lo).start()

    def window_core():
        @pl.when(same_core)
        def _():
            @pl.when(jnp.logical_not(same_line))
            def _():
                wait(wbuf, wrecv.at[1])
            remote(wbuf, wbuf, wsend.at[ny], wrecv.at[2], twin_core).start()

    def window_done():
        @pl.when(jnp.logical_not(same_core))
        def _():
            wait(wbuf, wrecv.at[2])

        @pl.loop(0, pairs // GSR)
        def _(b):
            at = pl.multiple_of(b * GSR, GSR)
            block = wbuf[b // 4, pl.ds(lax.rem(b, 4) * 4, 4)].reshape(GSR, GSR)
            turned = block.astype(jnp.float32).T
            for w in range(NW):
                lhs[w * GSR:(w + 1) * GSR, pl.ds(at, GSR)] = (
                    turned * weights[w, pl.ds(b, 1), :]
                ).astype(jnp.bfloat16)

    def multiply(buf, to, at, sem):
        width = buf.shape[-1]
        chi = jnp.dot(lhs[...], buf[...].reshape(pairs, width), preferred_element_type=jnp.float32)
        to[...] = chi.astype(jnp.bfloat16).reshape(NW, GSR, width)
        write(to, at, sem).start()

    def write(to, at, sem):
        return pltpu.make_async_copy(to, out.at[:, :, pl.ds(at, to.shape[-1])], osem.at[sem])

    def place_of(h, j):
        return pl.multiple_of(sum(OWN) + h * sum(LENT) + j * LENT[0], 128)

    for n, (lent, own) in enumerate(rounds):
        if n == 0:
            mine[0].wait()
            wait(parts_lent.at[pl.ds(0, plane - 1)], part_recv.at[0])
        begin(lent)
        for h in range(2):
            tick(lent, h, 0)
        if n == 0:
            mine[1].wait()
            wait(parts_own.at[pl.ds(0, plane - 1)], part_recv.at[1])
        begin(own)
        for h in range(2):
            tick(own, h, 0)
        if n == 0:
            ticks(0, 1, half - 1)
        else:
            for chunk in rounds[0]:
                last(chunk)
            window_y()
            ticks(1, 1, 3)
            window_x()
            ticks(1, 3, 5)
            window_core()
            ticks(1, 5, half - 1)
            window_done()
        ticks(n, half - 1, half)

    multiply(own_a, out_own_a, 0, 0)
    last(3)
    for j in range(2):
        if j == 1:
            last(1)
            multiply(own_b, out_own_b, OWN[0], 1)

        @pl.loop(0, 2)
        def _(h):
            wait(got[j].at[h], xrecv.at[h, j])
            multiply(got[j].at[h], (out_a, out_b)[j].at[h], place_of(h, j), 2 + 2 * j + h)

    for chunk in range(4):
        for way in range(2):
            for h in range(2):
                wait(bufs[chunk].at[h, pl.ds(0, half if way == h else half - 1)], zsend.at[way, chunk, h])
    for j in range(2):
        for n in range(2):
            wait(bufs[2 + j], xsend.at[n, j])
    for n, (_, parts) in enumerate(ranges):
        wait(parts.at[pl.ds(0, plane - 1)], part_send.at[n])

    @pl.when(is_source)
    def _():
        for k in range(ny - 1):
            wait(wbuf, wsend.at[k])

    @pl.when(same_line)
    def _():
        wait(wbuf, wsend.at[ny - 1])

    @pl.when(same_core)
    def _():
        wait(wbuf, wsend.at[ny])

    write(out_own_a, 0, 0).wait()
    write(out_own_b, OWN[0], 1).wait()
    for j in range(2):
        for h in range(2):
            write((out_a, out_b)[j].at[h], place_of(h, j), 2 + 2 * j + h).wait()


def on_device(pair_elements, energy_gaps, frequencies):
    rows, cols = lax.axis_size("row"), lax.axis_size("col")
    local, full = pair_elements.shape
    pairs = local * rows * cols
    block = full // cols
    nz, ny = rows // 2, cols // 4
    depth = local * cols
    plane = 2 * cols
    dma = pltpu.SemaphoreType.DMA

    def panels(*shape):
        return pltpu.VMEM(shape[:-1] + (2, nz, depth) + shape[-1:], jnp.bfloat16)

    def results(*shape):
        return pltpu.VMEM(shape[:-1] + (NW, GSR) + shape[-1:], jnp.bfloat16)

    return pl.pallas_call(
        functools.partial(kernel, nz, ny, pairs),
        out_shape=jax.ShapeDtypeStruct((NW, GSR, block), jnp.bfloat16),
        in_specs=[pl.BlockSpec(memory_space=pl.ANY)] * 3,
        out_specs=pl.BlockSpec(memory_space=pl.ANY),
        scratch_shapes=[
            pltpu.VMEM((pairs // GSR, GSR), jnp.float32),
            pltpu.VMEM((4, pairs // GSR, GSR), jnp.float32),
            pltpu.VMEM((NW, pairs // GSR, GSR), jnp.float32),
            pltpu.SMEM((NW,), jnp.float32),
            pltpu.VMEM((plane, local, sum(OWN)), jnp.bfloat16),
            pltpu.VMEM((plane, local, sum(LENT)), jnp.bfloat16),
            panels(OWN[0]),
            panels(OWN[1]),
            panels(LENT[0]),
            panels(LENT[1]),
            panels(2, LENT[0]),
            panels(2, LENT[1]),
            pltpu.VMEM((2, nz, depth, GSR), jnp.bfloat16),
            pltpu.VMEM((NW * GSR, pairs), jnp.bfloat16),
            results(OWN[0]),
            results(OWN[1]),
            results(2, LENT[0]),
            results(2, LENT[1]),
            dma((2,)),
            dma((2,)),
            dma((2,)),
            dma((2,)),
            dma((2, 4, 2, nz // 2)),
            dma((2, 4, 2)),
            dma((2, 2)),
            dma((2, 2)),
            dma((3,)),
            dma((ny + 1,)),
            dma((6,)),
        ],
        compiler_params=pltpu.CompilerParams(
            collective_id=0, has_side_effects=True, vmem_limit_bytes=60 * 1024 * 1024
        ),
        cost_estimate=pl.CostEstimate(
            flops=2 * NW * GSR * pairs * block, bytes_accessed=2 * NW * GSR * block, transcendentals=0
        ),
    )(
        pair_elements.reshape(local, cols, block).transpose(1, 0, 2),
        energy_gaps.reshape(pairs // GSR, GSR),
        frequencies,
    )


def solution(mesh):
    in_specs = (P(("row", "col"), None), P(), P())
    out_specs = P(None, "row", "col")
    return jax.shard_map(
        on_device, mesh=mesh, in_specs=in_specs, out_specs=out_specs, check_vma=False
    )
```

```python
import functools
import math

import jax
import jax.numpy as jnp
from jax import lax
from jax.experimental import pallas as pl
from jax.experimental.pallas import tpu as pltpu
from jax.sharding import PartitionSpec as P

NW = 3
GSR = 128
OWN = (640, 896)
LENT = (640, 512)
MESH = pl.DeviceIdType.MESH


def kernel(nz, ny, pairs, elements, gaps_in, freqs_in, out, gaps, turned_gaps, weights, freqs,
           packed_a, packed_b, parts_a, parts_b, own_a, own_b, lent_a, lent_b, got_a, got_b, wbuf, lhs,
           out_own_a, out_own_b, out_a, out_b, in_sem, pack_sem, part_recv, part_send,
           zrecv, zsend, xrecv, xsend, wrecv, wsend, osem):
    row, col = lax.axis_index("row"), lax.axis_index("col")
    hi, z = row // nz, lax.rem(row, nz)
    ncol = ny * 4
    plane = 2 * ncol
    seat = hi * ncol + col
    y = col // 4
    in_y = lax.rem(col, 4)
    lo, core = in_y // 2, lax.rem(in_y, 2)
    up = (hi * nz + lax.rem(z + 1, nz), col)
    down = (hi * nz + lax.rem(z + nz - 1, nz), col)
    other_lo = y * 4 + (1 - lo) * 2 + core
    side = [(z, other_lo), (nz + z, other_lo)]
    in_column = [(row, lax.rem(y + k, ny) * 4 + in_y) for k in (1, 3, 2)]
    twin_lo = (row, other_lo)
    twin_core = (row, y * 4 + lo * 2 + (1 - core))
    half = nz // 2

    def seated(k):
        to = lax.rem(seat + k, plane)
        return to // ncol, lax.rem(to, ncol) // 4, lax.rem(to, 4) // 2, lax.rem(to, 2)

    def device_at(h, y, lo, core):
        return h * nz + z, y * 4 + lo * 2 + core

    barrier = pltpu.get_barrier_semaphore()
    for device in (up, down):
        pl.semaphore_signal(barrier, inc=1, device_id=device, device_id_type=MESH)

    @pl.loop(1, plane)
    def _(k):
        pl.semaphore_signal(barrier, inc=1, device_id=device_at(*seated(k)), device_id_type=MESH)

    packing = []
    for n, packed in enumerate((packed_a, packed_b)):
        lent_at, own_at = sum(LENT[:n]), sum(OWN[:n])
        for h in range(2):
            for to in range(2):
                packing.append(pltpu.make_async_copy(
                    elements.at[:, 1 - to, :, :, pl.ds(sum(OWN) + h * sum(LENT) + lent_at, LENT[n])],
                    packed.at[h, :, to, :, :, pl.ds(0, LENT[n])], pack_sem.at[n, 2 * h + to],
                ))
            packing.append(pltpu.make_async_copy(
                elements.at[:, :, :, :, pl.ds(own_at, OWN[n])],
                packed.at[h, :, :, :, :, pl.ds(LENT[n], OWN[n])], pack_sem.at[n, 4 + h],
            ))
    for copy in packing:
        copy.start()
    loads = [
        pltpu.make_async_copy(gaps_in, gaps, in_sem.at[0]),
        pltpu.make_async_copy(freqs_in, freqs, in_sem.at[1]),
    ]
    for load in loads:
        load.start()

    for copy in packing[:6]:
        copy.wait()
    pl.semaphore_wait(barrier, plane + 1)

    def remote(src, dst, send, recv, device):
        return pltpu.make_async_remote_copy(
            src_ref=src, dst_ref=dst, send_sem=send, recv_sem=recv, device_id=device, device_id_type=MESH
        )

    def wait(ref, sem):
        pltpu.make_async_copy(ref, ref, sem).wait()

    def exchange(n):
        packed, parts = ((packed_a, parts_a), (packed_b, parts_b))[n]

        @pl.loop(1, plane)
        def _(k):
            to = seated(k)
            remote(packed.at[to], parts.at[seat], part_send.at[n], part_recv.at[n], device_at(*to)).start()

        parts[seat] = packed[hi, y, lo, core]

    exchange(0)

    for load in loads:
        load.wait()
    for k in range(4):
        turned_gaps[k] = pltpu.roll(gaps[...], k * 32, 1)
    quarter = lax.broadcasted_iota(jnp.int32, (1, GSR), 1) // 32

    @pl.loop(0, pairs // GSR)
    def _(b):
        line = jnp.zeros((1, GSR), jnp.float32)
        for q in range(4):
            at = lax.rem(b, 4) * 4 + q
            away = (at + 1) // 2 if q % 2 == 0 else nz - (at + 1) // 2
            if q % 2 == 1:
                away = lax.rem(away, nz)
            plane_at = lax.rem(z + away, nz)
            shift = lax.rem(q + 4 - lax.rem(plane_at, 4), 4)
            piece = turned_gaps[shift, pl.ds(b // 4 * 4 + plane_at // 4, 1), :]
            line = jnp.where(quarter == q, piece, line)
        for w in range(NW):
            weights[w, pl.ds(b, 1), :] = (
                -4.0 * line / ((line * line + freqs[w] * freqs[w]) * math.sqrt(pairs))
            )

    bufs = (own_a, own_b, lent_a, lent_b)
    got = (got_a, got_b)
    rounds = ((2, 0), (3, 1))

    def begin(chunk):
        n, parts = chunk % 2, (parts_a, parts_b)[chunk % 2]
        start, width = (0, LENT[n]) if chunk >= 2 else (LENT[n], OWN[n])
        for h in range(2):
            part = parts[h * ncol:(h + 1) * ncol, :, start:start + width]
            bufs[chunk][h, 0] = part.reshape(2 * ncol, width)

    def place(way, s):
        return 2 * s - 1 + way

    def push(chunk, first, count):
        j = chunk - 2
        for n in range(2):
            remote(
                bufs[chunk].at[:, pl.ds(first, count)], got[j].at[hi, :, pl.ds(first, count)],
                xsend.at[n, j], xrecv.at[hi, j], side[n],
            ).start()

    def arrived(chunk, h, way, s):
        at = place(way, s) if not isinstance(s, int) or s < half else nz - 1
        wait(bufs[chunk].at[h, at], zrecv.at[way, chunk, h, s - 1])

    def tick(chunk, h, s):
        first, final = isinstance(s, int) and s == 0, isinstance(s, int) and s == half - 1
        buf = bufs[chunk]
        for way, device in ((0, up), (1, down)):
            if not first:
                arrived(chunk, h, way, s)
            if final and way != h:
                continue
            src = 0 if first else place(way, s)
            dst = nz - 1 if final else place(way, s + 1)
            remote(
                buf.at[h, src], buf.at[h, dst],
                zsend.at[way, chunk, h], zrecv.at[way, chunk, h, s], device,
            ).start()

    def last(chunk):
        for h in range(2):
            arrived(chunk, h, h, half)
        if chunk >= 2:
            push(chunk, nz - 1, 1)

    def ticks(n, low, high):
        def one(s):
            for chunk in rounds[n]:
                for h in range(2):
                    tick(chunk, h, s)
            push(rounds[n][0], place(0, s), 2)

        if high - low == 1:
            one(low)
        else:
            pl.loop(low, high)(one)

    window_col = row // 2
    in_w = lax.rem(window_col, 4)
    same_core = core == lax.rem(in_w, 2)
    same_line = jnp.logical_and(same_core, lo == in_w // 2)
    is_source = jnp.logical_and(same_line, y == window_col // 4)

    def window_y():
        @pl.when(is_source)
        def _():
            for b in range(2):
                @pl.when(lax.rem(row, 2) == b)
                def _():
                    wbuf[...] = own_a[:, :, :, b * GSR:(b + 1) * GSR]
            for k, device in enumerate(in_column):
                remote(wbuf, wbuf, wsend.at[k], wrecv.at[0], device).start()

    def window_x():
        @pl.when(same_line)
        def _():
            @pl.when(jnp.logical_not(is_source))
            def _():
                wait(wbuf, wrecv.at[0])
            remote(wbuf, wbuf, wsend.at[ny - 1], wrecv.at[1], twin_lo).start()

    def window_core():
        @pl.when(same_core)
        def _():
            @pl.when(jnp.logical_not(same_line))
            def _():
                wait(wbuf, wrecv.at[1])
            remote(wbuf, wbuf, wsend.at[ny], wrecv.at[2], twin_core).start()

    def window_done():
        @pl.when(jnp.logical_not(same_core))
        def _():
            wait(wbuf, wrecv.at[2])

        @pl.loop(0, pairs // GSR)
        def _(b):
            at = pl.multiple_of(b * GSR, GSR)
            block = wbuf[b // 4, pl.ds(lax.rem(b, 4) * 4, 4)].reshape(GSR, GSR)
            turned = block.astype(jnp.float32).T
            for w in range(NW):
                lhs[w * GSR:(w + 1) * GSR, pl.ds(at, GSR)] = (
                    turned * weights[w, pl.ds(b, 1), :]
                ).astype(jnp.bfloat16)

    def multiply(buf, to, at, sem):
        width = buf.shape[-1]
        chi = jnp.dot(lhs[...], buf[...].reshape(pairs, width), preferred_element_type=jnp.float32)
        to[...] = chi.astype(jnp.bfloat16).reshape(NW, GSR, width)
        write(to, at, sem).start()

    def write(to, at, sem):
        return pltpu.make_async_copy(to, out.at[:, :, pl.ds(at, to.shape[-1])], osem.at[sem])

    def place_of(h, j):
        return pl.multiple_of(sum(OWN) + h * sum(LENT) + j * LENT[0], 128)

    for n, (lent, own) in enumerate(rounds):
        parts = (parts_a, parts_b)[n]
        wait(parts.at[pl.ds(0, plane - 1)], part_recv.at[n])
        for chunk in (lent, own):
            begin(chunk)
            for h in range(2):
                tick(chunk, h, 0)
            if chunk == lent:
                push(chunk, 0, 1)
        if n == 0:
            for copy in packing[6:]:
                copy.wait()
            exchange(1)
            ticks(0, 1, half - 1)
        else:
            for chunk in rounds[0]:
                last(chunk)
            window_y()
            ticks(1, 1, 4)
            window_x()
            ticks(1, 4, 6)
            window_core()
            ticks(1, 6, half - 1)
            window_done()
        ticks(n, half - 1, half)

    multiply(own_a, out_own_a, 0, 0)
    last(3)
    for j in range(2):
        if j == 1:
            last(1)
            multiply(own_b, out_own_b, OWN[0], 1)

        @pl.loop(0, 2)
        def _(h):
            wait(got[j].at[h], xrecv.at[h, j])
            multiply(got[j].at[h], (out_a, out_b)[j].at[h], place_of(h, j), 2 + 2 * j + h)

    for chunk in range(4):
        for way in range(2):
            for h in range(2):
                wait(bufs[chunk].at[h, pl.ds(0, half if way == h else half - 1)], zsend.at[way, chunk, h])
    for j in range(2):
        for n in range(2):
            wait(bufs[2 + j], xsend.at[n, j])
    for n, parts in enumerate((parts_a, parts_b)):
        wait(parts.at[pl.ds(0, plane - 1)], part_send.at[n])

    @pl.when(is_source)
    def _():
        for k in range(ny - 1):
            wait(wbuf, wsend.at[k])

    @pl.when(same_line)
    def _():
        wait(wbuf, wsend.at[ny - 1])

    @pl.when(same_core)
    def _():
        wait(wbuf, wsend.at[ny])

    write(out_own_a, 0, 0).wait()
    write(out_own_b, OWN[0], 1).wait()
    for j in range(2):
        for h in range(2):
            write((out_a, out_b)[j].at[h], place_of(h, j), 2 + 2 * j + h).wait()


def on_device(pair_elements, energy_gaps, frequencies):
    rows, cols = lax.axis_size("row"), lax.axis_size("col")
    local, full = pair_elements.shape
    pairs = local * rows * cols
    block = full // cols
    nz, ny = rows // 2, cols // 4
    depth = local * cols
    plane = 2 * cols
    dma = pltpu.SemaphoreType.DMA

    def panels(*shape):
        return pltpu.VMEM(shape[:-1] + (2, nz, depth) + shape[-1:], jnp.bfloat16)

    def results(*shape):
        return pltpu.VMEM(shape[:-1] + (NW, GSR) + shape[-1:], jnp.bfloat16)

    operands = [
        pltpu.with_memory_space_constraint(operand, pltpu.HBM)
        for operand in (
            pair_elements.reshape(local, ny, 2, 2, block).transpose(1, 2, 3, 0, 4),
            energy_gaps.reshape(pairs // GSR, GSR),
            frequencies,
        )
    ]
    return pl.pallas_call(
        functools.partial(kernel, nz, ny, pairs),
        out_shape=jax.ShapeDtypeStruct((NW, GSR, block), jnp.bfloat16),
        in_specs=[pl.BlockSpec(memory_space=pl.ANY)] * 3,
        out_specs=pl.BlockSpec(memory_space=pl.ANY),
        scratch_shapes=[
            pltpu.VMEM((pairs // GSR, GSR), jnp.float32),
            pltpu.VMEM((4, pairs // GSR, GSR), jnp.float32),
            pltpu.VMEM((NW, pairs // GSR, GSR), jnp.float32),
            pltpu.SMEM((NW,), jnp.float32),
            pltpu.VMEM((2, ny, 2, 2, local, LENT[0] + OWN[0]), jnp.bfloat16),
            pltpu.VMEM((2, ny, 2, 2, local, LENT[1] + OWN[1]), jnp.bfloat16),
            pltpu.VMEM((plane, local, LENT[0] + OWN[0]), jnp.bfloat16),
            pltpu.VMEM((plane, local, LENT[1] + OWN[1]), jnp.bfloat16),
            panels(OWN[0]),
            panels(OWN[1]),
            panels(LENT[0]),
            panels(LENT[1]),
            panels(2, LENT[0]),
            panels(2, LENT[1]),
            pltpu.VMEM((2, nz, depth, GSR), jnp.bfloat16),
            pltpu.VMEM((NW * GSR, pairs), jnp.bfloat16),
            results(OWN[0]),
            results(OWN[1]),
            results(2, LENT[0]),
            results(2, LENT[1]),
            dma((2,)),
            dma((2, 6)),
            dma((2,)),
            dma((2,)),
            dma((2, 4, 2, nz // 2)),
            dma((2, 4, 2)),
            dma((2, 2)),
            dma((2, 2)),
            dma((3,)),
            dma((ny + 1,)),
            dma((6,)),
        ],
        compiler_params=pltpu.CompilerParams(
            collective_id=0, has_side_effects=True, vmem_limit_bytes=36 * 1024 * 1024
        ),
        cost_estimate=pl.CostEstimate(
            flops=2 * NW * GSR * pairs * block, bytes_accessed=2 * NW * GSR * block, transcendentals=0
        ),
    )(*operands)


def solution(mesh):
    in_specs = (P(("row", "col"), None), P(), P())
    out_specs = P(None, "row", "col")
    return jax.shard_map(
        on_device, mesh=mesh, in_specs=in_specs, out_specs=out_specs, check_vma=False
    )
```

```python
import functools
import math

import jax
import jax.numpy as jnp
from jax import lax
from jax.experimental import pallas as pl
from jax.experimental.pallas import tpu as pltpu
from jax.sharding import PartitionSpec as P

NW = 3
GSR = 128
WINDOW = 256
OWN = 1280
LENT = 1152
EARLY = 12
MESH = pl.DeviceIdType.MESH


def kernel(nz, ny, pairs, elements, gaps_in, freqs_in, out, gaps, turned_gaps, weights, freqs,
           packed_a, packed_b, parts_a, parts_b, win, own, lent, got, wbuf, lhs,
           sum_own, sum_got, out_win, out_own, out_got, in_sem, pack_sem, part_recv, part_send,
           nrecv, nsend, zrecv, zsend, xrecv, xsend, wrecv, wsend, osem):
    row, col = lax.axis_index("row"), lax.axis_index("col")
    hi, z = row // nz, lax.rem(row, nz)
    ncol = ny * 4
    plane = 2 * ncol
    seat = hi * ncol + col
    y = col // 4
    in_y = lax.rem(col, 4)
    lo, core = in_y // 2, lax.rem(in_y, 2)
    up = (hi * nz + lax.rem(z + 1, nz), col)
    down = (hi * nz + lax.rem(z + nz - 1, nz), col)
    other_lo = y * 4 + (1 - lo) * 2 + core
    side = [(z, other_lo), (nz + z, other_lo)]
    in_column = [(row, lax.rem(y + k, ny) * 4 + in_y) for k in (1, 3, 2)]
    twin_lo = (row, other_lo)
    twin_core = (row, y * 4 + lo * 2 + (1 - core))
    half = nz // 2

    def seated(k):
        to = lax.rem(seat + k, plane)
        return to // ncol, lax.rem(to, ncol) // 4, lax.rem(to, 4) // 2, lax.rem(to, 2)

    def device_at(h, y, lo, core):
        return h * nz + z, y * 4 + lo * 2 + core

    barrier = pltpu.get_barrier_semaphore()
    for device in (up, down):
        pl.semaphore_signal(barrier, inc=1, device_id=device, device_id_type=MESH)

    @pl.loop(1, plane)
    def _(k):
        pl.semaphore_signal(barrier, inc=1, device_id=device_at(*seated(k)), device_id_type=MESH)

    packing = []
    for h in range(2):
        for to in range(2):
            packing.append(pltpu.make_async_copy(
                elements.at[:, 1 - to, :, :, pl.ds(WINDOW + OWN + h * LENT, LENT)],
                packed_a.at[h, :, to, :, :, pl.ds(WINDOW, LENT)], pack_sem.at[2 * h + to],
            ))
        packing.append(pltpu.make_async_copy(
            elements.at[:, :, :, :, pl.ds(0, WINDOW)],
            packed_a.at[h, :, :, :, :, pl.ds(0, WINDOW)], pack_sem.at[4 + h],
        ))
    for h in range(2):
        packing.append(pltpu.make_async_copy(
            elements.at[:, :, :, :, pl.ds(WINDOW, OWN)], packed_b.at[h], pack_sem.at[6 + h],
        ))
    for copy in packing:
        copy.start()
    loads = [
        pltpu.make_async_copy(gaps_in, gaps, in_sem.at[0]),
        pltpu.make_async_copy(freqs_in, freqs, in_sem.at[1]),
    ]
    for load in loads:
        load.start()

    for copy in packing[:6]:
        copy.wait()
    pl.semaphore_wait(barrier, plane + 1)

    def remote(src, dst, send, recv, device):
        return pltpu.make_async_remote_copy(
            src_ref=src, dst_ref=dst, send_sem=send, recv_sem=recv, device_id=device, device_id_type=MESH
        )

    def wait(ref, sem):
        pltpu.make_async_copy(ref, ref, sem).wait()

    def exchange(n):
        packed, parts = ((packed_a, parts_a), (packed_b, parts_b))[n]

        @pl.loop(1, plane)
        def _(k):
            to = seated(k)
            remote(packed.at[to], parts.at[seat], part_send.at[n], part_recv.at[n], device_at(*to)).start()

        parts[seat] = packed[hi, y, lo, core]

    exchange(0)

    for load in loads:
        load.wait()
    for k in range(4):
        turned_gaps[k] = pltpu.roll(gaps[...], k * 32, 1)
    quarter = lax.broadcasted_iota(jnp.int32, (1, GSR), 1) // 32

    @pl.loop(0, pairs // GSR)
    def _(b):
        line = jnp.zeros((1, GSR), jnp.float32)
        for q in range(4):
            plane_at = lax.rem(z + (b if q < 2 else nz - 1 - b), nz)
            shift = lax.rem(q + 4 - lax.rem(plane_at, 4), 4)
            piece = turned_gaps[shift, pl.ds(q % 2 * 4 + plane_at // 4, 1), :]
            line = jnp.where(quarter == q, piece, line)
        for w in range(NW):
            weights[w, pl.ds(b, 1), :] = (
                -4.0 * line / ((line * line + freqs[w] * freqs[w]) * math.sqrt(pairs))
            )

    bufs = (lent, own)

    def begin(buf, parts, start):
        width = buf.shape[-1]
        for h in range(2):
            part = parts[h * ncol:(h + 1) * ncol, :, start:start + width]
            buf[0, h] = part.reshape(2 * ncol, width)

    def place(way, s):
        return 0 if s == 0 else nz - 1 if s == half else 2 * s - 1 + way

    def push(first, count):
        late = int(first > EARLY)
        for n in range(2):
            remote(
                lent.at[pl.ds(first, count)], got.at[hi, pl.ds(first, count)],
                xsend.at[n], xrecv.at[hi, late], side[n],
            ).start()

    def arrived(n, h, way, s):
        wait(bufs[n].at[place(way, s), h], zrecv.at[way, n, h, s - 1])

    def tick(n, s):
        for h in range(2):
            for way, device in ((0, up), (1, down)):
                if s > 0:
                    arrived(n, h, way, s)
                if s == half - 1 and way != h:
                    continue
                remote(
                    bufs[n].at[place(way, s), h], bufs[n].at[place(way, s + 1), h],
                    zsend.at[way, n, h], zrecv.at[way, n, h, s], device,
                ).start()

    def last(n):
        for h in range(2):
            arrived(n, h, h, half)

    def window_arrived(way, s):
        slab = win.at[place(way, s)]
        wait(slab.at[way] if s == half else slab, nrecv.at[way, s - 1])

    def window_tick(s):
        for way, device in ((0, up), (1, down)):
            if s > 0:
                window_arrived(way, s)
            src, dst = win.at[place(way, s)], win.at[place(way, s + 1)]
            if s == half - 1:
                src, dst = src.at[way], dst.at[way]
            remote(src, dst, nsend.at[way], nrecv.at[way, s], device).start()

    window_col = row // 2
    in_w = lax.rem(window_col, 4)
    same_core = core == lax.rem(in_w, 2)
    same_line = jnp.logical_and(same_core, lo == in_w // 2)
    is_source = jnp.logical_and(same_line, y == window_col // 4)

    def window_y():
        @pl.when(is_source)
        def _():
            for b in range(2):
                @pl.when(lax.rem(row, 2) == b)
                def _():
                    wbuf[...] = win[:, :, :, b * GSR:(b + 1) * GSR]
            for k, device in enumerate(in_column):
                remote(wbuf, wbuf, wsend.at[k], wrecv.at[0], device).start()

    def window_x():
        @pl.when(same_line)
        def _():
            @pl.when(jnp.logical_not(is_source))
            def _():
                wait(wbuf, wrecv.at[0])
            remote(wbuf, wbuf, wsend.at[ny - 1], wrecv.at[1], twin_lo).start()

    def window_core():
        @pl.when(same_core)
        def _():
            @pl.when(jnp.logical_not(same_line))
            def _():
                wait(wbuf, wrecv.at[1])
            remote(wbuf, wbuf, wsend.at[ny], wrecv.at[2], twin_core).start()

    def window_done():
        @pl.when(jnp.logical_not(same_core))
        def _():
            wait(wbuf, wrecv.at[2])

        @pl.loop(0, pairs // GSR)
        def _(b):
            at = pl.multiple_of(b * GSR, GSR)
            block = wbuf[pl.ds(b * 2, 2)].reshape(GSR, GSR)
            turned = block.astype(jnp.float32).T
            for w in range(NW):
                lhs[w * GSR:(w + 1) * GSR, pl.ds(at, GSR)] = (
                    turned * weights[w, pl.ds(b, 1), :]
                ).astype(jnp.bfloat16)

    early = EARLY * 4 * ncol

    def product(panel, low, high):
        return jnp.dot(
            lhs[:, low:high], panel.reshape(high - low, panel.shape[-1]), preferred_element_type=jnp.float32
        )

    def finish(chi, to, at, sem):
        to[...] = chi.astype(jnp.bfloat16).reshape(to.shape)
        write(to, at, sem).start()

    def write(to, at, sem):
        return pltpu.make_async_copy(to, out.at[:, :, pl.ds(at, to.shape[-1])], osem.at[sem])

    def lent_at(h):
        return pl.multiple_of(WINDOW + OWN + h * LENT, 128)

    wait(parts_a.at[pl.ds(0, plane - 1)], part_recv.at[0])
    begin(win, parts_a, 0)
    window_tick(0)
    begin(lent, parts_a, WINDOW)
    for t in range(half + 1):
        if 0 < t < half // 2:
            window_tick(2 * t)
        if t == half // 2:
            for way in range(2):
                window_arrived(way, half)
            window_y()
        if t < half:
            tick(0, t)
        else:
            last(0)
        push(*((0, 1) if t == 0 else (nz - 1, 1) if t == half else (place(0, t), 2)))
        if t == 0:
            for copy in packing[6:]:
                copy.wait()
            exchange(1)
        if t < half // 2:
            window_tick(2 * t + 1)
        if t == 1:
            wait(parts_b.at[pl.ds(0, plane - 1)], part_recv.at[1])
            begin(own, parts_b, 0)
        if t > 0:
            tick(1, t - 1)
        if t == half // 2 + 1:
            window_x()
        if t == half // 2 + 2:
            window_core()
        if t == half // 2 + 3:
            window_done()

    finish(product(win[...], 0, pairs), out_win, 0, 0)
    sum_own[...] = product(own[:EARLY], 0, early)

    @pl.loop(0, 2)
    def _(h):
        wait(got.at[h, pl.ds(0, EARLY + 1)], xrecv.at[h, 0])
        sum_got[h] = product(got[h, :EARLY], 0, early)

    last(1)
    finish(sum_own[...] + product(own[EARLY:], early, pairs), out_own, WINDOW, 1)

    @pl.loop(0, 2)
    def _(h):
        wait(got.at[h, pl.ds(EARLY + 1, nz - EARLY - 1)], xrecv.at[h, 1])
        finish(sum_got[h] + product(got[h, EARLY:], early, pairs), out_got.at[h], lent_at(h), 2 + h)

    for way in range(2):
        wait(win.at[pl.ds(0, nz - 1), 0], nsend.at[way])
        for n in range(2):
            for h in range(2):
                wait(bufs[n].at[pl.ds(0, half if way == h else half - 1), h], zsend.at[way, n, h])
    for n in range(2):
        wait(lent, xsend.at[n])
    for n, parts in enumerate((parts_a, parts_b)):
        wait(parts.at[pl.ds(0, plane - 1)], part_send.at[n])

    @pl.when(is_source)
    def _():
        for k in range(ny - 1):
            wait(wbuf, wsend.at[k])

    @pl.when(same_line)
    def _():
        wait(wbuf, wsend.at[ny - 1])

    @pl.when(same_core)
    def _():
        wait(wbuf, wsend.at[ny])

    write(out_win, 0, 0).wait()
    write(out_own, WINDOW, 1).wait()
    for h in range(2):
        write(out_got.at[h], lent_at(h), 2 + h).wait()


def on_device(pair_elements, energy_gaps, frequencies):
    rows, cols = lax.axis_size("row"), lax.axis_size("col")
    local, full = pair_elements.shape
    pairs = local * rows * cols
    block = full // cols
    nz, ny = rows // 2, cols // 4
    depth = local * cols
    plane = 2 * cols
    dma = pltpu.SemaphoreType.DMA

    def panels(width):
        return pltpu.VMEM((nz, 2, depth, width), jnp.bfloat16)

    def results(width):
        return pltpu.VMEM((NW, GSR, width), jnp.bfloat16)

    operands = [
        pltpu.with_memory_space_constraint(operand, pltpu.HBM)
        for operand in (
            pair_elements.reshape(local, ny, 2, 2, block).transpose(1, 2, 3, 0, 4),
            energy_gaps.reshape(pairs // GSR, GSR),
            frequencies,
        )
    ]
    return pl.pallas_call(
        functools.partial(kernel, nz, ny, pairs),
        out_shape=jax.ShapeDtypeStruct((NW, GSR, block), jnp.bfloat16),
        in_specs=[pl.BlockSpec(memory_space=pl.ANY)] * 3,
        out_specs=pl.BlockSpec(memory_space=pl.ANY),
        scratch_shapes=[
            pltpu.VMEM((pairs // GSR, GSR), jnp.float32),
            pltpu.VMEM((4, pairs // GSR, GSR), jnp.float32),
            pltpu.VMEM((NW, pairs // GSR, GSR), jnp.float32),
            pltpu.SMEM((NW,), jnp.float32),
            pltpu.VMEM((2, ny, 2, 2, local, WINDOW + LENT), jnp.bfloat16),
            pltpu.VMEM((2, ny, 2, 2, local, OWN), jnp.bfloat16),
            pltpu.VMEM((plane, local, WINDOW + LENT), jnp.bfloat16),
            pltpu.VMEM((plane, local, OWN), jnp.bfloat16),
            panels(WINDOW),
            panels(OWN),
            panels(LENT),
            pltpu.VMEM((2, nz, 2, depth, LENT), jnp.bfloat16),
            panels(GSR),
            pltpu.VMEM((NW * GSR, pairs), jnp.bfloat16),
            pltpu.VMEM((NW * GSR, OWN), jnp.float32),
            pltpu.VMEM((2, NW * GSR, LENT), jnp.float32),
            results(WINDOW),
            results(OWN),
            pltpu.VMEM((2, NW, GSR, LENT), jnp.bfloat16),
            dma((2,)),
            dma((8,)),
            dma((2,)),
            dma((2,)),
            dma((2, nz // 2)),
            dma((2,)),
            dma((2, 2, 2, nz // 2)),
            dma((2, 2, 2)),
            dma((2, 2)),
            dma((2,)),
            dma((3,)),
            dma((ny + 1,)),
            dma((4,)),
        ],
        compiler_params=pltpu.CompilerParams(
            collective_id=0, has_side_effects=True, vmem_limit_bytes=36 * 1024 * 1024
        ),
        cost_estimate=pl.CostEstimate(
            flops=2 * NW * GSR * pairs * block, bytes_accessed=2 * NW * GSR * block, transcendentals=0
        ),
    )(*operands)


def solution(mesh):
    in_specs = (P(("row", "col"), None), P(), P())
    out_specs = P(None, "row", "col")
    return jax.shard_map(
        on_device, mesh=mesh, in_specs=in_specs, out_specs=out_specs, check_vma=False
    )
```

```python
import functools
import math

import jax
import jax.numpy as jnp
from jax import lax
from jax.experimental import pallas as pl
from jax.experimental.pallas import tpu as pltpu
from jax.sharding import PartitionSpec as P

NW = 3
GSR = 128
WINDOW = 256
OWN = 1280
LENT = 1152
EARLY = 12
MESH = pl.DeviceIdType.MESH


def kernel(nz, ny, pairs, elements, gaps_in, freqs_in, out, gaps, turned_gaps, weights, freqs,
           packed_a, packed_b, parts_a, parts_b, win, own, lent, got, wbuf, lhs,
           sum_own, sum_got, out_win, out_own, out_got, in_sem, pack_sem, part_recv, part_send,
           nrecv, nsend, zrecv, zsend, xrecv, xsend, wrecv, wsend, osem):
    row, col = lax.axis_index("row"), lax.axis_index("col")
    hi, z = row // nz, lax.rem(row, nz)
    ncol = ny * 4
    plane = 2 * ncol
    seat = hi * ncol + col
    y = col // 4
    in_y = lax.rem(col, 4)
    lo, core = in_y // 2, lax.rem(in_y, 2)
    up = (hi * nz + lax.rem(z + 1, nz), col)
    down = (hi * nz + lax.rem(z + nz - 1, nz), col)
    other_lo = y * 4 + (1 - lo) * 2 + core
    side = [(z, other_lo), (nz + z, other_lo)]
    in_column = [(row, lax.rem(y + k, ny) * 4 + in_y) for k in (1, 3, 2)]
    twin_lo = (row, other_lo)
    twin_core = (row, y * 4 + lo * 2 + (1 - core))
    half = nz // 2

    def seated(h, k):
        c = lax.rem(col + k, ncol)
        return h, c // 4, lax.rem(c, 4) // 2, lax.rem(c, 2)

    def device_at(h, y, lo, core):
        return h * nz + z, y * 4 + lo * 2 + core

    barrier = pltpu.get_barrier_semaphore()
    for device in (up, down):
        pl.semaphore_signal(barrier, inc=1, device_id=device, device_id_type=MESH)

    def for_others(do):
        pl.loop(1, ncol)(lambda k: do(seated(hi, k)))
        pl.loop(0, ncol)(lambda k: do(seated(1 - hi, k)))

    for_others(lambda to: pl.semaphore_signal(barrier, inc=1, device_id=device_at(*to), device_id_type=MESH))

    packing = []
    for h in range(2):
        for to in range(2):
            packing.append(pltpu.make_async_copy(
                elements.at[:, 1 - to, :, :, pl.ds(WINDOW + OWN + h * LENT, LENT)],
                packed_a.at[h, :, to, :, :, pl.ds(WINDOW, LENT)], pack_sem.at[2 * h + to],
            ))
        packing.append(pltpu.make_async_copy(
            elements.at[:, :, :, :, pl.ds(0, WINDOW)],
            packed_a.at[h, :, :, :, :, pl.ds(0, WINDOW)], pack_sem.at[4 + h],
        ))
    for h in range(2):
        packing.append(pltpu.make_async_copy(
            elements.at[:, :, :, :, pl.ds(WINDOW, OWN)], packed_b.at[h], pack_sem.at[6 + h],
        ))
    for copy in packing:
        copy.start()
    loads = [
        pltpu.make_async_copy(gaps_in, gaps, in_sem.at[0]),
        pltpu.make_async_copy(freqs_in, freqs, in_sem.at[1]),
    ]
    for load in loads:
        load.start()

    for copy in packing[:6]:
        copy.wait()
    pl.semaphore_wait(barrier, plane + 1)

    def remote(src, dst, send, recv, device):
        return pltpu.make_async_remote_copy(
            src_ref=src, dst_ref=dst, send_sem=send, recv_sem=recv, device_id=device, device_id_type=MESH
        )

    def wait(ref, sem):
        pltpu.make_async_copy(ref, ref, sem).wait()

    def exchange(n):
        packed, parts = ((packed_a, parts_a), (packed_b, parts_b))[n]

        for_others(lambda to: remote(
            packed.at[to], parts.at[seat], part_send.at[n], part_recv.at[n, hi], device_at(*to)
        ).start())
        parts[seat] = packed[hi, y, lo, core]

    def exchanged(n, same):
        parts = (parts_a, parts_b)[n]
        wait(parts.at[pl.ds(0, ncol - 1 if same else ncol)], part_recv.at[n, hi if same else 1 - hi])

    exchange(0)

    for load in loads:
        load.wait()
    for k in range(4):
        turned_gaps[k] = pltpu.roll(gaps[...], k * 32, 1)
    quarter = lax.broadcasted_iota(jnp.int32, (1, GSR), 1) // 32

    @pl.loop(0, pairs // GSR)
    def _(b):
        line = jnp.zeros((1, GSR), jnp.float32)
        for q in range(4):
            plane_at = lax.rem(z + (b if q < 2 else nz - 1 - b), nz)
            shift = lax.rem(q + 4 - lax.rem(plane_at, 4), 4)
            piece = turned_gaps[shift, pl.ds(q % 2 * 4 + plane_at // 4, 1), :]
            line = jnp.where(quarter == q, piece, line)
        for w in range(NW):
            weights[w, pl.ds(b, 1), :] = (
                -4.0 * line / ((line * line + freqs[w] * freqs[w]) * math.sqrt(pairs))
            )

    bufs = (lent, own)

    def begin(buf, h, parts, start):
        width = buf.shape[-1]
        part = parts[pl.ds(pl.multiple_of(h * ncol, ncol), ncol), :, start:start + width]
        buf[0, h] = part.reshape(2 * ncol, width)

    def place(way, s):
        return 0 if s == 0 else nz - 1 if s == half else 2 * s - 1 + way

    def push(first, count):
        late = int(first > EARLY)
        for n in range(2):
            remote(
                lent.at[pl.ds(first, count)], got.at[hi, pl.ds(first, count)],
                xsend.at[n], xrecv.at[hi, late], side[n],
            ).start()

    def arrived(n, h, way, s):
        wait(bufs[n].at[place(way, s), h], zrecv.at[way, n, h, s - 1])

    def tick(n, s, lanes=(0, 1)):
        for h in lanes:
            for way, device in ((0, up), (1, down)):
                if s > 0:
                    arrived(n, h, way, s)
                if s == half - 1 and way != h:
                    continue
                remote(
                    bufs[n].at[place(way, s), h], bufs[n].at[place(way, s + 1), h],
                    zsend.at[way, n, h], zrecv.at[way, n, h, s], device,
                ).start()

    def last(n):
        for h in range(2):
            arrived(n, h, h, half)

    def window_arrived(way, s):
        slab = win.at[place(way, s)]
        wait(slab.at[way] if s == half else slab, nrecv.at[way, s - 1])

    def window_tick(s):
        for way, device in ((0, up), (1, down)):
            if s > 0:
                window_arrived(way, s)
            src, dst = win.at[place(way, s)], win.at[place(way, s + 1)]
            if s == half - 1:
                src, dst = src.at[way], dst.at[way]
            remote(src, dst, nsend.at[way], nrecv.at[way, s], device).start()

    window_col = row // 2
    in_w = lax.rem(window_col, 4)
    same_core = core == lax.rem(in_w, 2)
    same_line = jnp.logical_and(same_core, lo == in_w // 2)
    is_source = jnp.logical_and(same_line, y == window_col // 4)

    def window_y():
        @pl.when(is_source)
        def _():
            for b in range(2):
                @pl.when(lax.rem(row, 2) == b)
                def _():
                    wbuf[...] = win[:, :, :, b * GSR:(b + 1) * GSR]
            for k, device in enumerate(in_column):
                remote(wbuf, wbuf, wsend.at[k], wrecv.at[0], device).start()

    def window_x():
        @pl.when(same_line)
        def _():
            @pl.when(jnp.logical_not(is_source))
            def _():
                wait(wbuf, wrecv.at[0])
            remote(wbuf, wbuf, wsend.at[ny - 1], wrecv.at[1], twin_lo).start()

    def window_core():
        @pl.when(same_core)
        def _():
            @pl.when(jnp.logical_not(same_line))
            def _():
                wait(wbuf, wrecv.at[1])
            remote(wbuf, wbuf, wsend.at[ny], wrecv.at[2], twin_core).start()

    def window_done():
        @pl.when(jnp.logical_not(same_core))
        def _():
            wait(wbuf, wrecv.at[2])

        @pl.loop(0, pairs // GSR)
        def _(b):
            at = pl.multiple_of(b * GSR, GSR)
            block = wbuf[pl.ds(b * 2, 2)].reshape(GSR, GSR)
            turned = block.astype(jnp.float32).T
            for w in range(NW):
                lhs[w * GSR:(w + 1) * GSR, pl.ds(at, GSR)] = (
                    turned * weights[w, pl.ds(b, 1), :]
                ).astype(jnp.bfloat16)

    early = EARLY * 4 * ncol

    def product(panel, low, high):
        return jnp.dot(
            lhs[:, low:high], panel.reshape(high - low, panel.shape[-1]), preferred_element_type=jnp.float32
        )

    def finish(chi, to, at, sem):
        to[...] = chi.astype(jnp.bfloat16).reshape(to.shape)
        write(to, at, sem).start()

    def write(to, at, sem):
        return pltpu.make_async_copy(to, out.at[:, :, pl.ds(at, to.shape[-1])], osem.at[sem])

    def lent_at(h):
        return pl.multiple_of(WINDOW + OWN + h * LENT, 128)

    for same, h in ((True, hi), (False, 1 - hi)):
        exchanged(0, same)
        begin(lent, h, parts_a, WINDOW)
        tick(0, 0, (h,))
    for h in range(2):
        begin(win, h, parts_a, 0)
    window_tick(0)
    push(0, 1)
    for copy in packing[6:]:
        copy.wait()
    exchange(1)
    window_tick(1)
    for t in range(1, half + 1):
        if t < half // 2:
            window_tick(2 * t)
        if t == half // 2:
            for way in range(2):
                window_arrived(way, half)
            window_y()
        if t < half:
            tick(0, t)
            push(place(0, t), 2)
        else:
            last(0)
            push(nz - 1, 1)
        if t < half // 2:
            window_tick(2 * t + 1)
        if t == half // 2 + 1:
            window_x()
        if t == half // 2 + 3:
            window_done()
        if t == 1:
            for same, h in ((True, hi), (False, 1 - hi)):
                exchanged(1, same)
                begin(own, h, parts_b, 0)
                tick(1, 0, (h,))
        else:
            tick(1, t - 1)
        if t == half // 2 + 2:
            window_core()
        if t == half // 2 + 3:
            finish(product(win[...], 0, pairs), out_win, 0, 0)
            sum_own[...] = product(own[:EARLY], 0, early)

    @pl.loop(0, 2)
    def _(h):
        wait(got.at[h, pl.ds(0, EARLY + 1)], xrecv.at[h, 0])
        sum_got[h] = product(got[h, :EARLY], 0, early)

    last(1)
    finish(sum_own[...] + product(own[EARLY:], early, pairs), out_own, WINDOW, 1)

    @pl.loop(0, 2)
    def _(h):
        wait(got.at[h, pl.ds(EARLY + 1, nz - EARLY - 1)], xrecv.at[h, 1])
        finish(sum_got[h] + product(got[h, EARLY:], early, pairs), out_got.at[h], lent_at(h), 2 + h)

    for way in range(2):
        wait(win.at[pl.ds(0, nz - 1), 0], nsend.at[way])
        for n in range(2):
            for h in range(2):
                wait(bufs[n].at[pl.ds(0, half if way == h else half - 1), h], zsend.at[way, n, h])
    for n in range(2):
        wait(lent, xsend.at[n])
    for n, parts in enumerate((parts_a, parts_b)):
        wait(parts.at[pl.ds(0, plane - 1)], part_send.at[n])

    @pl.when(is_source)
    def _():
        for k in range(ny - 1):
            wait(wbuf, wsend.at[k])

    @pl.when(same_line)
    def _():
        wait(wbuf, wsend.at[ny - 1])

    @pl.when(same_core)
    def _():
        wait(wbuf, wsend.at[ny])

    write(out_win, 0, 0).wait()
    write(out_own, WINDOW, 1).wait()
    for h in range(2):
        write(out_got.at[h], lent_at(h), 2 + h).wait()


def on_device(pair_elements, energy_gaps, frequencies):
    rows, cols = lax.axis_size("row"), lax.axis_size("col")
    local, full = pair_elements.shape
    pairs = local * rows * cols
    block = full // cols
    nz, ny = rows // 2, cols // 4
    depth = local * cols
    plane = 2 * cols
    dma = pltpu.SemaphoreType.DMA

    def panels(width):
        return pltpu.VMEM((nz, 2, depth, width), jnp.bfloat16)

    def results(width):
        return pltpu.VMEM((NW, GSR, width), jnp.bfloat16)

    operands = [
        pltpu.with_memory_space_constraint(operand, pltpu.HBM)
        for operand in (
            pair_elements.reshape(local, ny, 2, 2, block).transpose(1, 2, 3, 0, 4),
            energy_gaps.reshape(pairs // GSR, GSR),
            frequencies,
        )
    ]
    return pl.pallas_call(
        functools.partial(kernel, nz, ny, pairs),
        out_shape=jax.ShapeDtypeStruct((NW, GSR, block), jnp.bfloat16),
        in_specs=[pl.BlockSpec(memory_space=pl.ANY)] * 3,
        out_specs=pl.BlockSpec(memory_space=pl.ANY),
        scratch_shapes=[
            pltpu.VMEM((pairs // GSR, GSR), jnp.float32),
            pltpu.VMEM((4, pairs // GSR, GSR), jnp.float32),
            pltpu.VMEM((NW, pairs // GSR, GSR), jnp.float32),
            pltpu.SMEM((NW,), jnp.float32),
            pltpu.VMEM((2, ny, 2, 2, local, WINDOW + LENT), jnp.bfloat16),
            pltpu.VMEM((2, ny, 2, 2, local, OWN), jnp.bfloat16),
            pltpu.VMEM((plane, local, WINDOW + LENT), jnp.bfloat16),
            pltpu.VMEM((plane, local, OWN), jnp.bfloat16),
            panels(WINDOW),
            panels(OWN),
            panels(LENT),
            pltpu.VMEM((2, nz, 2, depth, LENT), jnp.bfloat16),
            panels(GSR),
            pltpu.VMEM((NW * GSR, pairs), jnp.bfloat16),
            pltpu.VMEM((NW * GSR, OWN), jnp.float32),
            pltpu.VMEM((2, NW * GSR, LENT), jnp.float32),
            results(WINDOW),
            results(OWN),
            pltpu.VMEM((2, NW, GSR, LENT), jnp.bfloat16),
            dma((2,)),
            dma((8,)),
            dma((2, 2)),
            dma((2,)),
            dma((2, nz // 2)),
            dma((2,)),
            dma((2, 2, 2, nz // 2)),
            dma((2, 2, 2)),
            dma((2, 2)),
            dma((2,)),
            dma((3,)),
            dma((ny + 1,)),
            dma((4,)),
        ],
        compiler_params=pltpu.CompilerParams(
            collective_id=0, has_side_effects=True, vmem_limit_bytes=36 * 1024 * 1024
        ),
        cost_estimate=pl.CostEstimate(
            flops=2 * NW * GSR * pairs * block, bytes_accessed=2 * NW * GSR * block, transcendentals=0
        ),
    )(*operands)


def solution(mesh):
    in_specs = (P(("row", "col"), None), P(), P())
    out_specs = P(None, "row", "col")
    return jax.shard_map(
        on_device, mesh=mesh, in_specs=in_specs, out_specs=out_specs, check_vma=False
    )
```

```python
import functools
import math

import jax
import jax.numpy as jnp
from jax import lax
from jax.experimental import pallas as pl
from jax.experimental.pallas import tpu as pltpu
from jax.sharding import PartitionSpec as P

NW = 3
GSR = 128
WINDOW = 256
OWN = 1536
LENT = 1024
EARLY = 12
MESH = pl.DeviceIdType.MESH


def kernel(nz, ny, pairs, elements, gaps_in, freqs_in, out, gaps, turned_gaps, weights, freqs,
           packed_a, packed_b, parts_a, parts_b, win, own, lent, got, wbuf, lhs,
           sum_own, sum_got, out_win, out_own, out_got, in_sem, pack_sem, part_recv, part_send,
           nrecv, nsend, zrecv, zsend, xrecv, xsend, wrecv, wsend, osem):
    row, col = lax.axis_index("row"), lax.axis_index("col")
    hi, z = row // nz, lax.rem(row, nz)
    ncol = ny * 4
    plane = 2 * ncol
    seat = hi * ncol + col
    y = col // 4
    in_y = lax.rem(col, 4)
    lo, core = in_y // 2, lax.rem(in_y, 2)
    up = (hi * nz + lax.rem(z + 1, nz), col)
    down = (hi * nz + lax.rem(z + nz - 1, nz), col)
    other_lo = y * 4 + (1 - lo) * 2 + core
    side = [(z, other_lo), (nz + z, other_lo)]
    in_column = [(row, lax.rem(y + k, ny) * 4 + in_y) for k in (1, 3, 2)]
    twin_lo = (row, other_lo)
    twin_core = (row, y * 4 + lo * 2 + (1 - core))
    half = nz // 2

    def seated(h, k):
        c = lax.rem(col + k, ncol)
        return h, c // 4, lax.rem(c, 4) // 2, lax.rem(c, 2)

    def device_at(h, y, lo, core):
        return h * nz + z, y * 4 + lo * 2 + core

    barrier = pltpu.get_barrier_semaphore()
    for device in (up, down):
        pl.semaphore_signal(barrier, inc=1, device_id=device, device_id_type=MESH)

    def for_others(do):
        pl.loop(1, ncol)(lambda k: do(seated(hi, k)))
        pl.loop(0, ncol)(lambda k: do(seated(1 - hi, k)))

    for_others(lambda to: pl.semaphore_signal(barrier, inc=1, device_id=device_at(*to), device_id_type=MESH))

    packing = []
    for h in range(2):
        for to in range(2):
            packing.append(pltpu.make_async_copy(
                elements.at[:, 1 - to, :, :, pl.ds(WINDOW + OWN + h * LENT, LENT)],
                packed_a.at[h, :, to, :, :, pl.ds(WINDOW, LENT)], pack_sem.at[2 * h + to],
            ))
        packing.append(pltpu.make_async_copy(
            elements.at[:, :, :, :, pl.ds(0, WINDOW)],
            packed_a.at[h, :, :, :, :, pl.ds(0, WINDOW)], pack_sem.at[4 + h],
        ))
    for h in range(2):
        packing.append(pltpu.make_async_copy(
            elements.at[:, :, :, :, pl.ds(WINDOW, OWN)], packed_b.at[h], pack_sem.at[6 + h],
        ))
    for copy in packing:
        copy.start()
    loads = [
        pltpu.make_async_copy(gaps_in, gaps, in_sem.at[0]),
        pltpu.make_async_copy(freqs_in, freqs, in_sem.at[1]),
    ]
    for load in loads:
        load.start()

    for copy in packing[:6]:
        copy.wait()
    pl.semaphore_wait(barrier, plane + 1)

    def remote(src, dst, send, recv, device):
        return pltpu.make_async_remote_copy(
            src_ref=src, dst_ref=dst, send_sem=send, recv_sem=recv, device_id=device, device_id_type=MESH
        )

    def wait(ref, sem):
        pltpu.make_async_copy(ref, ref, sem).wait()

    def exchange(n):
        packed, parts = ((packed_a, parts_a), (packed_b, parts_b))[n]

        for_others(lambda to: remote(
            packed.at[to], parts.at[seat], part_send.at[n], part_recv.at[n, hi], device_at(*to)
        ).start())
        parts[seat] = packed[hi, y, lo, core]

    def exchanged(n, same):
        parts = (parts_a, parts_b)[n]
        wait(parts.at[pl.ds(0, ncol - 1 if same else ncol)], part_recv.at[n, hi if same else 1 - hi])

    exchange(0)

    for load in loads:
        load.wait()
    for k in range(4):
        turned_gaps[k] = pltpu.roll(gaps[...], k * 32, 1)
    quarter = lax.broadcasted_iota(jnp.int32, (1, GSR), 1) // 32

    @pl.loop(0, pairs // GSR)
    def _(b):
        line = jnp.zeros((1, GSR), jnp.float32)
        for q in range(4):
            plane_at = lax.rem(z + (b if q < 2 else nz - 1 - b), nz)
            shift = lax.rem(q + 4 - lax.rem(plane_at, 4), 4)
            piece = turned_gaps[shift, pl.ds(q % 2 * 4 + plane_at // 4, 1), :]
            line = jnp.where(quarter == q, piece, line)
        for w in range(NW):
            weights[w, pl.ds(b, 1), :] = (
                -4.0 * line / ((line * line + freqs[w] * freqs[w]) * math.sqrt(pairs))
            )

    bufs = (lent, own)

    def begin(buf, h, parts, start):
        width = buf.shape[-1]
        part = parts[pl.ds(pl.multiple_of(h * ncol, ncol), ncol), :, start:start + width]
        buf[0, h] = part.reshape(2 * ncol, width)

    def place(way, s):
        return 0 if s == 0 else nz - 1 if s == half else 2 * s - 1 + way

    def push(first, count):
        late = int(first > EARLY)
        for n in range(2):
            remote(
                lent.at[pl.ds(first, count)], got.at[hi, pl.ds(first, count)],
                xsend.at[n], xrecv.at[hi, late], side[n],
            ).start()

    def arrived(n, h, way, s):
        wait(bufs[n].at[place(way, s), h], zrecv.at[way, n, h, s - 1])

    def tick(n, s, lanes=(0, 1)):
        for h in lanes:
            for way, device in ((0, up), (1, down)):
                if s > 0:
                    arrived(n, h, way, s)
                if s == half - 1 and way != h:
                    continue
                remote(
                    bufs[n].at[place(way, s), h], bufs[n].at[place(way, s + 1), h],
                    zsend.at[way, n, h], zrecv.at[way, n, h, s], device,
                ).start()

    def last(n):
        for h in range(2):
            arrived(n, h, h, half)

    def window_arrived(way, s):
        slab = win.at[place(way, s)]
        wait(slab.at[way] if s == half else slab, nrecv.at[way, s - 1])

    def window_tick(s):
        for way, device in ((0, up), (1, down)):
            if s > 0:
                window_arrived(way, s)
            src, dst = win.at[place(way, s)], win.at[place(way, s + 1)]
            if s == half - 1:
                src, dst = src.at[way], dst.at[way]
            remote(src, dst, nsend.at[way], nrecv.at[way, s], device).start()

    window_col = row // 2
    in_w = lax.rem(window_col, 4)
    same_core = core == lax.rem(in_w, 2)
    same_line = jnp.logical_and(same_core, lo == in_w // 2)
    is_source = jnp.logical_and(same_line, y == window_col // 4)

    def window_y():
        @pl.when(is_source)
        def _():
            for b in range(2):
                @pl.when(lax.rem(row, 2) == b)
                def _():
                    wbuf[...] = win[:, :, :, b * GSR:(b + 1) * GSR]
            for k, device in enumerate(in_column):
                remote(wbuf, wbuf, wsend.at[k], wrecv.at[0], device).start()

    def window_x():
        @pl.when(same_line)
        def _():
            @pl.when(jnp.logical_not(is_source))
            def _():
                wait(wbuf, wrecv.at[0])
            remote(wbuf, wbuf, wsend.at[ny - 1], wrecv.at[1], twin_lo).start()

    def window_core():
        @pl.when(same_core)
        def _():
            @pl.when(jnp.logical_not(same_line))
            def _():
                wait(wbuf, wrecv.at[1])
            remote(wbuf, wbuf, wsend.at[ny], wrecv.at[2], twin_core).start()

    def window_done():
        @pl.when(jnp.logical_not(same_core))
        def _():
            wait(wbuf, wrecv.at[2])

        @pl.loop(0, pairs // GSR)
        def _(b):
            at = pl.multiple_of(b * GSR, GSR)
            block = wbuf[pl.ds(b * 2, 2)].reshape(GSR, GSR)
            turned = block.astype(jnp.float32).T
            for w in range(NW):
                lhs[w * GSR:(w + 1) * GSR, pl.ds(at, GSR)] = (
                    turned * weights[w, pl.ds(b, 1), :]
                ).astype(jnp.bfloat16)

    early = EARLY * 4 * ncol

    def product(panel, low, high):
        return jnp.dot(
            lhs[:, low:high], panel.reshape(high - low, panel.shape[-1]), preferred_element_type=jnp.float32
        )

    def finish(chi, to, at, sem):
        to[...] = chi.astype(jnp.bfloat16).reshape(to.shape)
        write(to, at, sem).start()

    def write(to, at, sem):
        return pltpu.make_async_copy(to, out.at[:, :, pl.ds(at, to.shape[-1])], osem.at[sem])

    def lent_at(h):
        return pl.multiple_of(WINDOW + OWN + h * LENT, 128)

    for same, h in ((True, hi), (False, 1 - hi)):
        exchanged(0, same)
        begin(lent, h, parts_a, WINDOW)
        tick(0, 0, (h,))
    for h in range(2):
        begin(win, h, parts_a, 0)
    window_tick(0)
    push(0, 1)
    for copy in packing[6:]:
        copy.wait()
    exchange(1)
    window_tick(1)
    for t in range(1, half + 1):
        if t < half // 2:
            window_tick(2 * t)
        if t == half // 2:
            for way in range(2):
                window_arrived(way, half)
            window_y()
        if t < half:
            tick(0, t)
            push(place(0, t), 2)
        else:
            last(0)
            push(nz - 1, 1)
        if t < half // 2:
            window_tick(2 * t + 1)
        if t == half // 2 + 1:
            window_x()
        if t == half // 2 + 3:
            window_done()
        if t == 1:
            for same, h in ((True, hi), (False, 1 - hi)):
                exchanged(1, same)
                begin(own, h, parts_b, 0)
                tick(1, 0, (h,))
        else:
            tick(1, t - 1)
        if t == half // 2 + 2:
            window_core()
        if t == half // 2 + 3:
            finish(product(win[...], 0, pairs), out_win, 0, 0)
            sum_own[...] = product(own[:EARLY], 0, early)

    @pl.loop(0, 2)
    def _(h):
        wait(got.at[h, pl.ds(0, EARLY + 1)], xrecv.at[h, 0])
        sum_got[h] = product(got[h, :EARLY], 0, early)

    last(1)
    finish(sum_own[...] + product(own[EARLY:], early, pairs), out_own, WINDOW, 1)

    @pl.loop(0, 2)
    def _(h):
        wait(got.at[h, pl.ds(EARLY + 1, nz - EARLY - 1)], xrecv.at[h, 1])
        finish(sum_got[h] + product(got[h, EARLY:], early, pairs), out_got.at[h], lent_at(h), 2 + h)

    for way in range(2):
        wait(win.at[pl.ds(0, nz - 1), 0], nsend.at[way])
        for n in range(2):
            for h in range(2):
                wait(bufs[n].at[pl.ds(0, half if way == h else half - 1), h], zsend.at[way, n, h])
    for n in range(2):
        wait(lent, xsend.at[n])
    for n, parts in enumerate((parts_a, parts_b)):
        wait(parts.at[pl.ds(0, plane - 1)], part_send.at[n])

    @pl.when(is_source)
    def _():
        for k in range(ny - 1):
            wait(wbuf, wsend.at[k])

    @pl.when(same_line)
    def _():
        wait(wbuf, wsend.at[ny - 1])

    @pl.when(same_core)
    def _():
        wait(wbuf, wsend.at[ny])

    write(out_win, 0, 0).wait()
    write(out_own, WINDOW, 1).wait()
    for h in range(2):
        write(out_got.at[h], lent_at(h), 2 + h).wait()


def on_device(pair_elements, energy_gaps, frequencies):
    rows, cols = lax.axis_size("row"), lax.axis_size("col")
    local, full = pair_elements.shape
    pairs = local * rows * cols
    block = full // cols
    nz, ny = rows // 2, cols // 4
    depth = local * cols
    plane = 2 * cols
    dma = pltpu.SemaphoreType.DMA

    def panels(width):
        return pltpu.VMEM((nz, 2, depth, width), jnp.bfloat16)

    def results(width):
        return pltpu.VMEM((NW, GSR, width), jnp.bfloat16)

    operands = [
        pltpu.with_memory_space_constraint(operand, pltpu.HBM)
        for operand in (
            pair_elements.reshape(local, ny, 2, 2, block).transpose(1, 2, 3, 0, 4),
            energy_gaps.reshape(pairs // GSR, GSR),
            frequencies,
        )
    ]
    return pl.pallas_call(
        functools.partial(kernel, nz, ny, pairs),
        out_shape=jax.ShapeDtypeStruct((NW, GSR, block), jnp.bfloat16),
        in_specs=[pl.BlockSpec(memory_space=pl.ANY)] * 3,
        out_specs=pl.BlockSpec(memory_space=pl.ANY),
        scratch_shapes=[
            pltpu.VMEM((pairs // GSR, GSR), jnp.float32),
            pltpu.VMEM((4, pairs // GSR, GSR), jnp.float32),
            pltpu.VMEM((NW, pairs // GSR, GSR), jnp.float32),
            pltpu.SMEM((NW,), jnp.float32),
            pltpu.VMEM((2, ny, 2, 2, local, WINDOW + LENT), jnp.bfloat16),
            pltpu.VMEM((2, ny, 2, 2, local, OWN), jnp.bfloat16),
            pltpu.VMEM((plane, local, WINDOW + LENT), jnp.bfloat16),
            pltpu.VMEM((plane, local, OWN), jnp.bfloat16),
            panels(WINDOW),
            panels(OWN),
            panels(LENT),
            pltpu.VMEM((2, nz, 2, depth, LENT), jnp.bfloat16),
            panels(GSR),
            pltpu.VMEM((NW * GSR, pairs), jnp.bfloat16),
            pltpu.VMEM((NW * GSR, OWN), jnp.float32),
            pltpu.VMEM((2, NW * GSR, LENT), jnp.float32),
            results(WINDOW),
            results(OWN),
            pltpu.VMEM((2, NW, GSR, LENT), jnp.bfloat16),
            dma((2,)),
            dma((8,)),
            dma((2, 2)),
            dma((2,)),
            dma((2, nz // 2)),
            dma((2,)),
            dma((2, 2, 2, nz // 2)),
            dma((2, 2, 2)),
            dma((2, 2)),
            dma((2,)),
            dma((3,)),
            dma((ny + 1,)),
            dma((4,)),
        ],
        compiler_params=pltpu.CompilerParams(
            collective_id=0, has_side_effects=True, vmem_limit_bytes=36 * 1024 * 1024
        ),
        cost_estimate=pl.CostEstimate(
            flops=2 * NW * GSR * pairs * block, bytes_accessed=2 * NW * GSR * block, transcendentals=0
        ),
    )(*operands)


def solution(mesh):
    in_specs = (P(("row", "col"), None), P(), P())
    out_specs = P(None, "row", "col")
    return jax.shard_map(
        on_device, mesh=mesh, in_specs=in_specs, out_specs=out_specs, check_vma=False
    )
```

```python
import functools
import math

import jax
import jax.numpy as jnp
from jax import lax
from jax.experimental import pallas as pl
from jax.experimental.pallas import tpu as pltpu
from jax.sharding import PartitionSpec as P

NW = 3
GSR = 128
WINDOW = 256
OWN = 1024
LENT = 1280
EARLY = 12
MESH = pl.DeviceIdType.MESH


def kernel(nz, ny, pairs, elements, gaps_in, freqs_in, out, gaps, turned_gaps, weights, freqs,
           packed_a, packed_b, parts_a, parts_b, win, own, lent, got, wbuf, lhs,
           sum_own, sum_got, out_win, out_own, out_got, in_sem, pack_sem, part_recv, part_send,
           nrecv, nsend, zrecv, zsend, xrecv, xsend, wrecv, wsend, osem):
    row, col = lax.axis_index("row"), lax.axis_index("col")
    hi, z = row // nz, lax.rem(row, nz)
    ncol = ny * 4
    plane = 2 * ncol
    seat = hi * ncol + col
    y = col // 4
    in_y = lax.rem(col, 4)
    lo, core = in_y // 2, lax.rem(in_y, 2)
    up = (hi * nz + lax.rem(z + 1, nz), col)
    down = (hi * nz + lax.rem(z + nz - 1, nz), col)
    other_lo = y * 4 + (1 - lo) * 2 + core
    side = [(z, other_lo), (nz + z, other_lo)]
    in_column = [(row, lax.rem(y + k, ny) * 4 + in_y) for k in (1, 3, 2)]
    twin_lo = (row, other_lo)
    twin_core = (row, y * 4 + lo * 2 + (1 - core))
    half = nz // 2

    def seated(h, k):
        c = lax.rem(col + k, ncol)
        return h, c // 4, lax.rem(c, 4) // 2, lax.rem(c, 2)

    def device_at(h, y, lo, core):
        return h * nz + z, y * 4 + lo * 2 + core

    barrier = pltpu.get_barrier_semaphore()
    for device in (up, down):
        pl.semaphore_signal(barrier, inc=1, device_id=device, device_id_type=MESH)

    def for_others(do):
        pl.loop(1, ncol)(lambda k: do(seated(hi, k)))
        pl.loop(0, ncol)(lambda k: do(seated(1 - hi, k)))

    for_others(lambda to: pl.semaphore_signal(barrier, inc=1, device_id=device_at(*to), device_id_type=MESH))

    packing = []
    for h in range(2):
        for to in range(2):
            packing.append(pltpu.make_async_copy(
                elements.at[:, 1 - to, :, :, pl.ds(WINDOW + OWN + h * LENT, LENT)],
                packed_a.at[h, :, to, :, :, pl.ds(WINDOW, LENT)], pack_sem.at[2 * h + to],
            ))
        packing.append(pltpu.make_async_copy(
            elements.at[:, :, :, :, pl.ds(0, WINDOW)],
            packed_a.at[h, :, :, :, :, pl.ds(0, WINDOW)], pack_sem.at[4 + h],
        ))
    for h in range(2):
        packing.append(pltpu.make_async_copy(
            elements.at[:, :, :, :, pl.ds(WINDOW, OWN)], packed_b.at[h], pack_sem.at[6 + h],
        ))
    for copy in packing:
        copy.start()
    loads = [
        pltpu.make_async_copy(gaps_in, gaps, in_sem.at[0]),
        pltpu.make_async_copy(freqs_in, freqs, in_sem.at[1]),
    ]
    for load in loads:
        load.start()

    for copy in packing[:6]:
        copy.wait()
    pl.semaphore_wait(barrier, plane + 1)

    def remote(src, dst, send, recv, device):
        return pltpu.make_async_remote_copy(
            src_ref=src, dst_ref=dst, send_sem=send, recv_sem=recv, device_id=device, device_id_type=MESH
        )

    def wait(ref, sem):
        pltpu.make_async_copy(ref, ref, sem).wait()

    def exchange(n):
        packed, parts = ((packed_a, parts_a), (packed_b, parts_b))[n]

        for_others(lambda to: remote(
            packed.at[to], parts.at[seat], part_send.at[n], part_recv.at[n, hi], device_at(*to)
        ).start())
        parts[seat] = packed[hi, y, lo, core]

    def exchanged(n, same):
        parts = (parts_a, parts_b)[n]
        wait(parts.at[pl.ds(0, ncol - 1 if same else ncol)], part_recv.at[n, hi if same else 1 - hi])

    exchange(0)

    for load in loads:
        load.wait()
    for k in range(4):
        turned_gaps[k] = pltpu.roll(gaps[...], k * 32, 1)
    quarter = lax.broadcasted_iota(jnp.int32, (1, GSR), 1) // 32

    @pl.loop(0, pairs // GSR)
    def _(b):
        line = jnp.zeros((1, GSR), jnp.float32)
        for q in range(4):
            plane_at = lax.rem(z + (b if q < 2 else nz - 1 - b), nz)
            shift = lax.rem(q + 4 - lax.rem(plane_at, 4), 4)
            piece = turned_gaps[shift, pl.ds(q % 2 * 4 + plane_at // 4, 1), :]
            line = jnp.where(quarter == q, piece, line)
        for w in range(NW):
            weights[w, pl.ds(b, 1), :] = (
                -4.0 * line / ((line * line + freqs[w] * freqs[w]) * math.sqrt(pairs))
            )

    bufs = (lent, own)

    def begin(buf, h, parts, start):
        width = buf.shape[-1]
        part = parts[pl.ds(pl.multiple_of(h * ncol, ncol), ncol), :, start:start + width]
        buf[0, h] = part.reshape(2 * ncol, width)

    def place(way, s):
        return 0 if s == 0 else nz - 1 if s == half else 2 * s - 1 + way

    def push(first, count):
        late = int(first > EARLY)
        for n in range(2):
            remote(
                lent.at[pl.ds(first, count)], got.at[hi, pl.ds(first, count)],
                xsend.at[n], xrecv.at[hi, late], side[n],
            ).start()

    def arrived(n, h, way, s):
        wait(bufs[n].at[place(way, s), h], zrecv.at[way, n, h, s - 1])

    def tick(n, s, lanes=(0, 1)):
        for h in lanes:
            for way, device in ((0, up), (1, down)):
                if s > 0:
                    arrived(n, h, way, s)
                if s == half - 1 and way != h:
                    continue
                remote(
                    bufs[n].at[place(way, s), h], bufs[n].at[place(way, s + 1), h],
                    zsend.at[way, n, h], zrecv.at[way, n, h, s], device,
                ).start()

    def last(n):
        for h in range(2):
            arrived(n, h, h, half)

    def window_arrived(way, s):
        slab = win.at[place(way, s)]
        wait(slab.at[way] if s == half else slab, nrecv.at[way, s - 1])

    def window_tick(s):
        for way, device in ((0, up), (1, down)):
            if s > 0:
                window_arrived(way, s)
            src, dst = win.at[place(way, s)], win.at[place(way, s + 1)]
            if s == half - 1:
                src, dst = src.at[way], dst.at[way]
            remote(src, dst, nsend.at[way], nrecv.at[way, s], device).start()

    window_col = row // 2
    in_w = lax.rem(window_col, 4)
    same_core = core == lax.rem(in_w, 2)
    same_line = jnp.logical_and(same_core, lo == in_w // 2)
    is_source = jnp.logical_and(same_line, y == window_col // 4)

    def window_y():
        @pl.when(is_source)
        def _():
            for b in range(2):
                @pl.when(lax.rem(row, 2) == b)
                def _():
                    wbuf[...] = win[:, :, :, b * GSR:(b + 1) * GSR]
            for k, device in enumerate(in_column):
                remote(wbuf, wbuf, wsend.at[k], wrecv.at[0], device).start()

    def window_x():
        @pl.when(same_line)
        def _():
            @pl.when(jnp.logical_not(is_source))
            def _():
                wait(wbuf, wrecv.at[0])
            remote(wbuf, wbuf, wsend.at[ny - 1], wrecv.at[1], twin_lo).start()

    def window_core():
        @pl.when(same_core)
        def _():
            @pl.when(jnp.logical_not(same_line))
            def _():
                wait(wbuf, wrecv.at[1])
            remote(wbuf, wbuf, wsend.at[ny], wrecv.at[2], twin_core).start()

    def window_done():
        @pl.when(jnp.logical_not(same_core))
        def _():
            wait(wbuf, wrecv.at[2])

        @pl.loop(0, pairs // GSR)
        def _(b):
            at = pl.multiple_of(b * GSR, GSR)
            block = wbuf[pl.ds(b * 2, 2)].reshape(GSR, GSR)
            turned = block.astype(jnp.float32).T
            for w in range(NW):
                lhs[w * GSR:(w + 1) * GSR, pl.ds(at, GSR)] = (
                    turned * weights[w, pl.ds(b, 1), :]
                ).astype(jnp.bfloat16)

    early = EARLY * 4 * ncol

    def product(panel, low, high):
        return jnp.dot(
            lhs[:, low:high], panel.reshape(high - low, panel.shape[-1]), preferred_element_type=jnp.float32
        )

    def finish(chi, to, at, sem):
        to[...] = chi.astype(jnp.bfloat16).reshape(to.shape)
        write(to, at, sem).start()

    def write(to, at, sem):
        return pltpu.make_async_copy(to, out.at[:, :, pl.ds(at, to.shape[-1])], osem.at[sem])

    def lent_at(h):
        return pl.multiple_of(WINDOW + OWN + h * LENT, 128)

    for same, h in ((True, hi), (False, 1 - hi)):
        exchanged(0, same)
        begin(lent, h, parts_a, WINDOW)
        tick(0, 0, (h,))
    for h in range(2):
        begin(win, h, parts_a, 0)
    window_tick(0)
    push(0, 1)
    for copy in packing[6:]:
        copy.wait()
    exchange(1)
    window_tick(1)
    for t in range(1, half + 1):
        if t < half // 2:
            window_tick(2 * t)
        if t == half // 2:
            for way in range(2):
                window_arrived(way, half)
            window_y()
        if t < half:
            tick(0, t)
            push(place(0, t), 2)
        else:
            last(0)
            push(nz - 1, 1)
        if t < half // 2:
            window_tick(2 * t + 1)
        if t == half // 2 + 1:
            window_x()
        if t == half // 2 + 3:
            window_done()
        if t == 1:
            for same, h in ((True, hi), (False, 1 - hi)):
                exchanged(1, same)
                begin(own, h, parts_b, 0)
                tick(1, 0, (h,))
        else:
            tick(1, t - 1)
        if t == half // 2 + 2:
            window_core()
        if t == half // 2 + 3:
            finish(product(win[...], 0, pairs), out_win, 0, 0)
            sum_own[...] = product(own[:EARLY], 0, early)

    @pl.loop(0, 2)
    def _(h):
        wait(got.at[h, pl.ds(0, EARLY + 1)], xrecv.at[h, 0])
        sum_got[h] = product(got[h, :EARLY], 0, early)

    last(1)
    finish(sum_own[...] + product(own[EARLY:], early, pairs), out_own, WINDOW, 1)

    @pl.loop(0, 2)
    def _(h):
        wait(got.at[h, pl.ds(EARLY + 1, nz - EARLY - 1)], xrecv.at[h, 1])
        finish(sum_got[h] + product(got[h, EARLY:], early, pairs), out_got.at[h], lent_at(h), 2 + h)

    for way in range(2):
        wait(win.at[pl.ds(0, nz - 1), 0], nsend.at[way])
        for n in range(2):
            for h in range(2):
                wait(bufs[n].at[pl.ds(0, half if way == h else half - 1), h], zsend.at[way, n, h])
    for n in range(2):
        wait(lent, xsend.at[n])
    for n, parts in enumerate((parts_a, parts_b)):
        wait(parts.at[pl.ds(0, plane - 1)], part_send.at[n])

    @pl.when(is_source)
    def _():
        for k in range(ny - 1):
            wait(wbuf, wsend.at[k])

    @pl.when(same_line)
    def _():
        wait(wbuf, wsend.at[ny - 1])

    @pl.when(same_core)
    def _():
        wait(wbuf, wsend.at[ny])

    write(out_win, 0, 0).wait()
    write(out_own, WINDOW, 1).wait()
    for h in range(2):
        write(out_got.at[h], lent_at(h), 2 + h).wait()


def on_device(pair_elements, energy_gaps, frequencies):
    rows, cols = lax.axis_size("row"), lax.axis_size("col")
    local, full = pair_elements.shape
    pairs = local * rows * cols
    block = full // cols
    nz, ny = rows // 2, cols // 4
    depth = local * cols
    plane = 2 * cols
    dma = pltpu.SemaphoreType.DMA

    def panels(width):
        return pltpu.VMEM((nz, 2, depth, width), jnp.bfloat16)

    def results(width):
        return pltpu.VMEM((NW, GSR, width), jnp.bfloat16)

    operands = [
        pltpu.with_memory_space_constraint(operand, pltpu.HBM)
        for operand in (
            pair_elements.reshape(local, ny, 2, 2, block).transpose(1, 2, 3, 0, 4),
            energy_gaps.reshape(pairs // GSR, GSR),
            frequencies,
        )
    ]
    return pl.pallas_call(
        functools.partial(kernel, nz, ny, pairs),
        out_shape=jax.ShapeDtypeStruct((NW, GSR, block), jnp.bfloat16),
        in_specs=[pl.BlockSpec(memory_space=pl.ANY)] * 3,
        out_specs=pl.BlockSpec(memory_space=pl.ANY),
        scratch_shapes=[
            pltpu.VMEM((pairs // GSR, GSR), jnp.float32),
            pltpu.VMEM((4, pairs // GSR, GSR), jnp.float32),
            pltpu.VMEM((NW, pairs // GSR, GSR), jnp.float32),
            pltpu.SMEM((NW,), jnp.float32),
            pltpu.VMEM((2, ny, 2, 2, local, WINDOW + LENT), jnp.bfloat16),
            pltpu.VMEM((2, ny, 2, 2, local, OWN), jnp.bfloat16),
            pltpu.VMEM((plane, local, WINDOW + LENT), jnp.bfloat16),
            pltpu.VMEM((plane, local, OWN), jnp.bfloat16),
            panels(WINDOW),
            panels(OWN),
            panels(LENT),
            pltpu.VMEM((2, nz, 2, depth, LENT), jnp.bfloat16),
            panels(GSR),
            pltpu.VMEM((NW * GSR, pairs), jnp.bfloat16),
            pltpu.VMEM((NW * GSR, OWN), jnp.float32),
            pltpu.VMEM((2, NW * GSR, LENT), jnp.float32),
            results(WINDOW),
            results(OWN),
            pltpu.VMEM((2, NW, GSR, LENT), jnp.bfloat16),
            dma((2,)),
            dma((8,)),
            dma((2, 2)),
            dma((2,)),
            dma((2, nz // 2)),
            dma((2,)),
            dma((2, 2, 2, nz // 2)),
            dma((2, 2, 2)),
            dma((2, 2)),
            dma((2,)),
            dma((3,)),
            dma((ny + 1,)),
            dma((4,)),
        ],
        compiler_params=pltpu.CompilerParams(
            collective_id=0, has_side_effects=True, vmem_limit_bytes=36 * 1024 * 1024
        ),
        cost_estimate=pl.CostEstimate(
            flops=2 * NW * GSR * pairs * block, bytes_accessed=2 * NW * GSR * block, transcendentals=0
        ),
    )(*operands)


def solution(mesh):
    in_specs = (P(("row", "col"), None), P(), P())
    out_specs = P(None, "row", "col")
    return jax.shard_map(
        on_device, mesh=mesh, in_specs=in_specs, out_specs=out_specs, check_vma=False
    )
```

```python
import functools
import math

import jax
import jax.numpy as jnp
from jax import lax
from jax.experimental import pallas as pl
from jax.experimental.pallas import tpu as pltpu
from jax.sharding import PartitionSpec as P

NW = 3
GSR = 128
WINDOW = 256
LENT = 1152
OWN = 1536
EARLY = 12
MESH = pl.DeviceIdType.MESH


def kernel(nz, ny, pairs, elements, gaps_in, freqs_in, out, gaps, turned_gaps, weights, freqs,
           parts_a, parts_b, win, own, lent, got_win, got, wbuf, lhs,
           sum_own, sum_got, out_win, out_own, out_got, in_sem, part_sem, part_recv, part_send,
           nrecv, nsend, zrecv, zsend, xwrecv, xwsend, xrecv, xsend, wrecv, wsend, osem):
    row, col = lax.axis_index("row"), lax.axis_index("col")
    hi, z = row // nz, lax.rem(row, nz)
    ncol = ny * 4
    plane = 2 * ncol
    seat = hi * ncol + col
    y = col // 4
    in_y = lax.rem(col, 4)
    lo, core = in_y // 2, lax.rem(in_y, 2)
    up = (hi * nz + lax.rem(z + 1, nz), col)
    down = (hi * nz + lax.rem(z + nz - 1, nz), col)
    other_lo = y * 4 + (1 - lo) * 2 + core
    side = [(z, other_lo), (nz + z, other_lo)]
    in_column = [(row, lax.rem(y + k, ny) * 4 + in_y) for k in (1, 3, 2)]
    twin_core = (row, y * 4 + lo * 2 + (1 - core))
    half = nz // 2

    def seated(h, k):
        c = lax.rem(col + k, ncol)
        return h, c // 4, lax.rem(c, 4) // 2, lax.rem(c, 2)

    def device_at(h, y, lo, core):
        return h * nz + z, y * 4 + lo * 2 + core

    barrier = pltpu.get_barrier_semaphore()
    for device in (up, down):
        pl.semaphore_signal(barrier, inc=1, device_id=device, device_id_type=MESH)

    def for_others(do):
        pl.loop(1, ncol)(lambda k: do(seated(hi, k)))
        pl.loop(0, ncol)(lambda k: do(seated(1 - hi, k)))

    for_others(lambda to: pl.semaphore_signal(barrier, inc=1, device_id=device_at(*to), device_id_type=MESH))

    loads = [
        pltpu.make_async_copy(gaps_in, gaps, in_sem.at[0]),
        pltpu.make_async_copy(freqs_in, freqs, in_sem.at[1]),
    ]
    for load in loads:
        load.start()

    def lent_at(h, y):
        first = y // 2
        return pl.multiple_of((h + first - 2 * h * first) * LENT, 128)

    def lent_range(h, y, lo, core):
        return elements.at[y, 1 - lo, core, :, pl.ds(lent_at(h, y), LENT)]

    def own_range(h, y, lo, core):
        return elements.at[y, lo, core, :, pl.ds(2 * LENT, OWN)]

    ranges = ((lent_range, parts_a), (own_range, parts_b))
    mine = [
        pltpu.make_async_copy(source(hi, y, lo, core), parts.at[seat], part_sem.at[n])
        for n, (source, parts) in enumerate(ranges)
    ]
    for copy in mine:
        copy.start()
    pl.semaphore_wait(barrier, plane + 1)

    def remote(src, dst, send, recv, device):
        return pltpu.make_async_remote_copy(
            src_ref=src, dst_ref=dst, send_sem=send, recv_sem=recv, device_id=device, device_id_type=MESH
        )

    def wait(ref, sem):
        pltpu.make_async_copy(ref, ref, sem).wait()

    def exchange(n):
        source, parts = ranges[n]
        for_others(lambda to: remote(
            source(*to), parts.at[seat], part_send.at[n], part_recv.at[n, hi], device_at(*to)
        ).start())

    def exchanged(n, same):
        parts = ranges[n][1]
        if same:
            mine[n].wait()
        wait(parts.at[pl.ds(0, ncol - 1 if same else ncol)], part_recv.at[n, hi if same else 1 - hi])

    exchange(0)

    for load in loads:
        load.wait()
    for k in range(4):
        turned_gaps[k] = pltpu.roll(gaps[...], k * 32, 1)
    quarter = lax.broadcasted_iota(jnp.int32, (1, GSR), 1) // 32

    @pl.loop(0, pairs // GSR)
    def _(b):
        line = jnp.zeros((1, GSR), jnp.float32)
        for q in range(4):
            plane_at = lax.rem(z + (b if q < 2 else nz - 1 - b), nz)
            shift = lax.rem(q + 4 - lax.rem(plane_at, 4), 4)
            piece = turned_gaps[shift, pl.ds(q % 2 * 4 + plane_at // 4, 1), :]
            line = jnp.where(quarter == q, piece, line)
        for w in range(NW):
            weights[w, pl.ds(b, 1), :] = (
                -4.0 * line / ((line * line + freqs[w] * freqs[w]) * math.sqrt(pairs))
            )

    bufs = (lent, own)

    def begin(buf, h, parts, start):
        width = buf.shape[-1]
        part = parts[pl.ds(pl.multiple_of(h * ncol, ncol), ncol), :, start:start + width]
        buf[0, h] = part.reshape(2 * ncol, width)

    def place(way, s):
        return 0 if s == 0 else nz - 1 if s == half else 2 * s - 1 + way

    def push(first, count):
        late = int(first > EARLY)
        for n in range(2):
            remote(
                lent.at[pl.ds(first, count)], got.at[hi, pl.ds(first, count)],
                xsend.at[n], xrecv.at[hi, late], side[n],
            ).start()

    def arrived(n, h, way, s):
        wait(bufs[n].at[place(way, s), h], zrecv.at[way, n, h, s - 1])

    def tick(n, s, lanes=(0, 1)):
        for h in lanes:
            for way, device in ((0, up), (1, down)):
                if s > 0:
                    arrived(n, h, way, s)
                if s == half - 1 and way != h:
                    continue
                remote(
                    bufs[n].at[place(way, s), h], bufs[n].at[place(way, s + 1), h],
                    zsend.at[way, n, h], zrecv.at[way, n, h, s], device,
                ).start()

    def last(n):
        for h in range(2):
            arrived(n, h, h, half)

    def window_arrived(way, s):
        slab = win.at[place(way, s)]
        wait(slab.at[way] if s == half else slab, nrecv.at[way, s - 1])

    def window_tick(s):
        for way, device in ((0, up), (1, down)):
            if s > 0:
                window_arrived(way, s)
            src, dst = win.at[place(way, s)], win.at[place(way, s + 1)]
            if s == half - 1:
                src, dst = src.at[way], dst.at[way]
            remote(src, dst, nsend.at[way], nrecv.at[way, s], device).start()

    def window_push(first, count):
        for n in range(2):
            remote(
                win.at[pl.ds(first, count)], got_win.at[hi, pl.ds(first, count)],
                xwsend.at[n], xwrecv.at[hi], side[n],
            ).start()

    window_col = row // 2
    in_w = lax.rem(window_col, 4)
    same_core = core == lax.rem(in_w, 2)
    is_source = jnp.logical_and(same_core, y == window_col // 4)
    gathers = lo != in_w // 2

    def window_y():
        for h in range(2):
            wait(got_win.at[h], xwrecv.at[h])

        @pl.when(is_source)
        def _():
            for b in range(2):
                cut = slice(b * GSR, (b + 1) * GSR)
                this = lax.rem(row, 2) == b

                @pl.when(jnp.logical_and(this, gathers))
                def _():
                    wbuf[...] = win[:, :, :, cut]

                @pl.when(jnp.logical_and(this, jnp.logical_not(gathers)))
                def _():
                    wbuf[...] = got_win[hi, :, :, :, cut]
            for k, device in enumerate(in_column):
                remote(wbuf, wbuf, wsend.at[k], wrecv.at[0], device).start()

    def window_core():
        @pl.when(same_core)
        def _():
            @pl.when(jnp.logical_not(is_source))
            def _():
                wait(wbuf, wrecv.at[0])
            remote(wbuf, wbuf, wsend.at[ny - 1], wrecv.at[1], twin_core).start()

    def window_done():
        @pl.when(jnp.logical_not(same_core))
        def _():
            wait(wbuf, wrecv.at[1])

        @pl.loop(0, pairs // GSR)
        def _(b):
            at = pl.multiple_of(b * GSR, GSR)
            block = wbuf[pl.ds(b * 2, 2)].reshape(GSR, GSR)
            turned = block.astype(jnp.float32).T
            for w in range(NW):
                lhs[w * GSR:(w + 1) * GSR, pl.ds(at, GSR)] = (
                    turned * weights[w, pl.ds(b, 1), :]
                ).astype(jnp.bfloat16)

    early = EARLY * 4 * ncol

    def product(panel, low, high):
        return jnp.dot(
            lhs[:, low:high], panel.reshape(high - low, panel.shape[-1]), preferred_element_type=jnp.float32
        )

    def finish(chi, to, at, sem):
        to[...] = chi.astype(jnp.bfloat16).reshape(to.shape)
        write(to, at, sem).start()

    def write(to, at, sem):
        return pltpu.make_async_copy(to, out.at[:, :, pl.ds(at, to.shape[-1])], osem.at[sem])

    for same, h in ((True, hi), (False, 1 - hi)):
        exchanged(0, same)
        begin(lent, h, parts_a, WINDOW)
        tick(0, 0, (h,))
    for h in range(2):
        begin(win, h, parts_a, 0)
    window_tick(0)
    push(0, 1)
    exchange(1)
    window_tick(1)
    window_push(0, 3)
    for t in range(1, half + 1):
        if t < half // 2:
            window_tick(2 * t)
        if t == half // 2:
            for way in range(2):
                window_arrived(way, half)
            window_push(nz - 1, 1)
        if t == half // 2 + 1:
            window_y()
        if t < half:
            tick(0, t)
            push(place(0, t), 2)
        else:
            last(0)
            push(nz - 1, 1)
        if t < half // 2:
            window_tick(2 * t + 1)
            window_push(4 * t - 1, 4)
        if t == half // 2 + 3:
            window_done()
        if t == 1:
            for same, h in ((True, hi), (False, 1 - hi)):
                exchanged(1, same)
                begin(own, h, parts_b, 0)
                tick(1, 0, (h,))
        else:
            tick(1, t - 1)
        if t == half // 2 + 2:
            window_core()
        if t == half // 2 + 3:
            @pl.loop(0, 2)
            def _(h):
                finish(product(got_win[h], 0, pairs), out_win.at[h], lent_at(h, y), h)

            sum_own[...] = product(own[:EARLY], 0, early)

    @pl.loop(0, 2)
    def _(h):
        wait(got.at[h, pl.ds(0, EARLY + 1)], xrecv.at[h, 0])
        sum_got[h] = product(got[h, :EARLY], 0, early)

    last(1)
    finish(sum_own[...] + product(own[EARLY:], early, pairs), out_own, 2 * LENT, 2)

    @pl.loop(0, 2)
    def _(h):
        wait(got.at[h, pl.ds(EARLY + 1, nz - EARLY - 1)], xrecv.at[h, 1])
        finish(sum_got[h] + product(got[h, EARLY:], early, pairs), out_got.at[h], lent_at(h, y) + WINDOW, 3 + h)

    for way in range(2):
        wait(win.at[pl.ds(0, nz - 1), 0], nsend.at[way])
        for n in range(2):
            for h in range(2):
                wait(bufs[n].at[pl.ds(0, half if way == h else half - 1), h], zsend.at[way, n, h])
    for n in range(2):
        wait(lent, xsend.at[n])
        wait(win, xwsend.at[n])
    for n, parts in enumerate((parts_a, parts_b)):
        wait(parts.at[pl.ds(0, plane - 1)], part_send.at[n])

    @pl.when(is_source)
    def _():
        for k in range(ny - 1):
            wait(wbuf, wsend.at[k])

    @pl.when(same_core)
    def _():
        wait(wbuf, wsend.at[ny - 1])

    write(out_own, 2 * LENT, 2).wait()
    for h in range(2):
        write(out_win.at[h], lent_at(h, y), h).wait()
        write(out_got.at[h], lent_at(h, y) + WINDOW, 3 + h).wait()


def on_device(pair_elements, energy_gaps, frequencies):
    rows, cols = lax.axis_size("row"), lax.axis_size("col")
    local, full = pair_elements.shape
    pairs = local * rows * cols
    block = full // cols
    nz, ny = rows // 2, cols // 4
    depth = local * cols
    plane = 2 * cols
    dma = pltpu.SemaphoreType.DMA

    def panels(width):
        return pltpu.VMEM((nz, 2, depth, width), jnp.bfloat16)

    def results(width):
        return pltpu.VMEM((NW, GSR, width), jnp.bfloat16)

    operands = [
        pltpu.with_memory_space_constraint(operand, pltpu.HBM)
        for operand in (
            pair_elements.reshape(local, ny, 2, 2, block).transpose(1, 2, 3, 0, 4),
            energy_gaps.reshape(pairs // GSR, GSR),
            frequencies,
        )
    ]
    return pl.pallas_call(
        functools.partial(kernel, nz, ny, pairs),
        out_shape=jax.ShapeDtypeStruct((NW, GSR, block), jnp.bfloat16),
        in_specs=[pl.BlockSpec(memory_space=pl.ANY)] * 3,
        out_specs=pl.BlockSpec(memory_space=pl.ANY),
        scratch_shapes=[
            pltpu.VMEM((pairs // GSR, GSR), jnp.float32),
            pltpu.VMEM((4, pairs // GSR, GSR), jnp.float32),
            pltpu.VMEM((NW, pairs // GSR, GSR), jnp.float32),
            pltpu.SMEM((NW,), jnp.float32),
            pltpu.VMEM((plane, local, LENT), jnp.bfloat16),
            pltpu.VMEM((plane, local, OWN), jnp.bfloat16),
            panels(WINDOW),
            panels(OWN),
            panels(LENT - WINDOW),
            pltpu.VMEM((2, nz, 2, depth, WINDOW), jnp.bfloat16),
            pltpu.VMEM((2, nz, 2, depth, LENT - WINDOW), jnp.bfloat16),
            panels(GSR),
            pltpu.VMEM((NW * GSR, pairs), jnp.bfloat16),
            pltpu.VMEM((NW * GSR, OWN), jnp.float32),
            pltpu.VMEM((2, NW * GSR, LENT - WINDOW), jnp.float32),
            pltpu.VMEM((2, NW, GSR, WINDOW), jnp.bfloat16),
            results(OWN),
            pltpu.VMEM((2, NW, GSR, LENT - WINDOW), jnp.bfloat16),
            dma((2,)),
            dma((2,)),
            dma((2, 2)),
            dma((2,)),
            dma((2, nz // 2)),
            dma((2,)),
            dma((2, 2, 2, nz // 2)),
            dma((2, 2, 2)),
            dma((2,)),
            dma((2,)),
            dma((2, 2)),
            dma((2,)),
            dma((2,)),
            dma((ny,)),
            dma((5,)),
        ],
        compiler_params=pltpu.CompilerParams(
            collective_id=0, has_side_effects=True, vmem_limit_bytes=36 * 1024 * 1024
        ),
        cost_estimate=pl.CostEstimate(
            flops=2 * NW * GSR * pairs * block, bytes_accessed=2 * NW * GSR * block, transcendentals=0
        ),
    )(*operands)


def solution(mesh):
    in_specs = (P(("row", "col"), None), P(), P())
    out_specs = P(None, "row", "col")
    return jax.shard_map(
        on_device, mesh=mesh, in_specs=in_specs, out_specs=out_specs, check_vma=False
    )
```

```python
import functools
import math

import jax
import jax.numpy as jnp
from jax import lax
from jax.experimental import pallas as pl
from jax.experimental.pallas import tpu as pltpu
from jax.sharding import PartitionSpec as P

NW = 3
GSR = 128
WINDOW = 256
LENT = 1280
OWN = 640
EARLY = 12
MESH = pl.DeviceIdType.MESH


def kernel(nz, ny, pairs, elements, gaps_in, freqs_in, out, gaps, turned_gaps, weights, freqs,
           parts_a, parts_b, win, own_a, own_b, lent, got_win, got, wbuf, lhs,
           sum_own, sum_got, out_win, out_own, out_got, in_sem, part_sem, part_recv, part_send,
           nrecv, nsend, zrecv, zsend, xwrecv, xwsend, xrecv, xsend, wrecv, wsend, osem):
    row, col = lax.axis_index("row"), lax.axis_index("col")
    hi, z = row // nz, lax.rem(row, nz)
    ncol = ny * 4
    plane = 2 * ncol
    seat = hi * ncol + col
    y = col // 4
    in_y = lax.rem(col, 4)
    lo, core = in_y // 2, lax.rem(in_y, 2)
    up = (hi * nz + lax.rem(z + 1, nz), col)
    down = (hi * nz + lax.rem(z + nz - 1, nz), col)
    other_lo = y * 4 + (1 - lo) * 2 + core
    side = [(z, other_lo), (nz + z, other_lo)]
    in_column = [(row, lax.rem(y + k, ny) * 4 + in_y) for k in (1, 3, 2)]
    twin_core = (row, y * 4 + lo * 2 + (1 - core))
    half = nz // 2

    def seated(h, k):
        c = lax.rem(col + k, ncol)
        return h, c // 4, lax.rem(c, 4) // 2, lax.rem(c, 2)

    def device_at(h, y, lo, core):
        return h * nz + z, y * 4 + lo * 2 + core

    barrier = pltpu.get_barrier_semaphore()
    for device in (up, down):
        pl.semaphore_signal(barrier, inc=1, device_id=device, device_id_type=MESH)

    def for_others(do):
        pl.loop(1, ncol)(lambda k: do(seated(hi, k)))
        pl.loop(0, ncol)(lambda k: do(seated(1 - hi, k)))

    for_others(lambda to: pl.semaphore_signal(barrier, inc=1, device_id=device_at(*to), device_id_type=MESH))

    loads = [
        pltpu.make_async_copy(gaps_in, gaps, in_sem.at[0]),
        pltpu.make_async_copy(freqs_in, freqs, in_sem.at[1]),
    ]
    for load in loads:
        load.start()

    def lent_at(h, y):
        first = y // 2
        return pl.multiple_of((h + first - 2 * h * first) * LENT, 128)

    def lent_range(h, y, lo, core):
        return elements.at[y, 1 - lo, core, :, pl.ds(lent_at(h, y), LENT)]

    def own_range(h, y, lo, core):
        return elements.at[y, lo, core, :, pl.ds(2 * LENT, 2 * OWN)]

    ranges = ((lent_range, parts_a), (own_range, parts_b))
    mine = [
        pltpu.make_async_copy(source(hi, y, lo, core), parts.at[seat], part_sem.at[n])
        for n, (source, parts) in enumerate(ranges)
    ]
    for copy in mine:
        copy.start()
    pl.semaphore_wait(barrier, plane + 1)

    def remote(src, dst, send, recv, device):
        return pltpu.make_async_remote_copy(
            src_ref=src, dst_ref=dst, send_sem=send, recv_sem=recv, device_id=device, device_id_type=MESH
        )

    def wait(ref, sem):
        pltpu.make_async_copy(ref, ref, sem).wait()

    def exchange(n):
        source, parts = ranges[n]
        for_others(lambda to: remote(
            source(*to), parts.at[seat], part_send.at[n], part_recv.at[n, hi], device_at(*to)
        ).start())

    def exchanged(n, same):
        parts = ranges[n][1]
        if same:
            mine[n].wait()
        wait(parts.at[pl.ds(0, ncol - 1 if same else ncol)], part_recv.at[n, hi if same else 1 - hi])

    exchange(0)

    for load in loads:
        load.wait()
    for k in range(4):
        turned_gaps[k] = pltpu.roll(gaps[...], k * 32, 1)
    quarter = lax.broadcasted_iota(jnp.int32, (1, GSR), 1) // 32

    @pl.loop(0, pairs // GSR)
    def _(b):
        line = jnp.zeros((1, GSR), jnp.float32)
        for q in range(4):
            plane_at = lax.rem(z + (b if q < 2 else nz - 1 - b), nz)
            shift = lax.rem(q + 4 - lax.rem(plane_at, 4), 4)
            piece = turned_gaps[shift, pl.ds(q % 2 * 4 + plane_at // 4, 1), :]
            line = jnp.where(quarter == q, piece, line)
        for w in range(NW):
            weights[w, pl.ds(b, 1), :] = (
                -4.0 * line / ((line * line + freqs[w] * freqs[w]) * math.sqrt(pairs))
            )

    bufs = (lent, own_a, own_b)

    def begin(buf, h, parts, start):
        width = buf.shape[-1]
        part = parts[pl.ds(pl.multiple_of(h * ncol, ncol), ncol), :, start:start + width]
        buf[0, h] = part.reshape(2 * ncol, width)

    def place(way, s):
        return 0 if s == 0 else nz - 1 if s == half else 2 * s - 1 + way

    def push(first, count):
        late = int(first > EARLY)
        for n in range(2):
            remote(
                lent.at[pl.ds(first, count)], got.at[hi, pl.ds(first, count)],
                xsend.at[n], xrecv.at[hi, late], side[n],
            ).start()

    def arrived(n, h, way, s):
        wait(bufs[n].at[place(way, s), h], zrecv.at[way, n, h, s - 1])

    def tick(n, s, lanes=(0, 1)):
        for h in lanes:
            for way, device in ((0, up), (1, down)):
                if s > 0:
                    arrived(n, h, way, s)
                if s == half - 1 and way != h:
                    continue
                remote(
                    bufs[n].at[place(way, s), h], bufs[n].at[place(way, s + 1), h],
                    zsend.at[way, n, h], zrecv.at[way, n, h, s], device,
                ).start()

    def last(n):
        for h in range(2):
            arrived(n, h, h, half)

    def window_arrived(way, s):
        slab = win.at[place(way, s)]
        wait(slab.at[way] if s == half else slab, nrecv.at[way, s - 1])

    def window_tick(s):
        for way, device in ((0, up), (1, down)):
            if s > 0:
                window_arrived(way, s)
            src, dst = win.at[place(way, s)], win.at[place(way, s + 1)]
            if s == half - 1:
                src, dst = src.at[way], dst.at[way]
            remote(src, dst, nsend.at[way], nrecv.at[way, s], device).start()

    def window_push(first, count):
        for n in range(2):
            remote(
                win.at[pl.ds(first, count)], got_win.at[hi, pl.ds(first, count)],
                xwsend.at[n], xwrecv.at[hi], side[n],
            ).start()

    window_col = row // 2
    in_w = lax.rem(window_col, 4)
    same_core = core == lax.rem(in_w, 2)
    is_source = jnp.logical_and(same_core, y == window_col // 4)
    gathers = lo != in_w // 2

    def window_y():
        for h in range(2):
            wait(got_win.at[h], xwrecv.at[h])

        @pl.when(is_source)
        def _():
            for b in range(2):
                cut = slice(b * GSR, (b + 1) * GSR)
                this = lax.rem(row, 2) == b

                @pl.when(jnp.logical_and(this, gathers))
                def _():
                    wbuf[...] = win[:, :, :, cut]

                @pl.when(jnp.logical_and(this, jnp.logical_not(gathers)))
                def _():
                    wbuf[...] = got_win[hi, :, :, :, cut]
            for k, device in enumerate(in_column):
                remote(wbuf, wbuf, wsend.at[k], wrecv.at[0], device).start()

    def window_core():
        @pl.when(same_core)
        def _():
            @pl.when(jnp.logical_not(is_source))
            def _():
                wait(wbuf, wrecv.at[0])
            remote(wbuf, wbuf, wsend.at[ny - 1], wrecv.at[1], twin_core).start()

    def window_done():
        @pl.when(jnp.logical_not(same_core))
        def _():
            wait(wbuf, wrecv.at[1])

        @pl.loop(0, pairs // GSR)
        def _(b):
            at = pl.multiple_of(b * GSR, GSR)
            block = wbuf[pl.ds(b * 2, 2)].reshape(GSR, GSR)
            turned = block.astype(jnp.float32).T
            for w in range(NW):
                lhs[w * GSR:(w + 1) * GSR, pl.ds(at, GSR)] = (
                    turned * weights[w, pl.ds(b, 1), :]
                ).astype(jnp.bfloat16)

    early = EARLY * 4 * ncol

    def product(panel, low, high):
        return jnp.dot(
            lhs[:, low:high], panel.reshape(high - low, panel.shape[-1]), preferred_element_type=jnp.float32
        )

    def finish(chi, to, at, sem):
        to[...] = chi.astype(jnp.bfloat16).reshape(to.shape)
        write(to, at, sem).start()

    def write(to, at, sem):
        return pltpu.make_async_copy(to, out.at[:, :, pl.ds(at, to.shape[-1])], osem.at[sem])

    for same, h in ((True, hi), (False, 1 - hi)):
        exchanged(0, same)
        begin(lent, h, parts_a, WINDOW)
        tick(0, 0, (h,))
    for h in range(2):
        begin(win, h, parts_a, 0)
    window_tick(0)
    push(0, 1)
    exchange(1)
    window_tick(1)
    window_push(0, 3)
    for t in range(1, half + 1):
        if t < half // 2:
            window_tick(2 * t)
        if t == half // 2:
            for way in range(2):
                window_arrived(way, half)
            window_push(nz - 1, 1)
        if t == half // 2 + 1:
            window_y()
        if t < half:
            tick(0, t)
            push(place(0, t), 2)
        else:
            last(0)
            push(nz - 1, 1)
        if t < half // 2:
            window_tick(2 * t + 1)
            window_push(4 * t - 1, 4)
        if t == 1:
            for same, h in ((True, hi), (False, 1 - hi)):
                exchanged(1, same)
                for n in range(1, 3):
                    begin(bufs[n], h, parts_b, (n - 1) * OWN)
                    tick(n, 0, (h,))
        else:
            for n in range(1, 3):
                tick(n, t - 1)
        if t == half // 2 + 2:
            window_core()
        if t == half // 2 + 3:
            window_done()

            @pl.loop(0, 2)
            def _(h):
                finish(product(got_win[h], 0, pairs), out_win.at[h], lent_at(h, y), h)

    for n in range(2):
        sum_own[n] = product(bufs[1 + n][:EARLY], 0, early)

    @pl.loop(0, 2)
    def _(h):
        wait(got.at[h, pl.ds(0, EARLY + 1)], xrecv.at[h, 0])
        sum_got[h] = product(got[h, :EARLY], 0, early)

    for n in range(2):
        last(1 + n)
        finish(sum_own[n] + product(bufs[1 + n][EARLY:], early, pairs), out_own.at[n], 2 * LENT + n * OWN, 2 + n)

    @pl.loop(0, 2)
    def _(h):
        wait(got.at[h, pl.ds(EARLY + 1, nz - EARLY - 1)], xrecv.at[h, 1])
        finish(sum_got[h] + product(got[h, EARLY:], early, pairs), out_got.at[h], lent_at(h, y) + WINDOW, 4 + h)

    for way in range(2):
        wait(win.at[pl.ds(0, nz - 1), 0], nsend.at[way])
        for n in range(3):
            for h in range(2):
                wait(bufs[n].at[pl.ds(0, half if way == h else half - 1), h], zsend.at[way, n, h])
    for n in range(2):
        wait(lent, xsend.at[n])
        wait(win, xwsend.at[n])
    for n, parts in enumerate((parts_a, parts_b)):
        wait(parts.at[pl.ds(0, plane - 1)], part_send.at[n])

    @pl.when(is_source)
    def _():
        for k in range(ny - 1):
            wait(wbuf, wsend.at[k])

    @pl.when(same_core)
    def _():
        wait(wbuf, wsend.at[ny - 1])

    for h in range(2):
        write(out_own.at[h], 2 * LENT + h * OWN, 2 + h).wait()
        write(out_win.at[h], lent_at(h, y), h).wait()
        write(out_got.at[h], lent_at(h, y) + WINDOW, 4 + h).wait()


def on_device(pair_elements, energy_gaps, frequencies):
    rows, cols = lax.axis_size("row"), lax.axis_size("col")
    local, full = pair_elements.shape
    pairs = local * rows * cols
    block = full // cols
    nz, ny = rows // 2, cols // 4
    depth = local * cols
    plane = 2 * cols
    dma = pltpu.SemaphoreType.DMA

    def panels(width):
        return pltpu.VMEM((nz, 2, depth, width), jnp.bfloat16)

    operands = [
        pltpu.with_memory_space_constraint(operand, pltpu.HBM)
        for operand in (
            pair_elements.reshape(local, ny, 2, 2, block).transpose(1, 2, 3, 0, 4),
            energy_gaps.reshape(pairs // GSR, GSR),
            frequencies,
        )
    ]
    return pl.pallas_call(
        functools.partial(kernel, nz, ny, pairs),
        out_shape=jax.ShapeDtypeStruct((NW, GSR, block), jnp.bfloat16),
        in_specs=[pl.BlockSpec(memory_space=pl.ANY)] * 3,
        out_specs=pl.BlockSpec(memory_space=pl.ANY),
        scratch_shapes=[
            pltpu.VMEM((pairs // GSR, GSR), jnp.float32),
            pltpu.VMEM((4, pairs // GSR, GSR), jnp.float32),
            pltpu.VMEM((NW, pairs // GSR, GSR), jnp.float32),
            pltpu.SMEM((NW,), jnp.float32),
            pltpu.VMEM((plane, local, LENT), jnp.bfloat16),
            pltpu.VMEM((plane, local, 2 * OWN), jnp.bfloat16),
            panels(WINDOW),
            panels(OWN),
            panels(OWN),
            panels(LENT - WINDOW),
            pltpu.VMEM((2, nz, 2, depth, WINDOW), jnp.bfloat16),
            pltpu.VMEM((2, nz, 2, depth, LENT - WINDOW), jnp.bfloat16),
            panels(GSR),
            pltpu.VMEM((NW * GSR, pairs), jnp.bfloat16),
            pltpu.VMEM((2, NW * GSR, OWN), jnp.float32),
            pltpu.VMEM((2, NW * GSR, LENT - WINDOW), jnp.float32),
            pltpu.VMEM((2, NW, GSR, WINDOW), jnp.bfloat16),
            pltpu.VMEM((2, NW, GSR, OWN), jnp.bfloat16),
            pltpu.VMEM((2, NW, GSR, LENT - WINDOW), jnp.bfloat16),
            dma((2,)),
            dma((2,)),
            dma((2, 2)),
            dma((2,)),
            dma((2, nz // 2)),
            dma((2,)),
            dma((2, 3, 2, nz // 2)),
            dma((2, 3, 2)),
            dma((2,)),
            dma((2,)),
            dma((2, 2)),
            dma((2,)),
            dma((2,)),
            dma((ny,)),
            dma((6,)),
        ],
        compiler_params=pltpu.CompilerParams(
            collective_id=0, has_side_effects=True, vmem_limit_bytes=36 * 1024 * 1024
        ),
        cost_estimate=pl.CostEstimate(
            flops=2 * NW * GSR * pairs * block, bytes_accessed=2 * NW * GSR * block, transcendentals=0
        ),
    )(*operands)


def solution(mesh):
    in_specs = (P(("row", "col"), None), P(), P())
    out_specs = P(None, "row", "col")
    return jax.shard_map(
        on_device, mesh=mesh, in_specs=in_specs, out_specs=out_specs, check_vma=False
    )
```

```python
import functools
import math

import jax
import jax.numpy as jnp
from jax import lax
from jax.experimental import pallas as pl
from jax.experimental.pallas import tpu as pltpu
from jax.sharding import PartitionSpec as P

NW = 3
GSR = 128
WINDOW = 256
LENT = 1280
OWN = 640
EARLY = 12
MESH = pl.DeviceIdType.MESH


def kernel(nz, ny, pairs, elements, gaps_in, freqs_in, out, gaps, turned_gaps, weights, freqs,
           parts_a, parts_b, win, own_a, own_b, lent, got_win, got, wbuf, lhs,
           sum_own, sum_got, out_win, out_own, out_got, in_sem, part_sem, part_recv, part_send,
           nrecv, nsend, zrecv, zsend, xwrecv, xwsend, xrecv, xsend, wrecv, wsend, osem):
    row, col = lax.axis_index("row"), lax.axis_index("col")
    hi, z = row // nz, lax.rem(row, nz)
    ncol = ny * 4
    plane = 2 * ncol
    seat = hi * ncol + col
    y = col // 4
    in_y = lax.rem(col, 4)
    lo, core = in_y // 2, lax.rem(in_y, 2)
    up = (hi * nz + lax.rem(z + 1, nz), col)
    down = (hi * nz + lax.rem(z + nz - 1, nz), col)
    other_lo = y * 4 + (1 - lo) * 2 + core
    side = [(z, other_lo), (nz + z, other_lo)]
    in_column = [(row, lax.rem(y + k, ny) * 4 + in_y) for k in (1, 3, 2)]
    twin_core = (row, y * 4 + lo * 2 + (1 - core))
    half = nz // 2

    def seated(h, k):
        c = lax.rem(col + k, ncol)
        return h, c // 4, lax.rem(c, 4) // 2, lax.rem(c, 2)

    def device_at(h, y, lo, core):
        return h * nz + z, y * 4 + lo * 2 + core

    barrier = pltpu.get_barrier_semaphore()
    for device in (up, down):
        pl.semaphore_signal(barrier, inc=1, device_id=device, device_id_type=MESH)

    def for_others(do):
        pl.loop(1, ncol)(lambda k: do(seated(hi, k)))
        pl.loop(0, ncol)(lambda k: do(seated(1 - hi, k)))

    for_others(lambda to: pl.semaphore_signal(barrier, inc=1, device_id=device_at(*to), device_id_type=MESH))

    loads = [
        pltpu.make_async_copy(gaps_in, gaps, in_sem.at[0]),
        pltpu.make_async_copy(freqs_in, freqs, in_sem.at[1]),
    ]
    for load in loads:
        load.start()

    def lent_at(h, y):
        first = y // 2
        return pl.multiple_of((h + first - 2 * h * first) * LENT, 128)

    def lent_range(h, y, lo, core):
        return elements.at[y, 1 - lo, core, :, pl.ds(lent_at(h, y), LENT)]

    def own_range(h, y, lo, core):
        return elements.at[y, lo, core, :, pl.ds(2 * LENT, 2 * OWN)]

    ranges = ((lent_range, parts_a), (own_range, parts_b))
    mine = [
        pltpu.make_async_copy(source(hi, y, lo, core), parts.at[seat], part_sem.at[n])
        for n, (source, parts) in enumerate(ranges)
    ]
    for copy in mine:
        copy.start()
    pl.semaphore_wait(barrier, plane + 1)

    def remote(src, dst, send, recv, device):
        return pltpu.make_async_remote_copy(
            src_ref=src, dst_ref=dst, send_sem=send, recv_sem=recv, device_id=device, device_id_type=MESH
        )

    def wait(ref, sem):
        pltpu.make_async_copy(ref, ref, sem).wait()

    def exchange(n):
        source, parts = ranges[n]
        for_others(lambda to: remote(
            source(*to), parts.at[seat], part_send.at[n], part_recv.at[n, hi], device_at(*to)
        ).start())

    def exchanged(n, same):
        parts = ranges[n][1]
        if same:
            mine[n].wait()
        wait(parts.at[pl.ds(0, ncol - 1 if same else ncol)], part_recv.at[n, hi if same else 1 - hi])

    exchange(0)
    exchange(1)

    def weigh():
        for load in loads:
            load.wait()
        for k in range(4):
            turned_gaps[k] = pltpu.roll(gaps[...], k * 32, 1)
        quarter = lax.broadcasted_iota(jnp.int32, (1, GSR), 1) // 32

        @pl.loop(0, pairs // GSR)
        def _(b):
            line = jnp.zeros((1, GSR), jnp.float32)
            for q in range(4):
                plane_at = lax.rem(z + (b if q < 2 else nz - 1 - b), nz)
                shift = lax.rem(q + 4 - lax.rem(plane_at, 4), 4)
                piece = turned_gaps[shift, pl.ds(q % 2 * 4 + plane_at // 4, 1), :]
                line = jnp.where(quarter == q, piece, line)
            for w in range(NW):
                weights[w, pl.ds(b, 1), :] = (
                    -4.0 * line / ((line * line + freqs[w] * freqs[w]) * math.sqrt(pairs))
                )

    bufs = (lent, own_a, own_b)

    def begin(buf, h, parts, start):
        width = buf.shape[-1]
        part = parts[pl.ds(pl.multiple_of(h * ncol, ncol), ncol), :, start:start + width]
        buf[0, h] = part.reshape(2 * ncol, width)

    def place(way, s):
        return 0 if s == 0 else nz - 1 if s == half else 2 * s - 1 + way

    def push(first, count):
        late = int(first > EARLY)
        for n in range(2):
            remote(
                lent.at[pl.ds(first, count)], got.at[hi, pl.ds(first, count)],
                xsend.at[n], xrecv.at[hi, late], side[n],
            ).start()

    def arrived(n, h, way, s):
        wait(bufs[n].at[place(way, s), h], zrecv.at[way, n, h, s - 1])

    def tick(n, s, lanes=(0, 1)):
        for h in lanes:
            for way, device in ((0, up), (1, down)):
                if s > 0:
                    arrived(n, h, way, s)
                if s == half - 1 and way != h:
                    continue
                remote(
                    bufs[n].at[place(way, s), h], bufs[n].at[place(way, s + 1), h],
                    zsend.at[way, n, h], zrecv.at[way, n, h, s], device,
                ).start()

    def last(n):
        for h in range(2):
            arrived(n, h, h, half)

    def window_arrived(way, s):
        slab = win.at[place(way, s)]
        wait(slab.at[way] if s == half else slab, nrecv.at[way, s - 1])

    def window_tick(s):
        for way, device in ((0, up), (1, down)):
            if s > 0:
                window_arrived(way, s)
            src, dst = win.at[place(way, s)], win.at[place(way, s + 1)]
            if s == half - 1:
                src, dst = src.at[way], dst.at[way]
            remote(src, dst, nsend.at[way], nrecv.at[way, s], device).start()

    def window_push(first, count):
        for n in range(2):
            remote(
                win.at[pl.ds(first, count)], got_win.at[hi, pl.ds(first, count)],
                xwsend.at[n], xwrecv.at[hi], side[n],
            ).start()

    window_col = row // 2
    in_w = lax.rem(window_col, 4)
    same_core = core == lax.rem(in_w, 2)
    is_source = jnp.logical_and(same_core, y == window_col // 4)
    gathers = lo != in_w // 2

    def window_y():
        for h in range(2):
            wait(got_win.at[h], xwrecv.at[h])

        @pl.when(is_source)
        def _():
            for b in range(2):
                cut = slice(b * GSR, (b + 1) * GSR)
                this = lax.rem(row, 2) == b

                @pl.when(jnp.logical_and(this, gathers))
                def _():
                    wbuf[...] = win[:, :, :, cut]

                @pl.when(jnp.logical_and(this, jnp.logical_not(gathers)))
                def _():
                    wbuf[...] = got_win[hi, :, :, :, cut]
            for k, device in enumerate(in_column):
                remote(wbuf, wbuf, wsend.at[k], wrecv.at[0], device).start()

    def window_core():
        @pl.when(same_core)
        def _():
            @pl.when(jnp.logical_not(is_source))
            def _():
                wait(wbuf, wrecv.at[0])
            remote(wbuf, wbuf, wsend.at[ny - 1], wrecv.at[1], twin_core).start()

    def window_done():
        @pl.when(jnp.logical_not(same_core))
        def _():
            wait(wbuf, wrecv.at[1])

        @pl.loop(0, pairs // GSR)
        def _(b):
            at = pl.multiple_of(b * GSR, GSR)
            block = wbuf[pl.ds(b * 2, 2)].reshape(GSR, GSR)
            turned = block.astype(jnp.float32).T
            for w in range(NW):
                lhs[w * GSR:(w + 1) * GSR, pl.ds(at, GSR)] = (
                    turned * weights[w, pl.ds(b, 1), :]
                ).astype(jnp.bfloat16)

    early = EARLY * 4 * ncol

    def product(panel, low, high):
        return jnp.dot(
            lhs[:, low:high], panel.reshape(high - low, panel.shape[-1]), preferred_element_type=jnp.float32
        )

    def finish(chi, to, at, sem):
        to[...] = chi.astype(jnp.bfloat16).reshape(to.shape)
        write(to, at, sem).start()

    def write(to, at, sem):
        return pltpu.make_async_copy(to, out.at[:, :, pl.ds(at, to.shape[-1])], osem.at[sem])

    for same, h in ((True, hi), (False, 1 - hi)):
        exchanged(0, same)
        begin(lent, h, parts_a, WINDOW)
        tick(0, 0, (h,))
    for h in range(2):
        begin(win, h, parts_a, 0)
    window_tick(0)
    push(0, 1)
    window_tick(1)
    window_push(0, 3)
    for t in range(1, half + 1):
        if t < half // 2:
            window_tick(2 * t)
        if t == half // 2:
            for way in range(2):
                window_arrived(way, half)
            window_push(nz - 1, 1)
        if t == half // 2 + 1:
            window_y()
        if t < half:
            tick(0, t)
            push(place(0, t), 2)
        else:
            last(0)
            push(nz - 1, 1)
        if t < half // 2:
            window_tick(2 * t + 1)
            window_push(4 * t - 1, 4)
        if t == 1:
            for same, h in ((True, hi), (False, 1 - hi)):
                exchanged(1, same)
                for n in range(1, 3):
                    begin(bufs[n], h, parts_b, (n - 1) * OWN)
                    tick(n, 0, (h,))
        else:
            for n in range(1, 3):
                tick(n, t - 1)
        if t == 2:
            weigh()
        if t == half // 2 + 2:
            window_core()
        if t == half // 2 + 3:
            window_done()

            @pl.loop(0, 2)
            def _(h):
                finish(product(got_win[h], 0, pairs), out_win.at[h], lent_at(h, y), h)

            sum_own[0] = product(own_a[:EARLY], 0, early)

    sum_own[1] = product(own_b[:EARLY], 0, early)

    @pl.loop(0, 2)
    def _(h):
        wait(got.at[h, pl.ds(0, EARLY + 1)], xrecv.at[h, 0])
        sum_got[h] = product(got[h, :EARLY], 0, early)

    for n in range(2):
        last(1 + n)
        finish(sum_own[n] + product(bufs[1 + n][EARLY:], early, pairs), out_own.at[n], 2 * LENT + n * OWN, 2 + n)

    @pl.loop(0, 2)
    def _(h):
        wait(got.at[h, pl.ds(EARLY + 1, nz - EARLY - 1)], xrecv.at[h, 1])
        finish(sum_got[h] + product(got[h, EARLY:], early, pairs), out_got.at[h], lent_at(h, y) + WINDOW, 4 + h)

    for way in range(2):
        wait(win.at[pl.ds(0, nz - 1), 0], nsend.at[way])
        for n in range(3):
            for h in range(2):
                wait(bufs[n].at[pl.ds(0, half if way == h else half - 1), h], zsend.at[way, n, h])
    for n in range(2):
        wait(lent, xsend.at[n])
        wait(win, xwsend.at[n])
    for n, parts in enumerate((parts_a, parts_b)):
        wait(parts.at[pl.ds(0, plane - 1)], part_send.at[n])

    @pl.when(is_source)
    def _():
        for k in range(ny - 1):
            wait(wbuf, wsend.at[k])

    @pl.when(same_core)
    def _():
        wait(wbuf, wsend.at[ny - 1])

    for h in range(2):
        write(out_own.at[h], 2 * LENT + h * OWN, 2 + h).wait()
        write(out_win.at[h], lent_at(h, y), h).wait()
        write(out_got.at[h], lent_at(h, y) + WINDOW, 4 + h).wait()


def on_device(pair_elements, energy_gaps, frequencies):
    rows, cols = lax.axis_size("row"), lax.axis_size("col")
    local, full = pair_elements.shape
    pairs = local * rows * cols
    block = full // cols
    nz, ny = rows // 2, cols // 4
    depth = local * cols
    plane = 2 * cols
    dma = pltpu.SemaphoreType.DMA

    def panels(width):
        return pltpu.VMEM((nz, 2, depth, width), jnp.bfloat16)

    operands = [
        pltpu.with_memory_space_constraint(operand, pltpu.HBM)
        for operand in (
            pair_elements.reshape(local, ny, 2, 2, block).transpose(1, 2, 3, 0, 4),
            energy_gaps.reshape(pairs // GSR, GSR),
            frequencies,
        )
    ]
    return pl.pallas_call(
        functools.partial(kernel, nz, ny, pairs),
        out_shape=jax.ShapeDtypeStruct((NW, GSR, block), jnp.bfloat16),
        in_specs=[pl.BlockSpec(memory_space=pl.ANY)] * 3,
        out_specs=pl.BlockSpec(memory_space=pl.ANY),
        scratch_shapes=[
            pltpu.VMEM((pairs // GSR, GSR), jnp.float32),
            pltpu.VMEM((4, pairs // GSR, GSR), jnp.float32),
            pltpu.VMEM((NW, pairs // GSR, GSR), jnp.float32),
            pltpu.SMEM((NW,), jnp.float32),
            pltpu.VMEM((plane, local, LENT), jnp.bfloat16),
            pltpu.VMEM((plane, local, 2 * OWN), jnp.bfloat16),
            panels(WINDOW),
            panels(OWN),
            panels(OWN),
            panels(LENT - WINDOW),
            pltpu.VMEM((2, nz, 2, depth, WINDOW), jnp.bfloat16),
            pltpu.VMEM((2, nz, 2, depth, LENT - WINDOW), jnp.bfloat16),
            panels(GSR),
            pltpu.VMEM((NW * GSR, pairs), jnp.bfloat16),
            pltpu.VMEM((2, NW * GSR, OWN), jnp.float32),
            pltpu.VMEM((2, NW * GSR, LENT - WINDOW), jnp.float32),
            pltpu.VMEM((2, NW, GSR, WINDOW), jnp.bfloat16),
            pltpu.VMEM((2, NW, GSR, OWN), jnp.bfloat16),
            pltpu.VMEM((2, NW, GSR, LENT - WINDOW), jnp.bfloat16),
            dma((2,)),
            dma((2,)),
            dma((2, 2)),
            dma((2,)),
            dma((2, nz // 2)),
            dma((2,)),
            dma((2, 3, 2, nz // 2)),
            dma((2, 3, 2)),
            dma((2,)),
            dma((2,)),
            dma((2, 2)),
            dma((2,)),
            dma((2,)),
            dma((ny,)),
            dma((6,)),
        ],
        compiler_params=pltpu.CompilerParams(
            collective_id=0, has_side_effects=True, vmem_limit_bytes=36 * 1024 * 1024
        ),
        cost_estimate=pl.CostEstimate(
            flops=2 * NW * GSR * pairs * block, bytes_accessed=2 * NW * GSR * block, transcendentals=0
        ),
    )(*operands)


def solution(mesh):
    in_specs = (P(("row", "col"), None), P(), P())
    out_specs = P(None, "row", "col")
    return jax.shard_map(
        on_device, mesh=mesh, in_specs=in_specs, out_specs=out_specs, check_vma=False
    )
```

```python
import functools
import math

import jax
import jax.numpy as jnp
from jax import lax
from jax.experimental import pallas as pl
from jax.experimental.pallas import tpu as pltpu
from jax.sharding import PartitionSpec as P

NW = 3
GSR = 128
WINDOW = 256
LENT = 1024
OWN = 640
LENT_AT = 2 * WINDOW
OWN_AT = LENT_AT + 2 * LENT
EARLY = 12
MESH = pl.DeviceIdType.MESH


def kernel(nz, ny, pairs, elements, gaps_in, freqs_in, out, gaps, turned_gaps, weights, freqs,
           parts_lent, parts_win, parts_own, win, own_a, own_b, lent, got_win, got, wbuf, lhs,
           sum_own, sum_got, out_win, out_own, out_got, in_sem, part_sem, part_recv, part_send,
           nrecv, nsend, zrecv, zsend, xwrecv, xwsend, xrecv, xsend, wrecv, wsend, osem):
    row, col = lax.axis_index("row"), lax.axis_index("col")
    hi, z = row // nz, lax.rem(row, nz)
    ncol = ny * 4
    plane = 2 * ncol
    seat = hi * ncol + col
    y = col // 4
    in_y = lax.rem(col, 4)
    lo, core = in_y // 2, lax.rem(in_y, 2)
    up = (hi * nz + lax.rem(z + 1, nz), col)
    down = (hi * nz + lax.rem(z + nz - 1, nz), col)
    other_lo = y * 4 + (1 - lo) * 2 + core
    side = [(z, other_lo), (nz + z, other_lo)]
    in_column = [(row, lax.rem(y + k, ny) * 4 + in_y) for k in (1, 3, 2)]
    twin_core = (row, y * 4 + lo * 2 + (1 - core))
    half = nz // 2

    def seated(h, k):
        c = lax.rem(col + k, ncol)
        return h, c // 4, lax.rem(c, 4) // 2, lax.rem(c, 2)

    def device_at(h, y, lo, core):
        return h * nz + z, y * 4 + lo * 2 + core

    barrier = pltpu.get_barrier_semaphore()
    for device in (up, down):
        pl.semaphore_signal(barrier, inc=1, device_id=device, device_id_type=MESH)

    def for_same(do):
        pl.loop(1, ncol)(lambda k: do(seated(hi, k)))

    def for_others(do):
        for_same(do)
        pl.loop(0, ncol)(lambda k: do(seated(1 - hi, k)))

    for_others(lambda to: pl.semaphore_signal(barrier, inc=1, device_id=device_at(*to), device_id_type=MESH))

    loads = [
        pltpu.make_async_copy(gaps_in, gaps, in_sem.at[0]),
        pltpu.make_async_copy(freqs_in, freqs, in_sem.at[1]),
    ]
    for load in loads:
        load.start()

    def window_at(h, y):
        first = y // 2
        return pl.multiple_of((h + first - 2 * h * first) * WINDOW, 128)

    def lent_range(h, y, lo, core):
        return elements.at[y, 1 - lo, core, :, pl.ds(LENT_AT, 2 * LENT)]

    def window_range(h, y, lo, core):
        return elements.at[y, 1 - lo, core, :, pl.ds(window_at(h, y), WINDOW)]

    def own_range(h, y, lo, core):
        return elements.at[y, lo, core, :, pl.ds(OWN_AT, 2 * OWN)]

    ranges = ((lent_range, parts_lent), (window_range, parts_win), (own_range, parts_own))
    mine = [
        pltpu.make_async_copy(
            source(hi, y, lo, core), parts.at[col if n == 0 else seat], part_sem.at[n]
        )
        for n, (source, parts) in enumerate(ranges)
    ]
    for copy in mine:
        copy.start()
    pl.semaphore_wait(barrier, plane + 1)

    def remote(src, dst, send, recv, device):
        return pltpu.make_async_remote_copy(
            src_ref=src, dst_ref=dst, send_sem=send, recv_sem=recv, device_id=device, device_id_type=MESH
        )

    def wait(ref, sem):
        pltpu.make_async_copy(ref, ref, sem).wait()

    def exchange(n):
        source, parts = ranges[n]
        (for_same if n == 0 else for_others)(lambda to: remote(
            source(*to), parts.at[col if n == 0 else seat], part_send.at[n], part_recv.at[n, hi], device_at(*to)
        ).start())

    def exchanged(n, same):
        parts = ranges[n][1]
        if same:
            mine[n].wait()
        wait(parts.at[pl.ds(0, ncol - 1 if same else ncol)], part_recv.at[n, hi if same else 1 - hi])

    for n in range(3):
        exchange(n)

    def weigh():
        for load in loads:
            load.wait()
        for k in range(4):
            turned_gaps[k] = pltpu.roll(gaps[...], k * 32, 1)
        quarter = lax.broadcasted_iota(jnp.int32, (1, GSR), 1) // 32

        @pl.loop(0, pairs // GSR)
        def _(b):
            line = jnp.zeros((1, GSR), jnp.float32)
            for q in range(4):
                plane_at = lax.rem(z + (b if q < 2 else nz - 1 - b), nz)
                shift = lax.rem(q + 4 - lax.rem(plane_at, 4), 4)
                piece = turned_gaps[shift, pl.ds(q % 2 * 4 + plane_at // 4, 1), :]
                line = jnp.where(quarter == q, piece, line)
            for w in range(NW):
                weights[w, pl.ds(b, 1), :] = (
                    -4.0 * line / ((line * line + freqs[w] * freqs[w]) * math.sqrt(pairs))
                )

    owns = (own_a, own_b)

    def slab(n, h, at):
        return lent.at[h, at] if n == 0 else owns[n - 1].at[at, h]


    def begin(buf, h, parts, start):
        width = buf.shape[-1]
        part = parts[pl.ds(pl.multiple_of(h * ncol, ncol), ncol), :, start:start + width]
        buf[0, h] = part.reshape(2 * ncol, width)

    def place(way, s):
        return 0 if s == 0 else nz - 1 if s == half else 2 * s - 1 + way

    def push(first, count):
        late = int(first > EARLY)
        for n in range(2):
            remote(
                lent.at[:, pl.ds(first, count)], got.at[:, pl.ds(first, count), hi],
                xsend.at[n], xrecv.at[hi, late], side[n],
            ).start()

    def arrived(n, h, way, s):
        wait(slab(n, h, place(way, s)), zrecv.at[way, n, h, s - 1])

    def tick(n, s, lanes=(0, 1)):
        for h in lanes:
            for way, device in ((0, up), (1, down)):
                if s > 0:
                    arrived(n, h, way, s)
                if s == half - 1 and way != h:
                    continue
                remote(
                    slab(n, h, place(way, s)), slab(n, h, place(way, s + 1)),
                    zsend.at[way, n, h], zrecv.at[way, n, h, s], device,
                ).start()

    def last(n):
        for h in range(2):
            arrived(n, h, h, half)

    def window_arrived(way, s):
        part = win.at[place(way, s)]
        wait(part.at[way] if s == half else part, nrecv.at[way, s - 1])

    def window_tick(s):
        for way, device in ((0, up), (1, down)):
            if s > 0:
                window_arrived(way, s)
            src, dst = win.at[place(way, s)], win.at[place(way, s + 1)]
            if s == half - 1:
                src, dst = src.at[way], dst.at[way]
            remote(src, dst, nsend.at[way], nrecv.at[way, s], device).start()

    def window_push(first, count):
        for n in range(2):
            remote(
                win.at[pl.ds(first, count)], got_win.at[hi, pl.ds(first, count)],
                xwsend.at[n], xwrecv.at[hi], side[n],
            ).start()

    window_col = row // 2
    in_w = lax.rem(window_col, 4)
    same_core = core == lax.rem(in_w, 2)
    is_source = jnp.logical_and(same_core, y == window_col // 4)
    gathers = lo != in_w // 2

    def window_y():
        for h in range(2):
            wait(got_win.at[h], xwrecv.at[h])

        @pl.when(is_source)
        def _():
            for b in range(2):
                cut = slice(b * GSR, (b + 1) * GSR)
                this = lax.rem(row, 2) == b

                @pl.when(jnp.logical_and(this, gathers))
                def _():
                    wbuf[...] = win[:, :, :, cut]

                @pl.when(jnp.logical_and(this, jnp.logical_not(gathers)))
                def _():
                    wbuf[...] = got_win[hi, :, :, :, cut]
            for k, device in enumerate(in_column):
                remote(wbuf, wbuf, wsend.at[k], wrecv.at[0], device).start()

    def window_core():
        @pl.when(same_core)
        def _():
            @pl.when(jnp.logical_not(is_source))
            def _():
                wait(wbuf, wrecv.at[0])
            remote(wbuf, wbuf, wsend.at[ny - 1], wrecv.at[1], twin_core).start()

    def window_done():
        @pl.when(jnp.logical_not(same_core))
        def _():
            wait(wbuf, wrecv.at[1])

        @pl.loop(0, pairs // GSR)
        def _(b):
            at = pl.multiple_of(b * GSR, GSR)
            block = wbuf[pl.ds(b * 2, 2)].reshape(GSR, GSR)
            turned = block.astype(jnp.float32).T
            for w in range(NW):
                lhs[w * GSR:(w + 1) * GSR, pl.ds(at, GSR)] = (
                    turned * weights[w, pl.ds(b, 1), :]
                ).astype(jnp.bfloat16)

    early = EARLY * 4 * ncol

    def product(panel, low, high):
        return jnp.dot(
            lhs[:, low:high], panel.reshape(high - low, panel.shape[-1]), preferred_element_type=jnp.float32
        )

    def finish(chi, to, at, sem):
        to[...] = chi.astype(jnp.bfloat16).reshape(to.shape)
        write(to, at, sem).start()

    def write(to, at, sem):
        return pltpu.make_async_copy(to, out.at[:, :, pl.ds(at, to.shape[-1])], osem.at[sem])

    def lent_at(j):
        return pl.multiple_of(LENT_AT + j * LENT, 128)

    exchanged(0, True)
    for j in range(2):
        lent[j, 0] = parts_lent[:, :, j * LENT:(j + 1) * LENT].reshape(2 * ncol, LENT)
    tick(0, 0)
    push(0, 1)
    for same, h in ((True, hi), (False, 1 - hi)):
        exchanged(1, same)
        begin(win, h, parts_win, 0)
    window_tick(0)
    window_tick(1)
    window_push(0, 3)
    for t in range(1, half + 1):
        if t < half // 2:
            window_tick(2 * t)
        if t == half // 2:
            for way in range(2):
                window_arrived(way, half)
            window_push(nz - 1, 1)
        if t == half // 2 + 1:
            window_y()
        if t < half:
            tick(0, t)
            push(place(0, t), 2)
        else:
            last(0)
            push(nz - 1, 1)
        if t < half // 2:
            window_tick(2 * t + 1)
            window_push(4 * t - 1, 4)
        if t == 1:
            for same, h in ((True, hi), (False, 1 - hi)):
                exchanged(2, same)
                for n in range(1, 3):
                    begin(owns[n - 1], h, parts_own, (n - 1) * OWN)
                    tick(n, 0, (h,))
        else:
            for n in range(1, 3):
                tick(n, t - 1)
        if t == 2:
            weigh()
        if t == half // 2 + 2:
            window_core()
        if t == half // 2 + 3:
            window_done()

            @pl.loop(0, 2)
            def _(h):
                finish(product(got_win[h], 0, pairs), out_win.at[h], window_at(h, y), h)

            sum_own[0] = product(own_a[:EARLY], 0, early)

    sum_own[1] = product(own_b[:EARLY], 0, early)

    for h in range(2):
        wait(got.at[:, pl.ds(0, EARLY + 1), h], xrecv.at[h, 0])

    @pl.loop(0, 2)
    def _(j):
        sum_got[j] = product(got[j, :EARLY], 0, early)

    for n in range(2):
        last(1 + n)
        finish(sum_own[n] + product(owns[n][EARLY:], early, pairs), out_own.at[n], OWN_AT + n * OWN, 2 + n)
    for h in range(2):
        wait(got.at[:, pl.ds(EARLY + 1, nz - EARLY - 1), h], xrecv.at[h, 1])

    @pl.loop(0, 2)
    def _(j):
        finish(sum_got[j] + product(got[j, EARLY:], early, pairs), out_got.at[j], lent_at(j), 4 + j)

    for way in range(2):
        wait(win.at[pl.ds(0, nz - 1), 0], nsend.at[way])
        for h in range(2):
            count = half if way == h else half - 1
            wait(lent.at[h, pl.ds(0, count)], zsend.at[way, 0, h])
            for n in range(2):
                wait(owns[n].at[pl.ds(0, count), h], zsend.at[way, 1 + n, h])
    for n in range(2):
        wait(lent, xsend.at[n])
        wait(win, xwsend.at[n])
    wait(parts_lent.at[pl.ds(0, ncol - 1)], part_send.at[0])
    wait(parts_win.at[pl.ds(0, plane - 1)], part_send.at[1])
    wait(parts_own.at[pl.ds(0, plane - 1)], part_send.at[2])

    @pl.when(is_source)
    def _():
        for k in range(ny - 1):
            wait(wbuf, wsend.at[k])

    @pl.when(same_core)
    def _():
        wait(wbuf, wsend.at[ny - 1])

    for h in range(2):
        write(out_own.at[h], OWN_AT + h * OWN, 2 + h).wait()
        write(out_win.at[h], window_at(h, y), h).wait()
        write(out_got.at[h], lent_at(h), 4 + h).wait()


def on_device(pair_elements, energy_gaps, frequencies):
    rows, cols = lax.axis_size("row"), lax.axis_size("col")
    local, full = pair_elements.shape
    pairs = local * rows * cols
    block = full // cols
    nz, ny = rows // 2, cols // 4
    depth = local * cols
    plane = 2 * cols
    dma = pltpu.SemaphoreType.DMA

    def panels(width):
        return pltpu.VMEM((nz, 2, depth, width), jnp.bfloat16)

    operands = [
        pltpu.with_memory_space_constraint(operand, pltpu.HBM)
        for operand in (
            pair_elements.reshape(local, ny, 2, 2, block).transpose(1, 2, 3, 0, 4),
            energy_gaps.reshape(pairs // GSR, GSR),
            frequencies,
        )
    ]
    return pl.pallas_call(
        functools.partial(kernel, nz, ny, pairs),
        out_shape=jax.ShapeDtypeStruct((NW, GSR, block), jnp.bfloat16),
        in_specs=[pl.BlockSpec(memory_space=pl.ANY)] * 3,
        out_specs=pl.BlockSpec(memory_space=pl.ANY),
        scratch_shapes=[
            pltpu.VMEM((pairs // GSR, GSR), jnp.float32),
            pltpu.VMEM((4, pairs // GSR, GSR), jnp.float32),
            pltpu.VMEM((NW, pairs // GSR, GSR), jnp.float32),
            pltpu.SMEM((NW,), jnp.float32),
            pltpu.VMEM((cols, local, 2 * LENT), jnp.bfloat16),
            pltpu.VMEM((plane, local, WINDOW), jnp.bfloat16),
            pltpu.VMEM((plane, local, 2 * OWN), jnp.bfloat16),
            panels(WINDOW),
            panels(OWN),
            panels(OWN),
            pltpu.VMEM((2, nz, depth, LENT), jnp.bfloat16),
            pltpu.VMEM((2, nz, 2, depth, WINDOW), jnp.bfloat16),
            pltpu.VMEM((2, nz, 2, depth, LENT), jnp.bfloat16),
            panels(GSR),
            pltpu.VMEM((NW * GSR, pairs), jnp.bfloat16),
            pltpu.VMEM((2, NW * GSR, OWN), jnp.float32),
            pltpu.VMEM((2, NW * GSR, LENT), jnp.float32),
            pltpu.VMEM((2, NW, GSR, WINDOW), jnp.bfloat16),
            pltpu.VMEM((2, NW, GSR, OWN), jnp.bfloat16),
            pltpu.VMEM((2, NW, GSR, LENT), jnp.bfloat16),
            dma((2,)),
            dma((3,)),
            dma((3, 2)),
            dma((3,)),
            dma((2, nz // 2)),
            dma((2,)),
            dma((2, 3, 2, nz // 2)),
            dma((2, 3, 2)),
            dma((2,)),
            dma((2,)),
            dma((2, 2)),
            dma((2,)),
            dma((2,)),
            dma((ny,)),
            dma((6,)),
        ],
        compiler_params=pltpu.CompilerParams(
            collective_id=0, has_side_effects=True, vmem_limit_bytes=36 * 1024 * 1024
        ),
        cost_estimate=pl.CostEstimate(
            flops=2 * NW * GSR * pairs * block, bytes_accessed=2 * NW * GSR * block, transcendentals=0
        ),
    )(*operands)


def solution(mesh):
    in_specs = (P(("row", "col"), None), P(), P())
    out_specs = P(None, "row", "col")
    return jax.shard_map(
        on_device, mesh=mesh, in_specs=in_specs, out_specs=out_specs, check_vma=False
    )
```

```python
import functools
import math

import jax
import jax.numpy as jnp
from jax import lax
from jax.experimental import pallas as pl
from jax.experimental.pallas import tpu as pltpu
from jax.sharding import PartitionSpec as P

NW = 3
GSR = 128
WINDOW = 256
LENT = 1024
OWN = 640
LENT_AT = 2 * WINDOW
OWN_AT = LENT_AT + 2 * LENT
EARLY = 12
MESH = pl.DeviceIdType.MESH


def kernel(nz, ny, pairs, elements, gaps_in, freqs_in, out, gaps, turned_gaps, weights, freqs,
           parts_lent, parts_win, parts_own, win, own_a, own_b, lent, got_win, got, wbuf, lhs,
           sum_own, sum_got, out_win, out_own, out_got, in_sem, part_sem, part_recv, part_send,
           nrecv, nsend, zrecv, zsend, xwrecv, xwsend, xrecv, xsend, wrecv, wsend, osem):
    row, col = lax.axis_index("row"), lax.axis_index("col")
    hi, z = row // nz, lax.rem(row, nz)
    ncol = ny * 4
    plane = 2 * ncol
    seat = hi * ncol + col
    y = col // 4
    in_y = lax.rem(col, 4)
    lo, core = in_y // 2, lax.rem(in_y, 2)
    up = (hi * nz + lax.rem(z + 1, nz), col)
    down = (hi * nz + lax.rem(z + nz - 1, nz), col)
    other_lo = y * 4 + (1 - lo) * 2 + core
    side = [(z, other_lo), (nz + z, other_lo)]
    in_column = [(row, lax.rem(y + k, ny) * 4 + in_y) for k in (1, 3, 2)]
    twin_core = (row, y * 4 + lo * 2 + (1 - core))
    half = nz // 2

    def seated(h, k):
        c = lax.rem(col + k, ncol)
        return h, c // 4, lax.rem(c, 4) // 2, lax.rem(c, 2)

    def device_at(h, y, lo, core):
        return h * nz + z, y * 4 + lo * 2 + core

    barrier = pltpu.get_barrier_semaphore()
    for device in (up, down):
        pl.semaphore_signal(barrier, inc=1, device_id=device, device_id_type=MESH)

    def for_same(do):
        pl.loop(1, ncol)(lambda k: do(seated(hi, k)))

    def for_others(do):
        for_same(do)
        pl.loop(0, ncol)(lambda k: do(seated(1 - hi, k)))

    for_others(lambda to: pl.semaphore_signal(barrier, inc=1, device_id=device_at(*to), device_id_type=MESH))

    loads = [
        pltpu.make_async_copy(gaps_in, gaps, in_sem.at[0]),
        pltpu.make_async_copy(freqs_in, freqs, in_sem.at[1]),
    ]
    for load in loads:
        load.start()

    def window_at(h, y):
        first = y // 2
        return pl.multiple_of((h + first - 2 * h * first) * WINDOW, 128)

    def lent_range(h, y, lo, core):
        return elements.at[y, 1 - lo, core, :, pl.ds(LENT_AT, 2 * LENT)]

    def window_range(h, y, lo, core):
        return elements.at[y, 1 - lo, core, :, pl.ds(window_at(h, y), WINDOW)]

    def own_range(h, y, lo, core):
        return elements.at[y, lo, core, :, pl.ds(OWN_AT, 2 * OWN)]

    ranges = ((lent_range, parts_lent), (window_range, parts_win), (own_range, parts_own))
    mine = [
        pltpu.make_async_copy(
            source(hi, y, lo, core), parts.at[col if n == 0 else seat], part_sem.at[n]
        )
        for n, (source, parts) in enumerate(ranges)
    ]
    for copy in mine:
        copy.start()
    pl.semaphore_wait(barrier, plane + 1)

    def remote(src, dst, send, recv, device):
        return pltpu.make_async_remote_copy(
            src_ref=src, dst_ref=dst, send_sem=send, recv_sem=recv, device_id=device, device_id_type=MESH
        )

    def wait(ref, sem):
        pltpu.make_async_copy(ref, ref, sem).wait()

    def exchange(n):
        source, parts = ranges[n]
        (for_same if n == 0 else for_others)(lambda to: remote(
            source(*to), parts.at[col if n == 0 else seat], part_send.at[n], part_recv.at[n, hi], device_at(*to)
        ).start())

    def exchanged(n, same):
        parts = ranges[n][1]
        if same:
            mine[n].wait()
        wait(parts.at[pl.ds(0, ncol - 1 if same else ncol)], part_recv.at[n, hi if same else 1 - hi])

    for n in range(2):
        exchange(n)

    def weigh():
        for load in loads:
            load.wait()
        for k in range(4):
            turned_gaps[k] = pltpu.roll(gaps[...], k * 32, 1)
        quarter = lax.broadcasted_iota(jnp.int32, (1, GSR), 1) // 32

        @pl.loop(0, pairs // GSR)
        def _(b):
            line = jnp.zeros((1, GSR), jnp.float32)
            for q in range(4):
                plane_at = lax.rem(z + (b if q < 2 else nz - 1 - b), nz)
                shift = lax.rem(q + 4 - lax.rem(plane_at, 4), 4)
                piece = turned_gaps[shift, pl.ds(q % 2 * 4 + plane_at // 4, 1), :]
                line = jnp.where(quarter == q, piece, line)
            for w in range(NW):
                weights[w, pl.ds(b, 1), :] = (
                    -4.0 * line / ((line * line + freqs[w] * freqs[w]) * math.sqrt(pairs))
                )

    owns = (own_a, own_b)

    def slab(n, h, at):
        return lent.at[h, at] if n == 0 else owns[n - 1].at[at, h]


    def begin(buf, h, parts, start):
        width = buf.shape[-1]
        part = parts[pl.ds(pl.multiple_of(h * ncol, ncol), ncol), :, start:start + width]
        buf[0, h] = part.reshape(2 * ncol, width)

    def place(way, s):
        return 0 if s == 0 else nz - 1 if s == half else 2 * s - 1 + way

    def push(first, count):
        late = int(first > EARLY)
        for n in range(2):
            remote(
                lent.at[:, pl.ds(first, count)], got.at[:, pl.ds(first, count), hi],
                xsend.at[n], xrecv.at[hi, late], side[n],
            ).start()

    def arrived(n, h, way, s):
        wait(slab(n, h, place(way, s)), zrecv.at[way, n, h, s - 1])

    def tick(n, s, lanes=(0, 1)):
        for h in lanes:
            for way, device in ((0, up), (1, down)):
                if s > 0:
                    arrived(n, h, way, s)
                if s == half - 1 and way != h:
                    continue
                remote(
                    slab(n, h, place(way, s)), slab(n, h, place(way, s + 1)),
                    zsend.at[way, n, h], zrecv.at[way, n, h, s], device,
                ).start()

    def last(n):
        for h in range(2):
            arrived(n, h, h, half)

    def window_arrived(way, s):
        part = win.at[place(way, s)]
        wait(part.at[way] if s == half else part, nrecv.at[way, s - 1])

    def window_tick(s):
        for way, device in ((0, up), (1, down)):
            if s > 0:
                window_arrived(way, s)
            src, dst = win.at[place(way, s)], win.at[place(way, s + 1)]
            if s == half - 1:
                src, dst = src.at[way], dst.at[way]
            remote(src, dst, nsend.at[way], nrecv.at[way, s], device).start()

    def window_push(first, count):
        for n in range(2):
            remote(
                win.at[pl.ds(first, count)], got_win.at[hi, pl.ds(first, count)],
                xwsend.at[n], xwrecv.at[hi], side[n],
            ).start()

    window_col = row // 2
    in_w = lax.rem(window_col, 4)
    same_core = core == lax.rem(in_w, 2)
    is_source = jnp.logical_and(same_core, y == window_col // 4)
    gathers = lo != in_w // 2

    def window_y():
        for h in range(2):
            wait(got_win.at[h], xwrecv.at[h])

        @pl.when(is_source)
        def _():
            for b in range(2):
                cut = slice(b * GSR, (b + 1) * GSR)
                this = lax.rem(row, 2) == b

                @pl.when(jnp.logical_and(this, gathers))
                def _():
                    wbuf[...] = win[:, :, :, cut]

                @pl.when(jnp.logical_and(this, jnp.logical_not(gathers)))
                def _():
                    wbuf[...] = got_win[hi, :, :, :, cut]
            for k, device in enumerate(in_column):
                remote(wbuf, wbuf, wsend.at[k], wrecv.at[0], device).start()

    def window_core():
        @pl.when(same_core)
        def _():
            @pl.when(jnp.logical_not(is_source))
            def _():
                wait(wbuf, wrecv.at[0])
            remote(wbuf, wbuf, wsend.at[ny - 1], wrecv.at[1], twin_core).start()

    def window_done():
        @pl.when(jnp.logical_not(same_core))
        def _():
            wait(wbuf, wrecv.at[1])

        @pl.loop(0, pairs // GSR)
        def _(b):
            at = pl.multiple_of(b * GSR, GSR)
            block = wbuf[pl.ds(b * 2, 2)].reshape(GSR, GSR)
            turned = block.astype(jnp.float32).T
            for w in range(NW):
                lhs[w * GSR:(w + 1) * GSR, pl.ds(at, GSR)] = (
                    turned * weights[w, pl.ds(b, 1), :]
                ).astype(jnp.bfloat16)

    early = EARLY * 4 * ncol

    def product(panel, low, high):
        return jnp.dot(
            lhs[:, low:high], panel.reshape(high - low, panel.shape[-1]), preferred_element_type=jnp.float32
        )

    def finish(chi, to, at, sem):
        to[...] = chi.astype(jnp.bfloat16).reshape(to.shape)
        write(to, at, sem).start()

    def write(to, at, sem):
        return pltpu.make_async_copy(to, out.at[:, :, pl.ds(at, to.shape[-1])], osem.at[sem])

    def lent_at(j):
        return pl.multiple_of(LENT_AT + j * LENT, 128)

    exchanged(0, True)
    for j in range(2):
        lent[j, 0] = parts_lent[:, :, j * LENT:(j + 1) * LENT].reshape(2 * ncol, LENT)
    tick(0, 0)
    push(0, 1)
    exchange(2)
    for same, h in ((True, hi), (False, 1 - hi)):
        exchanged(1, same)
        begin(win, h, parts_win, 0)
    window_tick(0)
    window_tick(1)
    window_push(0, 3)
    for t in range(1, half + 1):
        if t < half // 2:
            window_tick(2 * t)
        if t == half // 2:
            for way in range(2):
                window_arrived(way, half)
            window_push(nz - 1, 1)
        if t == half // 2 + 1:
            window_y()
        if t < half:
            tick(0, t)
            push(place(0, t), 2)
        else:
            last(0)
            push(nz - 1, 1)
        if t < half // 2:
            window_tick(2 * t + 1)
            window_push(4 * t - 1, 4)
        if t == 1:
            for same, h in ((True, hi), (False, 1 - hi)):
                exchanged(2, same)
                for n in range(1, 3):
                    begin(owns[n - 1], h, parts_own, (n - 1) * OWN)
                    tick(n, 0, (h,))
        else:
            for n in range(1, 3):
                tick(n, t - 1)
        if t == 2:
            weigh()
        if t == half // 2 + 2:
            window_core()
        if t == half // 2 + 3:
            window_done()

            @pl.loop(0, 2)
            def _(h):
                finish(product(got_win[h], 0, pairs), out_win.at[h], window_at(h, y), h)

            sum_own[0] = product(own_a[:EARLY], 0, early)

    sum_own[1] = product(own_b[:EARLY], 0, early)

    for h in range(2):
        wait(got.at[:, pl.ds(0, EARLY + 1), h], xrecv.at[h, 0])

    @pl.loop(0, 2)
    def _(j):
        sum_got[j] = product(got[j, :EARLY], 0, early)

    for h in range(2):
        wait(got.at[:, pl.ds(EARLY + 1, nz - EARLY - 1), h], xrecv.at[h, 1])

    @pl.loop(0, 2)
    def _(j):
        finish(sum_got[j] + product(got[j, EARLY:], early, pairs), out_got.at[j], lent_at(j), 4 + j)

    for n in range(2):
        last(1 + n)
        finish(sum_own[n] + product(owns[n][EARLY:], early, pairs), out_own.at[n], OWN_AT + n * OWN, 2 + n)

    for way in range(2):
        wait(win.at[pl.ds(0, nz - 1), 0], nsend.at[way])
        for h in range(2):
            count = half if way == h else half - 1
            wait(lent.at[h, pl.ds(0, count)], zsend.at[way, 0, h])
            for n in range(2):
                wait(owns[n].at[pl.ds(0, count), h], zsend.at[way, 1 + n, h])
    for n in range(2):
        wait(lent, xsend.at[n])
        wait(win, xwsend.at[n])
    wait(parts_lent.at[pl.ds(0, ncol - 1)], part_send.at[0])
    wait(parts_win.at[pl.ds(0, plane - 1)], part_send.at[1])
    wait(parts_own.at[pl.ds(0, plane - 1)], part_send.at[2])

    @pl.when(is_source)
    def _():
        for k in range(ny - 1):
            wait(wbuf, wsend.at[k])

    @pl.when(same_core)
    def _():
        wait(wbuf, wsend.at[ny - 1])

    for h in range(2):
        write(out_own.at[h], OWN_AT + h * OWN, 2 + h).wait()
        write(out_win.at[h], window_at(h, y), h).wait()
        write(out_got.at[h], lent_at(h), 4 + h).wait()


def on_device(pair_elements, energy_gaps, frequencies):
    rows, cols = lax.axis_size("row"), lax.axis_size("col")
    local, full = pair_elements.shape
    pairs = local * rows * cols
    block = full // cols
    nz, ny = rows // 2, cols // 4
    depth = local * cols
    plane = 2 * cols
    dma = pltpu.SemaphoreType.DMA

    def panels(width):
        return pltpu.VMEM((nz, 2, depth, width), jnp.bfloat16)

    operands = [
        pltpu.with_memory_space_constraint(operand, pltpu.HBM)
        for operand in (
            pair_elements.reshape(local, ny, 2, 2, block).transpose(1, 2, 3, 0, 4),
            energy_gaps.reshape(pairs // GSR, GSR),
            frequencies,
        )
    ]
    return pl.pallas_call(
        functools.partial(kernel, nz, ny, pairs),
        out_shape=jax.ShapeDtypeStruct((NW, GSR, block), jnp.bfloat16),
        in_specs=[pl.BlockSpec(memory_space=pl.ANY)] * 3,
        out_specs=pl.BlockSpec(memory_space=pl.ANY),
        scratch_shapes=[
            pltpu.VMEM((pairs // GSR, GSR), jnp.float32),
            pltpu.VMEM((4, pairs // GSR, GSR), jnp.float32),
            pltpu.VMEM((NW, pairs // GSR, GSR), jnp.float32),
            pltpu.SMEM((NW,), jnp.float32),
            pltpu.VMEM((cols, local, 2 * LENT), jnp.bfloat16),
            pltpu.VMEM((plane, local, WINDOW), jnp.bfloat16),
            pltpu.VMEM((plane, local, 2 * OWN), jnp.bfloat16),
            panels(WINDOW),
            panels(OWN),
            panels(OWN),
            pltpu.VMEM((2, nz, depth, LENT), jnp.bfloat16),
            pltpu.VMEM((2, nz, 2, depth, WINDOW), jnp.bfloat16),
            pltpu.VMEM((2, nz, 2, depth, LENT), jnp.bfloat16),
            panels(GSR),
            pltpu.VMEM((NW * GSR, pairs), jnp.bfloat16),
            pltpu.VMEM((2, NW * GSR, OWN), jnp.float32),
            pltpu.VMEM((2, NW * GSR, LENT), jnp.float32),
            pltpu.VMEM((2, NW, GSR, WINDOW), jnp.bfloat16),
            pltpu.VMEM((2, NW, GSR, OWN), jnp.bfloat16),
            pltpu.VMEM((2, NW, GSR, LENT), jnp.bfloat16),
            dma((2,)),
            dma((3,)),
            dma((3, 2)),
            dma((3,)),
            dma((2, nz // 2)),
            dma((2,)),
            dma((2, 3, 2, nz // 2)),
            dma((2, 3, 2)),
            dma((2,)),
            dma((2,)),
            dma((2, 2)),
            dma((2,)),
            dma((2,)),
            dma((ny,)),
            dma((6,)),
        ],
        compiler_params=pltpu.CompilerParams(
            collective_id=0, has_side_effects=True, vmem_limit_bytes=36 * 1024 * 1024
        ),
        cost_estimate=pl.CostEstimate(
            flops=2 * NW * GSR * pairs * block, bytes_accessed=2 * NW * GSR * block, transcendentals=0
        ),
    )(*operands)


def solution(mesh):
    in_specs = (P(("row", "col"), None), P(), P())
    out_specs = P(None, "row", "col")
    return jax.shard_map(
        on_device, mesh=mesh, in_specs=in_specs, out_specs=out_specs, check_vma=False
    )
```

```python
import functools
import math

import jax
import jax.numpy as jnp
from jax import lax
from jax.experimental import pallas as pl
from jax.experimental.pallas import tpu as pltpu
from jax.sharding import PartitionSpec as P

NW = 3
GSR = 128
WINDOW = 256
LENT = 1024
OWN = 640
LENT_AT = 2 * WINDOW
OWN_AT = LENT_AT + 2 * LENT
EARLY = 12
MESH = pl.DeviceIdType.MESH


def kernel(nz, ny, pairs, elements, gaps_in, freqs_in, out, gaps, turned_gaps, weights, freqs,
           parts_lent, parts_win, parts_own, win, own_a, own_b, lent, got_win, got, wbuf, lhs,
           sum_own, sum_got, out_win, out_own, out_got, in_sem, part_sem, part_recv, part_send,
           nrecv, nsend, zrecv, zsend, xwrecv, xwsend, xrecv, xsend, wrecv, wsend, osem):
    row, col = lax.axis_index("row"), lax.axis_index("col")
    hi, z = row // nz, lax.rem(row, nz)
    ncol = ny * 4
    plane = 2 * ncol
    seat = hi * ncol + col
    y = col // 4
    in_y = lax.rem(col, 4)
    lo, core = in_y // 2, lax.rem(in_y, 2)
    up = (hi * nz + lax.rem(z + 1, nz), col)
    down = (hi * nz + lax.rem(z + nz - 1, nz), col)
    other_lo = y * 4 + (1 - lo) * 2 + core
    side = [(z, other_lo), (nz + z, other_lo)]
    in_column = [(row, lax.rem(y + k, ny) * 4 + in_y) for k in (1, 3, 2)]
    twin_core = (row, y * 4 + lo * 2 + (1 - core))
    half = nz // 2

    def seated(h, k):
        c = lax.rem(col + k, ncol)
        return h, c // 4, lax.rem(c, 4) // 2, lax.rem(c, 2)

    def device_at(h, y, lo, core):
        return h * nz + z, y * 4 + lo * 2 + core

    barrier = pltpu.get_barrier_semaphore()
    for device in (up, down):
        pl.semaphore_signal(barrier, inc=1, device_id=device, device_id_type=MESH)

    def for_same(do):
        pl.loop(1, ncol)(lambda k: do(seated(hi, k)))

    def for_others(do):
        for_same(do)
        pl.loop(0, ncol)(lambda k: do(seated(1 - hi, k)))

    for_others(lambda to: pl.semaphore_signal(barrier, inc=1, device_id=device_at(*to), device_id_type=MESH))

    loads = [
        pltpu.make_async_copy(gaps_in, gaps, in_sem.at[0]),
        pltpu.make_async_copy(freqs_in, freqs, in_sem.at[1]),
    ]
    for load in loads:
        load.start()

    def window_at(h, y):
        first = y // 2
        return pl.multiple_of((h + first - 2 * h * first) * WINDOW, 128)

    def lent_range(h, y, lo, core):
        return elements.at[y, 1 - lo, core, :, pl.ds(LENT_AT, 2 * LENT)]

    def window_range(h, y, lo, core):
        return elements.at[y, 1 - lo, core, :, pl.ds(window_at(h, y), WINDOW)]

    def own_range(h, y, lo, core):
        return elements.at[y, lo, core, :, pl.ds(OWN_AT, 2 * OWN)]

    ranges = ((lent_range, parts_lent), (window_range, parts_win), (own_range, parts_own))
    mine = [
        pltpu.make_async_copy(
            source(hi, y, lo, core), parts.at[col if n == 0 else seat], part_sem.at[n]
        )
        for n, (source, parts) in enumerate(ranges)
    ]
    for copy in mine:
        copy.start()
    pl.semaphore_wait(barrier, plane + 1)

    def remote(src, dst, send, recv, device):
        return pltpu.make_async_remote_copy(
            src_ref=src, dst_ref=dst, send_sem=send, recv_sem=recv, device_id=device, device_id_type=MESH
        )

    def wait(ref, sem):
        pltpu.make_async_copy(ref, ref, sem).wait()

    def exchange(n):
        source, parts = ranges[n]
        (for_same if n == 0 else for_others)(lambda to: remote(
            source(*to), parts.at[col if n == 0 else seat], part_send.at[n], part_recv.at[n, hi], device_at(*to)
        ).start())

    def exchanged(n, same):
        parts = ranges[n][1]
        if same:
            mine[n].wait()
        wait(parts.at[pl.ds(0, ncol - 1 if same else ncol)], part_recv.at[n, hi if same else 1 - hi])

    for n in range(2):
        exchange(n)

    def weigh():
        for load in loads:
            load.wait()
        for k in range(4):
            turned_gaps[k] = pltpu.roll(gaps[...], k * 32, 1)
        quarter = lax.broadcasted_iota(jnp.int32, (1, GSR), 1) // 32

        @pl.loop(0, pairs // GSR)
        def _(b):
            line = jnp.zeros((1, GSR), jnp.float32)
            for q in range(4):
                plane_at = lax.rem(z + (b if q < 2 else nz - 1 - b), nz)
                shift = lax.rem(q + 4 - lax.rem(plane_at, 4), 4)
                piece = turned_gaps[shift, pl.ds(q % 2 * 4 + plane_at // 4, 1), :]
                line = jnp.where(quarter == q, piece, line)
            for w in range(NW):
                weights[w, pl.ds(b, 1), :] = (
                    -4.0 * line / ((line * line + freqs[w] * freqs[w]) * math.sqrt(pairs))
                )

    owns = (own_a, own_b)

    def slab(n, h, at):
        return lent.at[h, at] if n == 0 else owns[n - 1].at[at, h]


    def begin(buf, h, parts, start):
        width = buf.shape[-1]
        part = parts[pl.ds(pl.multiple_of(h * ncol, ncol), ncol), :, start:start + width]
        buf[0, h] = part.reshape(2 * ncol, width)

    def place(way, s):
        return 0 if s == 0 else nz - 1 if s == half else 2 * s - 1 + way

    def push(j, first, count):
        late = int(first > EARLY)
        for n in range(2):
            remote(
                lent.at[j, pl.ds(first, count)], got.at[j, pl.ds(first, count), hi],
                xsend.at[n], xrecv.at[hi, late], side[n],
            ).start()

    def arrived(n, h, way, s):
        wait(slab(n, h, place(way, s)), zrecv.at[way, n, h, s - 1])

    def tick(n, s, lanes=(0, 1)):
        for h in lanes:
            for way, device in ((0, up), (1, down)):
                if s > 0:
                    arrived(n, h, way, s)
                if s == half - 1 and way != h:
                    continue
                remote(
                    slab(n, h, place(way, s)), slab(n, h, place(way, s + 1)),
                    zsend.at[way, n, h], zrecv.at[way, n, h, s], device,
                ).start()

    def last(n):
        for h in range(2):
            arrived(n, h, h, half)

    def window_arrived(way, s):
        part = win.at[place(way, s)]
        wait(part.at[way] if s == half else part, nrecv.at[way, s - 1])

    def window_tick(s):
        for way, device in ((0, up), (1, down)):
            if s > 0:
                window_arrived(way, s)
            src, dst = win.at[place(way, s)], win.at[place(way, s + 1)]
            if s == half - 1:
                src, dst = src.at[way], dst.at[way]
            remote(src, dst, nsend.at[way], nrecv.at[way, s], device).start()

    def window_push(first, count):
        for n in range(2):
            remote(
                win.at[pl.ds(first, count)], got_win.at[hi, pl.ds(first, count)],
                xwsend.at[n], xwrecv.at[hi], side[n],
            ).start()

    window_col = row // 2
    in_w = lax.rem(window_col, 4)
    same_core = core == lax.rem(in_w, 2)
    is_source = jnp.logical_and(same_core, y == window_col // 4)
    gathers = lo != in_w // 2

    def window_y():
        for h in range(2):
            wait(got_win.at[h], xwrecv.at[h])

        @pl.when(is_source)
        def _():
            for b in range(2):
                cut = slice(b * GSR, (b + 1) * GSR)
                this = lax.rem(row, 2) == b

                @pl.when(jnp.logical_and(this, gathers))
                def _():
                    wbuf[...] = win[:, :, :, cut]

                @pl.when(jnp.logical_and(this, jnp.logical_not(gathers)))
                def _():
                    wbuf[...] = got_win[hi, :, :, :, cut]
            for k, device in enumerate(in_column):
                remote(wbuf, wbuf, wsend.at[k], wrecv.at[0], device).start()

    def window_core():
        @pl.when(same_core)
        def _():
            @pl.when(jnp.logical_not(is_source))
            def _():
                wait(wbuf, wrecv.at[0])
            remote(wbuf, wbuf, wsend.at[ny - 1], wrecv.at[1], twin_core).start()

    def window_done():
        @pl.when(jnp.logical_not(same_core))
        def _():
            wait(wbuf, wrecv.at[1])

        @pl.loop(0, pairs // GSR)
        def _(b):
            at = pl.multiple_of(b * GSR, GSR)
            block = wbuf[pl.ds(b * 2, 2)].reshape(GSR, GSR)
            turned = block.astype(jnp.float32).T
            for w in range(NW):
                lhs[w * GSR:(w + 1) * GSR, pl.ds(at, GSR)] = (
                    turned * weights[w, pl.ds(b, 1), :]
                ).astype(jnp.bfloat16)

    early = EARLY * 4 * ncol

    def product(panel, low, high):
        return jnp.dot(
            lhs[:, low:high], panel.reshape(high - low, panel.shape[-1]), preferred_element_type=jnp.float32
        )

    def finish(chi, to, at, sem):
        to[...] = chi.astype(jnp.bfloat16).reshape(to.shape)
        write(to, at, sem).start()

    def write(to, at, sem):
        return pltpu.make_async_copy(to, out.at[:, :, pl.ds(at, to.shape[-1])], osem.at[sem])

    def lent_at(j):
        return pl.multiple_of(LENT_AT + j * LENT, 128)

    exchanged(0, True)
    for j in range(2):
        lent[j, 0] = parts_lent[:, :, j * LENT:(j + 1) * LENT].reshape(2 * ncol, LENT)
    tick(0, 0)
    for j in range(2):
        push(j, 0, 1)
    exchange(2)
    for same, h in ((True, hi), (False, 1 - hi)):
        exchanged(1, same)
        begin(win, h, parts_win, 0)
    window_tick(0)
    window_tick(1)
    window_push(0, 3)
    for t in range(1, half + 1):
        if t < half // 2:
            window_tick(2 * t)
        if t == half // 2:
            for way in range(2):
                window_arrived(way, half)
            window_push(nz - 1, 1)
        if t == half // 2 + 1:
            window_y()
        if t < half:
            tick(0, t)
            push(0, place(0, t), 2)
        else:
            last(0)
            for j in range(2):
                push(j, nz - 1, 1)
        if t < half // 2:
            window_tick(2 * t + 1)
            window_push(4 * t - 1, 4)
        if t == 1:
            for same, h in ((True, hi), (False, 1 - hi)):
                exchanged(2, same)
                for n in range(1, 3):
                    begin(owns[n - 1], h, parts_own, (n - 1) * OWN)
                    tick(n, 0, (h,))
            push(1, 1, 2)
        else:
            tick(1, t - 1)
            if t < half:
                push(1, place(0, t), 2)
            tick(2, t - 1)
        if t == 2:
            weigh()
        if t == half // 2 + 2:
            window_core()
        if t == half // 2 + 3:
            window_done()

            @pl.loop(0, 2)
            def _(h):
                finish(product(got_win[h], 0, pairs), out_win.at[h], window_at(h, y), h)

            sum_own[0] = product(own_a[:EARLY], 0, early)

    sum_own[1] = product(own_b[:EARLY], 0, early)

    for h in range(2):
        wait(got.at[:, pl.ds(0, EARLY + 1), h], xrecv.at[h, 0])

    @pl.loop(0, 2)
    def _(j):
        sum_got[j] = product(got[j, :EARLY], 0, early)

    for h in range(2):
        wait(got.at[:, pl.ds(EARLY + 1, nz - EARLY - 1), h], xrecv.at[h, 1])

    @pl.loop(0, 2)
    def _(j):
        finish(sum_got[j] + product(got[j, EARLY:], early, pairs), out_got.at[j], lent_at(j), 4 + j)

    for n in range(2):
        last(1 + n)
        finish(sum_own[n] + product(owns[n][EARLY:], early, pairs), out_own.at[n], OWN_AT + n * OWN, 2 + n)

    for way in range(2):
        wait(win.at[pl.ds(0, nz - 1), 0], nsend.at[way])
        for h in range(2):
            count = half if way == h else half - 1
            wait(lent.at[h, pl.ds(0, count)], zsend.at[way, 0, h])
            for n in range(2):
                wait(owns[n].at[pl.ds(0, count), h], zsend.at[way, 1 + n, h])
    for n in range(2):
        wait(lent, xsend.at[n])
        wait(win, xwsend.at[n])
    wait(parts_lent.at[pl.ds(0, ncol - 1)], part_send.at[0])
    wait(parts_win.at[pl.ds(0, plane - 1)], part_send.at[1])
    wait(parts_own.at[pl.ds(0, plane - 1)], part_send.at[2])

    @pl.when(is_source)
    def _():
        for k in range(ny - 1):
            wait(wbuf, wsend.at[k])

    @pl.when(same_core)
    def _():
        wait(wbuf, wsend.at[ny - 1])

    for h in range(2):
        write(out_own.at[h], OWN_AT + h * OWN, 2 + h).wait()
        write(out_win.at[h], window_at(h, y), h).wait()
        write(out_got.at[h], lent_at(h), 4 + h).wait()


def on_device(pair_elements, energy_gaps, frequencies):
    rows, cols = lax.axis_size("row"), lax.axis_size("col")
    local, full = pair_elements.shape
    pairs = local * rows * cols
    block = full // cols
    nz, ny = rows // 2, cols // 4
    depth = local * cols
    plane = 2 * cols
    dma = pltpu.SemaphoreType.DMA

    def panels(width):
        return pltpu.VMEM((nz, 2, depth, width), jnp.bfloat16)

    operands = [
        pltpu.with_memory_space_constraint(operand, pltpu.HBM)
        for operand in (
            pair_elements.reshape(local, ny, 2, 2, block).transpose(1, 2, 3, 0, 4),
            energy_gaps.reshape(pairs // GSR, GSR),
            frequencies,
        )
    ]
    return pl.pallas_call(
        functools.partial(kernel, nz, ny, pairs),
        out_shape=jax.ShapeDtypeStruct((NW, GSR, block), jnp.bfloat16),
        in_specs=[pl.BlockSpec(memory_space=pl.ANY)] * 3,
        out_specs=pl.BlockSpec(memory_space=pl.ANY),
        scratch_shapes=[
            pltpu.VMEM((pairs // GSR, GSR), jnp.float32),
            pltpu.VMEM((4, pairs // GSR, GSR), jnp.float32),
            pltpu.VMEM((NW, pairs // GSR, GSR), jnp.float32),
            pltpu.SMEM((NW,), jnp.float32),
            pltpu.VMEM((cols, local, 2 * LENT), jnp.bfloat16),
            pltpu.VMEM((plane, local, WINDOW), jnp.bfloat16),
            pltpu.VMEM((plane, local, 2 * OWN), jnp.bfloat16),
            panels(WINDOW),
            panels(OWN),
            panels(OWN),
            pltpu.VMEM((2, nz, depth, LENT), jnp.bfloat16),
            pltpu.VMEM((2, nz, 2, depth, WINDOW), jnp.bfloat16),
            pltpu.VMEM((2, nz, 2, depth, LENT), jnp.bfloat16),
            panels(GSR),
            pltpu.VMEM((NW * GSR, pairs), jnp.bfloat16),
            pltpu.VMEM((2, NW * GSR, OWN), jnp.float32),
            pltpu.VMEM((2, NW * GSR, LENT), jnp.float32),
            pltpu.VMEM((2, NW, GSR, WINDOW), jnp.bfloat16),
            pltpu.VMEM((2, NW, GSR, OWN), jnp.bfloat16),
            pltpu.VMEM((2, NW, GSR, LENT), jnp.bfloat16),
            dma((2,)),
            dma((3,)),
            dma((3, 2)),
            dma((3,)),
            dma((2, nz // 2)),
            dma((2,)),
            dma((2, 3, 2, nz // 2)),
            dma((2, 3, 2)),
            dma((2,)),
            dma((2,)),
            dma((2, 2)),
            dma((2,)),
            dma((2,)),
            dma((ny,)),
            dma((6,)),
        ],
        compiler_params=pltpu.CompilerParams(
            collective_id=0, has_side_effects=True, vmem_limit_bytes=36 * 1024 * 1024
        ),
        cost_estimate=pl.CostEstimate(
            flops=2 * NW * GSR * pairs * block, bytes_accessed=2 * NW * GSR * block, transcendentals=0
        ),
    )(*operands)


def solution(mesh):
    in_specs = (P(("row", "col"), None), P(), P())
    out_specs = P(None, "row", "col")
    return jax.shard_map(
        on_device, mesh=mesh, in_specs=in_specs, out_specs=out_specs, check_vma=False
    )
```

```python
import functools
import math

import jax
import jax.numpy as jnp
from jax import lax
from jax.experimental import pallas as pl
from jax.experimental.pallas import tpu as pltpu
from jax.sharding import PartitionSpec as P

NW = 3
GSR = 128
WINDOW = 256
LENT = 896
OWN = 768
LENT_AT = 2 * WINDOW
OWN_AT = LENT_AT + 2 * LENT
EARLY = 12
MESH = pl.DeviceIdType.MESH


def kernel(nz, ny, pairs, elements, gaps_in, freqs_in, out, gaps, turned_gaps, weights, freqs,
           parts_lent, parts_win, parts_own, win, own_a, own_b, lent, got_win, got, wbuf, lhs,
           sum_own, sum_got, out_win, out_own, out_got, in_sem, part_sem, part_recv, part_send,
           nrecv, nsend, zrecv, zsend, xwrecv, xwsend, xrecv, xsend, wrecv, wsend, osem):
    row, col = lax.axis_index("row"), lax.axis_index("col")
    hi, z = row // nz, lax.rem(row, nz)
    ncol = ny * 4
    plane = 2 * ncol
    seat = hi * ncol + col
    y = col // 4
    in_y = lax.rem(col, 4)
    lo, core = in_y // 2, lax.rem(in_y, 2)
    up = (hi * nz + lax.rem(z + 1, nz), col)
    down = (hi * nz + lax.rem(z + nz - 1, nz), col)
    other_lo = y * 4 + (1 - lo) * 2 + core
    side = [(z, other_lo), (nz + z, other_lo)]
    in_column = [(row, lax.rem(y + k, ny) * 4 + in_y) for k in (1, 3, 2)]
    twin_core = (row, y * 4 + lo * 2 + (1 - core))
    half = nz // 2

    def seated(h, k):
        c = lax.rem(col + k, ncol)
        return h, c // 4, lax.rem(c, 4) // 2, lax.rem(c, 2)

    def device_at(h, y, lo, core):
        return h * nz + z, y * 4 + lo * 2 + core

    barrier = pltpu.get_barrier_semaphore()
    for device in (up, down):
        pl.semaphore_signal(barrier, inc=1, device_id=device, device_id_type=MESH)

    def for_same(do):
        pl.loop(1, ncol)(lambda k: do(seated(hi, k)))

    def for_others(do):
        for_same(do)
        pl.loop(0, ncol)(lambda k: do(seated(1 - hi, k)))

    for_others(lambda to: pl.semaphore_signal(barrier, inc=1, device_id=device_at(*to), device_id_type=MESH))

    loads = [
        pltpu.make_async_copy(gaps_in, gaps, in_sem.at[0]),
        pltpu.make_async_copy(freqs_in, freqs, in_sem.at[1]),
    ]
    for load in loads:
        load.start()

    def window_at(h, y):
        first = y // 2
        return pl.multiple_of((h + first - 2 * h * first) * WINDOW, 128)

    def lent_range(h, y, lo, core):
        return elements.at[y, 1 - lo, core, :, pl.ds(LENT_AT, 2 * LENT)]

    def window_range(h, y, lo, core):
        return elements.at[y, 1 - lo, core, :, pl.ds(window_at(h, y), WINDOW)]

    def own_range(h, y, lo, core):
        return elements.at[y, lo, core, :, pl.ds(OWN_AT, 2 * OWN)]

    ranges = ((lent_range, parts_lent), (window_range, parts_win), (own_range, parts_own))
    mine = [
        pltpu.make_async_copy(
            source(hi, y, lo, core), parts.at[col if n == 0 else seat], part_sem.at[n]
        )
        for n, (source, parts) in enumerate(ranges)
    ]
    for copy in mine:
        copy.start()
    pl.semaphore_wait(barrier, plane + 1)

    def remote(src, dst, send, recv, device):
        return pltpu.make_async_remote_copy(
            src_ref=src, dst_ref=dst, send_sem=send, recv_sem=recv, device_id=device, device_id_type=MESH
        )

    def wait(ref, sem):
        pltpu.make_async_copy(ref, ref, sem).wait()

    def exchange(n):
        source, parts = ranges[n]
        (for_same if n == 0 else for_others)(lambda to: remote(
            source(*to), parts.at[col if n == 0 else seat], part_send.at[n], part_recv.at[n, hi], device_at(*to)
        ).start())

    def exchanged(n, same):
        parts = ranges[n][1]
        if same:
            mine[n].wait()
        wait(parts.at[pl.ds(0, ncol - 1 if same else ncol)], part_recv.at[n, hi if same else 1 - hi])

    for n in range(2):
        exchange(n)

    def weigh():
        for load in loads:
            load.wait()
        for k in range(4):
            turned_gaps[k] = pltpu.roll(gaps[...], k * 32, 1)
        quarter = lax.broadcasted_iota(jnp.int32, (1, GSR), 1) // 32

        @pl.loop(0, pairs // GSR)
        def _(b):
            line = jnp.zeros((1, GSR), jnp.float32)
            for q in range(4):
                plane_at = lax.rem(z + (b if q < 2 else nz - 1 - b), nz)
                shift = lax.rem(q + 4 - lax.rem(plane_at, 4), 4)
                piece = turned_gaps[shift, pl.ds(q % 2 * 4 + plane_at // 4, 1), :]
                line = jnp.where(quarter == q, piece, line)
            for w in range(NW):
                weights[w, pl.ds(b, 1), :] = (
                    -4.0 * line / ((line * line + freqs[w] * freqs[w]) * math.sqrt(pairs))
                )

    owns = (own_a, own_b)

    def slab(n, h, at):
        return lent.at[h, at] if n == 0 else owns[n - 1].at[at, h]


    def begin(buf, h, parts, start):
        width = buf.shape[-1]
        part = parts[pl.ds(pl.multiple_of(h * ncol, ncol), ncol), :, start:start + width]
        buf[0, h] = part.reshape(2 * ncol, width)

    def place(way, s):
        return 0 if s == 0 else nz - 1 if s == half else 2 * s - 1 + way

    def push(first, count):
        late = int(first > EARLY)
        for n in range(2):
            remote(
                lent.at[:, pl.ds(first, count)], got.at[:, pl.ds(first, count), hi],
                xsend.at[n], xrecv.at[hi, late], side[n],
            ).start()

    def arrived(n, h, way, s):
        wait(slab(n, h, place(way, s)), zrecv.at[way, n, h, s - 1])

    def tick(n, s, lanes=(0, 1)):
        for h in lanes:
            for way, device in ((0, up), (1, down)):
                if s > 0:
                    arrived(n, h, way, s)
                if s == half - 1 and way != h:
                    continue
                remote(
                    slab(n, h, place(way, s)), slab(n, h, place(way, s + 1)),
                    zsend.at[way, n, h], zrecv.at[way, n, h, s], device,
                ).start()

    def last(n):
        for h in range(2):
            arrived(n, h, h, half)

    def window_arrived(way, s):
        part = win.at[place(way, s)]
        wait(part.at[way] if s == half else part, nrecv.at[way, s - 1])

    def window_tick(s):
        for way, device in ((0, up), (1, down)):
            if s > 0:
                window_arrived(way, s)
            src, dst = win.at[place(way, s)], win.at[place(way, s + 1)]
            if s == half - 1:
                src, dst = src.at[way], dst.at[way]
            remote(src, dst, nsend.at[way], nrecv.at[way, s], device).start()

    def window_push(first, count):
        for n in range(2):
            remote(
                win.at[pl.ds(first, count)], got_win.at[hi, pl.ds(first, count)],
                xwsend.at[n], xwrecv.at[hi], side[n],
            ).start()

    window_col = row // 2
    in_w = lax.rem(window_col, 4)
    same_core = core == lax.rem(in_w, 2)
    is_source = jnp.logical_and(same_core, y == window_col // 4)
    gathers = lo != in_w // 2

    def window_y():
        for h in range(2):
            wait(got_win.at[h], xwrecv.at[h])

        @pl.when(is_source)
        def _():
            for b in range(2):
                cut = slice(b * GSR, (b + 1) * GSR)
                this = lax.rem(row, 2) == b

                @pl.when(jnp.logical_and(this, gathers))
                def _():
                    wbuf[...] = win[:, :, :, cut]

                @pl.when(jnp.logical_and(this, jnp.logical_not(gathers)))
                def _():
                    wbuf[...] = got_win[hi, :, :, :, cut]
            for k, device in enumerate(in_column):
                remote(wbuf, wbuf, wsend.at[k], wrecv.at[0], device).start()

    def window_core():
        @pl.when(same_core)
        def _():
            @pl.when(jnp.logical_not(is_source))
            def _():
                wait(wbuf, wrecv.at[0])
            remote(wbuf, wbuf, wsend.at[ny - 1], wrecv.at[1], twin_core).start()

    def window_done():
        @pl.when(jnp.logical_not(same_core))
        def _():
            wait(wbuf, wrecv.at[1])

        @pl.loop(0, pairs // GSR)
        def _(b):
            at = pl.multiple_of(b * GSR, GSR)
            block = wbuf[pl.ds(b * 2, 2)].reshape(GSR, GSR)
            turned = block.astype(jnp.float32).T
            for w in range(NW):
                lhs[w * GSR:(w + 1) * GSR, pl.ds(at, GSR)] = (
                    turned * weights[w, pl.ds(b, 1), :]
                ).astype(jnp.bfloat16)

    early = EARLY * 4 * ncol

    def product(panel, low, high):
        return jnp.dot(
            lhs[:, low:high], panel.reshape(high - low, panel.shape[-1]), preferred_element_type=jnp.float32
        )

    def finish(chi, to, at, sem):
        to[...] = chi.astype(jnp.bfloat16).reshape(to.shape)
        write(to, at, sem).start()

    def write(to, at, sem):
        return pltpu.make_async_copy(to, out.at[:, :, pl.ds(at, to.shape[-1])], osem.at[sem])

    def lent_at(j):
        return pl.multiple_of(LENT_AT + j * LENT, 128)

    exchanged(0, True)
    for j in range(2):
        lent[j, 0] = parts_lent[:, :, j * LENT:(j + 1) * LENT].reshape(2 * ncol, LENT)
    tick(0, 0)
    push(0, 1)
    exchange(2)
    for same, h in ((True, hi), (False, 1 - hi)):
        exchanged(1, same)
        begin(win, h, parts_win, 0)
    window_tick(0)
    window_tick(1)
    window_push(0, 3)
    for t in range(1, half + 1):
        if t < half // 2:
            window_tick(2 * t)
        if t == half // 2:
            for way in range(2):
                window_arrived(way, half)
            window_push(nz - 1, 1)
        if t == half // 2 + 1:
            window_y()
        if t < half:
            tick(0, t)
            push(place(0, t), 2)
        else:
            last(0)
            push(nz - 1, 1)
        if t < half // 2:
            window_tick(2 * t + 1)
            window_push(4 * t - 1, 4)
        if t == 1:
            for same, h in ((True, hi), (False, 1 - hi)):
                exchanged(2, same)
                for n in range(1, 3):
                    begin(owns[n - 1], h, parts_own, (n - 1) * OWN)
                    tick(n, 0, (h,))
        else:
            for n in range(1, 3):
                tick(n, t - 1)
        if t == 2:
            weigh()
        if t == half // 2 + 2:
            window_core()
        if t == half // 2 + 3:
            window_done()

            @pl.loop(0, 2)
            def _(h):
                finish(product(got_win[h], 0, pairs), out_win.at[h], window_at(h, y), h)

            sum_own[0] = product(own_a[:EARLY], 0, early)

    sum_own[1] = product(own_b[:EARLY], 0, early)

    for h in range(2):
        wait(got.at[:, pl.ds(0, EARLY + 1), h], xrecv.at[h, 0])

    @pl.loop(0, 2)
    def _(j):
        sum_got[j] = product(got[j, :EARLY], 0, early)

    for h in range(2):
        wait(got.at[:, pl.ds(EARLY + 1, nz - EARLY - 1), h], xrecv.at[h, 1])

    @pl.loop(0, 2)
    def _(j):
        finish(sum_got[j] + product(got[j, EARLY:], early, pairs), out_got.at[j], lent_at(j), 4 + j)

    for n in range(2):
        last(1 + n)
        finish(sum_own[n] + product(owns[n][EARLY:], early, pairs), out_own.at[n], OWN_AT + n * OWN, 2 + n)

    for way in range(2):
        wait(win.at[pl.ds(0, nz - 1), 0], nsend.at[way])
        for h in range(2):
            count = half if way == h else half - 1
            wait(lent.at[h, pl.ds(0, count)], zsend.at[way, 0, h])
            for n in range(2):
                wait(owns[n].at[pl.ds(0, count), h], zsend.at[way, 1 + n, h])
    for n in range(2):
        wait(lent, xsend.at[n])
        wait(win, xwsend.at[n])
    wait(parts_lent.at[pl.ds(0, ncol - 1)], part_send.at[0])
    wait(parts_win.at[pl.ds(0, plane - 1)], part_send.at[1])
    wait(parts_own.at[pl.ds(0, plane - 1)], part_send.at[2])

    @pl.when(is_source)
    def _():
        for k in range(ny - 1):
            wait(wbuf, wsend.at[k])

    @pl.when(same_core)
    def _():
        wait(wbuf, wsend.at[ny - 1])

    for h in range(2):
        write(out_own.at[h], OWN_AT + h * OWN, 2 + h).wait()
        write(out_win.at[h], window_at(h, y), h).wait()
        write(out_got.at[h], lent_at(h), 4 + h).wait()


def on_device(pair_elements, energy_gaps, frequencies):
    rows, cols = lax.axis_size("row"), lax.axis_size("col")
    local, full = pair_elements.shape
    pairs = local * rows * cols
    block = full // cols
    nz, ny = rows // 2, cols // 4
    depth = local * cols
    plane = 2 * cols
    dma = pltpu.SemaphoreType.DMA

    def panels(width):
        return pltpu.VMEM((nz, 2, depth, width), jnp.bfloat16)

    operands = [
        pltpu.with_memory_space_constraint(operand, pltpu.HBM)
        for operand in (
            pair_elements.reshape(local, ny, 2, 2, block).transpose(1, 2, 3, 0, 4),
            energy_gaps.reshape(pairs // GSR, GSR),
            frequencies,
        )
    ]
    return pl.pallas_call(
        functools.partial(kernel, nz, ny, pairs),
        out_shape=jax.ShapeDtypeStruct((NW, GSR, block), jnp.bfloat16),
        in_specs=[pl.BlockSpec(memory_space=pl.ANY)] * 3,
        out_specs=pl.BlockSpec(memory_space=pl.ANY),
        scratch_shapes=[
            pltpu.VMEM((pairs // GSR, GSR), jnp.float32),
            pltpu.VMEM((4, pairs // GSR, GSR), jnp.float32),
            pltpu.VMEM((NW, pairs // GSR, GSR), jnp.float32),
            pltpu.SMEM((NW,), jnp.float32),
            pltpu.VMEM((cols, local, 2 * LENT), jnp.bfloat16),
            pltpu.VMEM((plane, local, WINDOW), jnp.bfloat16),
            pltpu.VMEM((plane, local, 2 * OWN), jnp.bfloat16),
            panels(WINDOW),
            panels(OWN),
            panels(OWN),
            pltpu.VMEM((2, nz, depth, LENT), jnp.bfloat16),
            pltpu.VMEM((2, nz, 2, depth, WINDOW), jnp.bfloat16),
            pltpu.VMEM((2, nz, 2, depth, LENT), jnp.bfloat16),
            panels(GSR),
            pltpu.VMEM((NW * GSR, pairs), jnp.bfloat16),
            pltpu.VMEM((2, NW * GSR, OWN), jnp.float32),
            pltpu.VMEM((2, NW * GSR, LENT), jnp.float32),
            pltpu.VMEM((2, NW, GSR, WINDOW), jnp.bfloat16),
            pltpu.VMEM((2, NW, GSR, OWN), jnp.bfloat16),
            pltpu.VMEM((2, NW, GSR, LENT), jnp.bfloat16),
            dma((2,)),
            dma((3,)),
            dma((3, 2)),
            dma((3,)),
            dma((2, nz // 2)),
            dma((2,)),
            dma((2, 3, 2, nz // 2)),
            dma((2, 3, 2)),
            dma((2,)),
            dma((2,)),
            dma((2, 2)),
            dma((2,)),
            dma((2,)),
            dma((ny,)),
            dma((6,)),
        ],
        compiler_params=pltpu.CompilerParams(
            collective_id=0, has_side_effects=True, vmem_limit_bytes=36 * 1024 * 1024
        ),
        cost_estimate=pl.CostEstimate(
            flops=2 * NW * GSR * pairs * block, bytes_accessed=2 * NW * GSR * block, transcendentals=0
        ),
    )(*operands)


def solution(mesh):
    in_specs = (P(("row", "col"), None), P(), P())
    out_specs = P(None, "row", "col")
    return jax.shard_map(
        on_device, mesh=mesh, in_specs=in_specs, out_specs=out_specs, check_vma=False
    )
```

```python
import functools
import math

import jax
import jax.numpy as jnp
from jax import lax
from jax.experimental import pallas as pl
from jax.experimental.pallas import tpu as pltpu
from jax.sharding import PartitionSpec as P

NW = 3
GSR = 128
WINDOW = 256
LENT = 1024
OWN = 640
LENT_AT = 2 * WINDOW
OWN_AT = LENT_AT + 2 * LENT
EARLY = 12
MESH = pl.DeviceIdType.MESH


def kernel(nz, ny, pairs, elements, gaps_in, freqs_in, out, gaps, turned_gaps, weights, freqs,
           parts_lent, parts_win, parts_own, win, own_a, own_b, lent, got_win, got, wbuf, lhs,
           sum_own, sum_got, out_win, out_own, out_got, in_sem, part_sem, part_recv, part_send,
           nrecv, nsend, zrecv, zsend, xwrecv, xwsend, xrecv, xsend, wrecv, wsend, osem):
    row, col = lax.axis_index("row"), lax.axis_index("col")
    hi, z = row // nz, lax.rem(row, nz)
    ncol = ny * 4
    plane = 2 * ncol
    seat = hi * ncol + col
    y = col // 4
    in_y = lax.rem(col, 4)
    lo, core = in_y // 2, lax.rem(in_y, 2)
    up = (hi * nz + lax.rem(z + 1, nz), col)
    down = (hi * nz + lax.rem(z + nz - 1, nz), col)
    other_lo = y * 4 + (1 - lo) * 2 + core
    side = [(z, other_lo), (nz + z, other_lo)]
    in_column = [(row, lax.rem(y + k, ny) * 4 + in_y) for k in (1, 3, 2)]
    twin_core = (row, y * 4 + lo * 2 + (1 - core))
    half = nz // 2

    def seated(h, k):
        c = lax.rem(col + k, ncol)
        return h, c // 4, lax.rem(c, 4) // 2, lax.rem(c, 2)

    def device_at(h, y, lo, core):
        return h * nz + z, y * 4 + lo * 2 + core

    barrier = pltpu.get_barrier_semaphore()
    for device in (up, down):
        pl.semaphore_signal(barrier, inc=1, device_id=device, device_id_type=MESH)

    def for_same(do):
        pl.loop(1, ncol)(lambda k: do(seated(hi, k)))

    def for_others(do):
        for_same(do)
        pl.loop(0, ncol)(lambda k: do(seated(1 - hi, k)))

    for_others(lambda to: pl.semaphore_signal(barrier, inc=1, device_id=device_at(*to), device_id_type=MESH))

    loads = [
        pltpu.make_async_copy(gaps_in, gaps, in_sem.at[0]),
        pltpu.make_async_copy(freqs_in, freqs, in_sem.at[1]),
    ]
    for load in loads:
        load.start()

    def window_at(h, y):
        first = y // 2
        return pl.multiple_of((h + first - 2 * h * first) * WINDOW, 128)

    def lent_range(h, y, lo, core):
        return elements.at[y, 1 - lo, core, :, pl.ds(LENT_AT, 2 * LENT)]

    def window_range(h, y, lo, core):
        return elements.at[y, 1 - lo, core, :, pl.ds(window_at(h, y), WINDOW)]

    def own_range(h, y, lo, core):
        return elements.at[y, lo, core, :, pl.ds(OWN_AT, 2 * OWN)]

    ranges = ((lent_range, parts_lent), (window_range, parts_win), (own_range, parts_own))
    mine = [
        pltpu.make_async_copy(
            source(hi, y, lo, core), parts.at[col if n == 0 else seat], part_sem.at[n]
        )
        for n, (source, parts) in enumerate(ranges)
    ]
    for copy in mine:
        copy.start()
    pl.semaphore_wait(barrier, plane + 1)

    def remote(src, dst, send, recv, device):
        return pltpu.make_async_remote_copy(
            src_ref=src, dst_ref=dst, send_sem=send, recv_sem=recv, device_id=device, device_id_type=MESH
        )

    def wait(ref, sem):
        pltpu.make_async_copy(ref, ref, sem).wait()

    def exchange(n):
        source, parts = ranges[n]
        (for_same if n == 0 else for_others)(lambda to: remote(
            source(*to), parts.at[col if n == 0 else seat], part_send.at[n], part_recv.at[n, hi], device_at(*to)
        ).start())

    def exchanged(n, same):
        parts = ranges[n][1]
        if same:
            mine[n].wait()
        wait(parts.at[pl.ds(0, ncol - 1 if same else ncol)], part_recv.at[n, hi if same else 1 - hi])

    for n in range(2):
        exchange(n)

    def weigh():
        for load in loads:
            load.wait()
        for k in range(4):
            turned_gaps[k] = pltpu.roll(gaps[...], k * 32, 1)
        quarter = lax.broadcasted_iota(jnp.int32, (1, GSR), 1) // 32

        @pl.loop(0, pairs // GSR)
        def _(b):
            line = jnp.zeros((1, GSR), jnp.float32)
            for q in range(4):
                plane_at = lax.rem(z + (b if q < 2 else nz - 1 - b), nz)
                shift = lax.rem(q + 4 - lax.rem(plane_at, 4), 4)
                piece = turned_gaps[shift, pl.ds(q % 2 * 4 + plane_at // 4, 1), :]
                line = jnp.where(quarter == q, piece, line)
            for w in range(NW):
                weights[w, pl.ds(b, 1), :] = (
                    -4.0 * line / ((line * line + freqs[w] * freqs[w]) * math.sqrt(pairs))
                )

    owns = (own_a, own_b)

    def slab(n, h, at):
        return lent.at[h, at] if n == 0 else owns[n - 1].at[at, h]


    def begin(buf, h, parts, start):
        width = buf.shape[-1]
        part = parts[pl.ds(pl.multiple_of(h * ncol, ncol), ncol), :, start:start + width]
        buf[0, h] = part.reshape(2 * ncol, width)

    def place(way, s):
        return 0 if s == 0 else nz - 1 if s == half else 2 * s - 1 + way

    def push(first, count):
        late = int(first > EARLY)
        for n in range(2):
            remote(
                lent.at[:, pl.ds(first, count)], got.at[:, pl.ds(first, count), hi],
                xsend.at[n], xrecv.at[hi, late], side[n],
            ).start()

    def arrived(n, h, way, s):
        wait(slab(n, h, place(way, s)), zrecv.at[way, n, h, s - 1])

    def tick(n, s, lanes=(0, 1)):
        for h in lanes:
            for way, device in ((0, up), (1, down)):
                if s > 0:
                    arrived(n, h, way, s)
                if s == half - 1 and way != h:
                    continue
                remote(
                    slab(n, h, place(way, s)), slab(n, h, place(way, s + 1)),
                    zsend.at[way, n, h], zrecv.at[way, n, h, s], device,
                ).start()

    def last(n):
        for h in range(2):
            arrived(n, h, h, half)

    def window_arrived(way, s):
        part = win.at[place(way, s)]
        wait(part.at[way] if s == half else part, nrecv.at[way, s - 1])

    def window_tick(s):
        for way, device in ((0, up), (1, down)):
            if s > 0:
                window_arrived(way, s)
            src, dst = win.at[place(way, s)], win.at[place(way, s + 1)]
            if s == half - 1:
                src, dst = src.at[way], dst.at[way]
            remote(src, dst, nsend.at[way], nrecv.at[way, s], device).start()

    def window_push(first, count):
        for n in range(2):
            remote(
                win.at[pl.ds(first, count)], got_win.at[hi, pl.ds(first, count)],
                xwsend.at[n], xwrecv.at[hi], side[n],
            ).start()

    window_col = row // 2
    in_w = lax.rem(window_col, 4)
    same_core = core == lax.rem(in_w, 2)
    is_source = jnp.logical_and(same_core, y == window_col // 4)
    gathers = lo != in_w // 2

    def window_y():
        for h in range(2):
            wait(got_win.at[h], xwrecv.at[h])

        @pl.when(is_source)
        def _():
            for b in range(2):
                cut = slice(b * GSR, (b + 1) * GSR)
                this = lax.rem(row, 2) == b

                @pl.when(jnp.logical_and(this, gathers))
                def _():
                    wbuf[...] = win[:, :, :, cut]

                @pl.when(jnp.logical_and(this, jnp.logical_not(gathers)))
                def _():
                    wbuf[...] = got_win[hi, :, :, :, cut]
            for k, device in enumerate(in_column):
                remote(wbuf, wbuf, wsend.at[k], wrecv.at[0], device).start()

    def window_core():
        @pl.when(same_core)
        def _():
            @pl.when(jnp.logical_not(is_source))
            def _():
                wait(wbuf, wrecv.at[0])
            remote(wbuf, wbuf, wsend.at[ny - 1], wrecv.at[1], twin_core).start()

    def window_done():
        @pl.when(jnp.logical_not(same_core))
        def _():
            wait(wbuf, wrecv.at[1])

        @pl.loop(0, pairs // GSR)
        def _(b):
            at = pl.multiple_of(b * GSR, GSR)
            block = wbuf[pl.ds(b * 2, 2)].reshape(GSR, GSR)
            turned = block.astype(jnp.float32).T
            for w in range(NW):
                lhs[w * GSR:(w + 1) * GSR, pl.ds(at, GSR)] = (
                    turned * weights[w, pl.ds(b, 1), :]
                ).astype(jnp.bfloat16)

    early = EARLY * 4 * ncol

    def product(panel, low, high):
        return jnp.dot(
            lhs[:, low:high], panel.reshape(high - low, panel.shape[-1]), preferred_element_type=jnp.float32
        )

    def finish(chi, to, at, sem):
        to[...] = chi.astype(jnp.bfloat16).reshape(to.shape)
        write(to, at, sem).start()

    def write(to, at, sem):
        return pltpu.make_async_copy(to, out.at[:, :, pl.ds(at, to.shape[-1])], osem.at[sem])

    def lent_at(j):
        return pl.multiple_of(LENT_AT + j * LENT, 128)

    exchanged(0, True)
    for j in range(2):
        lent[j, 0] = parts_lent[:, :, j * LENT:(j + 1) * LENT].reshape(2 * ncol, LENT)
    tick(0, 0)
    push(0, 1)
    exchange(2)
    for same, h in ((True, hi), (False, 1 - hi)):
        exchanged(1, same)
        begin(win, h, parts_win, 0)
    window_tick(0)
    window_tick(1)
    window_push(0, 3)
    for t in range(1, half + 1):
        if t < half // 2:
            window_tick(2 * t)
        if t == half // 2:
            for way in range(2):
                window_arrived(way, half)
            window_push(nz - 1, 1)
        if t == half // 2 + 1:
            window_y()
        if t < half:
            tick(0, t)
            push(place(0, t), 2)
        if t < half // 2:
            window_tick(2 * t + 1)
            window_push(4 * t - 1, 4)
        if t == 1:
            for same, h in ((True, hi), (False, 1 - hi)):
                exchanged(2, same)
                for n in range(1, 3):
                    begin(owns[n - 1], h, parts_own, (n - 1) * OWN)
                    tick(n, 0, (h,))
        else:
            for n in range(1, 3):
                tick(n, t - 1)
        if t == 2:
            weigh()
        if t == half // 2 + 2:
            window_core()
        if t == half // 2 + 3:
            last(0)
            push(nz - 1, 1)
            window_done()

            @pl.loop(0, 2)
            def _(h):
                finish(product(got_win[h], 0, pairs), out_win.at[h], window_at(h, y), h)

            sum_own[0] = product(own_a[:EARLY], 0, early)

    sum_own[1] = product(own_b[:EARLY], 0, early)

    for h in range(2):
        wait(got.at[:, pl.ds(0, EARLY + 1), h], xrecv.at[h, 0])

    @pl.loop(0, 2)
    def _(j):
        sum_got[j] = product(got[j, :EARLY], 0, early)

    for h in range(2):
        wait(got.at[:, pl.ds(EARLY + 1, nz - EARLY - 1), h], xrecv.at[h, 1])

    @pl.loop(0, 2)
    def _(j):
        finish(sum_got[j] + product(got[j, EARLY:], early, pairs), out_got.at[j], lent_at(j), 4 + j)

    for n in range(2):
        last(1 + n)
        finish(sum_own[n] + product(owns[n][EARLY:], early, pairs), out_own.at[n], OWN_AT + n * OWN, 2 + n)

    for way in range(2):
        wait(win.at[pl.ds(0, nz - 1), 0], nsend.at[way])
        for h in range(2):
            count = half if way == h else half - 1
            wait(lent.at[h, pl.ds(0, count)], zsend.at[way, 0, h])
            for n in range(2):
                wait(owns[n].at[pl.ds(0, count), h], zsend.at[way, 1 + n, h])
    for n in range(2):
        wait(lent, xsend.at[n])
        wait(win, xwsend.at[n])
    wait(parts_lent.at[pl.ds(0, ncol - 1)], part_send.at[0])
    wait(parts_win.at[pl.ds(0, plane - 1)], part_send.at[1])
    wait(parts_own.at[pl.ds(0, plane - 1)], part_send.at[2])

    @pl.when(is_source)
    def _():
        for k in range(ny - 1):
            wait(wbuf, wsend.at[k])

    @pl.when(same_core)
    def _():
        wait(wbuf, wsend.at[ny - 1])

    for h in range(2):
        write(out_own.at[h], OWN_AT + h * OWN, 2 + h).wait()
        write(out_win.at[h], window_at(h, y), h).wait()
        write(out_got.at[h], lent_at(h), 4 + h).wait()


def on_device(pair_elements, energy_gaps, frequencies):
    rows, cols = lax.axis_size("row"), lax.axis_size("col")
    local, full = pair_elements.shape
    pairs = local * rows * cols
    block = full // cols
    nz, ny = rows // 2, cols // 4
    depth = local * cols
    plane = 2 * cols
    dma = pltpu.SemaphoreType.DMA

    def panels(width):
        return pltpu.VMEM((nz, 2, depth, width), jnp.bfloat16)

    operands = [
        pltpu.with_memory_space_constraint(operand, pltpu.HBM)
        for operand in (
            pair_elements.reshape(local, ny, 2, 2, block).transpose(1, 2, 3, 0, 4),
            energy_gaps.reshape(pairs // GSR, GSR),
            frequencies,
        )
    ]
    return pl.pallas_call(
        functools.partial(kernel, nz, ny, pairs),
        out_shape=jax.ShapeDtypeStruct((NW, GSR, block), jnp.bfloat16),
        in_specs=[pl.BlockSpec(memory_space=pl.ANY)] * 3,
        out_specs=pl.BlockSpec(memory_space=pl.ANY),
        scratch_shapes=[
            pltpu.VMEM((pairs // GSR, GSR), jnp.float32),
            pltpu.VMEM((4, pairs // GSR, GSR), jnp.float32),
            pltpu.VMEM((NW, pairs // GSR, GSR), jnp.float32),
            pltpu.SMEM((NW,), jnp.float32),
            pltpu.VMEM((cols, local, 2 * LENT), jnp.bfloat16),
            pltpu.VMEM((plane, local, WINDOW), jnp.bfloat16),
            pltpu.VMEM((plane, local, 2 * OWN), jnp.bfloat16),
            panels(WINDOW),
            panels(OWN),
            panels(OWN),
            pltpu.VMEM((2, nz, depth, LENT), jnp.bfloat16),
            pltpu.VMEM((2, nz, 2, depth, WINDOW), jnp.bfloat16),
            pltpu.VMEM((2, nz, 2, depth, LENT), jnp.bfloat16),
            panels(GSR),
            pltpu.VMEM((NW * GSR, pairs), jnp.bfloat16),
            pltpu.VMEM((2, NW * GSR, OWN), jnp.float32),
            pltpu.VMEM((2, NW * GSR, LENT), jnp.float32),
            pltpu.VMEM((2, NW, GSR, WINDOW), jnp.bfloat16),
            pltpu.VMEM((2, NW, GSR, OWN), jnp.bfloat16),
            pltpu.VMEM((2, NW, GSR, LENT), jnp.bfloat16),
            dma((2,)),
            dma((3,)),
            dma((3, 2)),
            dma((3,)),
            dma((2, nz // 2)),
            dma((2,)),
            dma((2, 3, 2, nz // 2)),
            dma((2, 3, 2)),
            dma((2,)),
            dma((2,)),
            dma((2, 2)),
            dma((2,)),
            dma((2,)),
            dma((ny,)),
            dma((6,)),
        ],
        compiler_params=pltpu.CompilerParams(
            collective_id=0, has_side_effects=True, vmem_limit_bytes=36 * 1024 * 1024
        ),
        cost_estimate=pl.CostEstimate(
            flops=2 * NW * GSR * pairs * block, bytes_accessed=2 * NW * GSR * block, transcendentals=0
        ),
    )(*operands)


def solution(mesh):
    in_specs = (P(("row", "col"), None), P(), P())
    out_specs = P(None, "row", "col")
    return jax.shard_map(
        on_device, mesh=mesh, in_specs=in_specs, out_specs=out_specs, check_vma=False
    )
```
